32 devices in a mesh: seq: 8 (over z, x), head: 4 (over y, core).
Axes of the slice: x: 2, y: 2, z: 4, core: 2. Of those that a mesh axis runs over, the one named last changes fastest.
Arguments:
- stream: bfloat16 [2048, 2048], P('seq'), may hold values from -9 to 9
- ln_gain: float32 [2048], replicated, may hold values from 0.25 to 1.75
- up_x: float32 [2048, 4096], P(None, 'head'), may hold values from -0.125 to 0.125
- up_z: float32 [2048, 4096], P(None, 'head'), may hold values from -0.125 to 0.125
- conv_w: float32 [4, 4096], P(None, 'head'), may hold values from -3 to 3
- conv_b: float32 [4096], P('head'), may hold values from -3 to 3
- qkv_w: float32 [3, 4, 4096], P(None, None, 'head'), may hold values from -3 to 3
- gate_w: float32 [8, 3, 4096], P(None, None, 'head'), may hold values from -0.0546875 to 0.0546875
- gate_bias: float32 [4], replicated, may hold values from 3.5 to 12
- gn_gain: float32 [4096], P('head'), may hold values from 0.25 to 1.75
- skip: float32 [4096], P('head'), may hold values from 0.25 to 1.75
- down_w: float32 [4096, 2048], P('head'), may hold values from -0.09375 to 0.09375
- cotangent: bfloat16 [2048, 2048], P('seq'), may hold values from -5 to 5
- lengths: int32 [4], replicated, may hold values from 1 to 2048, as said below
Outputs:
- output: bfloat16 [2048, 2048], P('seq')
- rms_pair: float32 [2], replicated
- grad_stream: float32 [2048, 2048], P('seq')
- grad_up_x: float32 [2048, 4096], P('seq', 'head')
- grad_up_z: float32 [2048, 4096], P('seq', 'head')
- grad_down: float32 [4096, 2048], P('head', 'seq')
- grad_ln_gain: float32 [2048], replicated
- grad_conv_w: float32 [4, 4096], P(None, 'head')
- grad_conv_b: float32 [4096], P('head')
- grad_qkv_w: float32 [3, 4, 4096], P(None, None, 'head')
- grad_gate_w: float32 [8, 3, 4096], P(None, None, 'head')
- grad_gate_bias: float32 [4], replicated
- grad_gn_gain: float32 [4096], P('head')
- grad_skip: float32 [4096], P('head')
The draws below stay inside these ranges and needn't reach their ends.
Inputs may be any that keep to these rules, and one draw needn't show every extreme that they name: `lengths`: four sequences laid end to end fill all 2048 positions; the first, third and fourth are each shorter than half of 256, so the second begins among the first 256 positions and ends among the last 256.
All inputs are finite; a program needn't handle non-finite values.
Results may differ from the reference program's by a relative error of at most 0.00045.
Values may be sent and summed in bfloat16 or wider, within the bound.
No kernel may reach another device: no remote copies, remote signals or barrier semaphores. Data moves between devices by JAX's collectives and lax.ppermute only.
A program may use at most 384 MiB of HBM per device.

```python
import math
import jax
import jax.numpy as jnp
from jax import lax

D = 2048
INNER = 4096
NH = 4
DH = 1024
KW = 4
QB = 4
TOK_DEV = 256
TOKENS = 2048


def draw_stream(key, part):
    key = jax.random.fold_in(key, 11)
    key_main, key_rough = jax.random.split(key)
    ramp = jnp.arange(TOKENS, dtype=jnp.float32) / TOKENS
    values = jnp.clip(jax.random.normal(key_main, (TOKENS, D), jnp.float32), -4.0, 4.0)
    scale = jnp.exp(jnp.log(0.5) + jnp.log(3.0) * ramp)
    rough = jax.random.uniform(key_rough, (TOKENS,), jnp.float32, 0.7, 1.4)
    return (values * (scale * rough)[:, None]).astype(jnp.bfloat16)


def draw_gate_bias(key, part):
    key = jax.random.fold_in(key, 12)
    keep_part = jax.random.uniform(key, (NH,), jnp.float32, 3.5, 11.0)
    return keep_part.astype(jnp.float32)


def draw_lengths(key, part):
    key = jax.random.fold_in(key, 13)
    lowest = max(TOK_DEV // 8, 1)
    short = jax.random.randint(key, (3,), lowest, TOK_DEV // 2)
    longest = TOKENS - jnp.sum(short)
    return jnp.stack([short[0], longest, short[1], short[2]]).astype(jnp.int32)


def levels(key, dims, pieces, low, top_value):
    level = 1.0
    for dim, shards_of in pieces:
        draws = jax.random.uniform(jax.random.fold_in(jax.random.fold_in(key, 6), dim), (shards_of,), jnp.float32, low / len(pieces), top_value / len(pieces))
        level = level * jnp.repeat(jnp.exp(draws), dims[dim] // shards_of).reshape((-1,) + (1,) * (len(dims) - 1 - dim))
    return level


def centred(own_key, dims, width, bound, shards=(), kind=jnp.bfloat16):
    level = levels(own_key, dims, shards, -0.22, 0.18) if shards else 1.0
    values = jax.random.normal(own_key, dims, jnp.float32) * width * level
    return jnp.minimum(jnp.maximum(values, -bound), bound).astype(kind)


def setup_inputs(seed: int = 0) -> dict:
    splits = jax.random.split(jax.random.key(seed), 15)
    return {
        "stream": draw_stream(jax.random.fold_in(splits[14], 71), 0),
        "ln_gain": jnp.clip(1.0 + 0.15 * jax.random.normal(splits[1], (D,), jnp.float32), 0.25, 1.75),
        "up_x": centred(splits[2], (D, INNER), D ** -0.5, 0.125, ((1, 4),), jnp.float32),
        "up_z": centred(splits[3], (D, INNER), D ** -0.5, 0.125, ((1, 4),), jnp.float32),
        "conv_w": centred(splits[4], (KW, INNER), KW ** -0.5, 3.0, ((1, 4),), jnp.float32),
        "conv_b": centred(splits[5], (INNER,), 0.5, 3.0, ((0, 4),), jnp.float32),
        "qkv_w": centred(splits[6], (3, QB, INNER), QB ** -0.5, 3.0, ((2, 4),), jnp.float32),
        "gate_w": centred(splits[7], (2 * NH, 3, INNER), (3 * INNER) ** -0.5, 0.0546875, ((2, 4),), jnp.float32),
        "gate_bias": draw_gate_bias(jax.random.fold_in(splits[14], 71), 0),
        "gn_gain": jnp.clip(1.0 + 0.15 * jax.random.normal(splits[9], (INNER,), jnp.float32), 0.25, 1.75),
        "skip": jnp.clip(1.0 + 0.15 * jax.random.normal(splits[10], (INNER,), jnp.float32), 0.25, 1.75),
        "down_w": centred(splits[11], (INNER, D), INNER ** -0.5, 0.09375, ((0, 4),), jnp.float32),
        "cotangent": centred(splits[12], (TOKENS, D), 1.0, 5.0, ((0, 8),)),
        "lengths": draw_lengths(jax.random.fold_in(splits[14], 71), 0),
    }


@jax.custom_vjp
def low(v):
    return lax.optimization_barrier(v.astype(jnp.bfloat16)).astype(jnp.float32)

@jax.custom_vjp
def low_back(v):
    return v

def low_keep(v):
    return (low(v), None)

def low_pass(kept, grad):
    return (grad,)

def back_keep(v):
    return (v, None)

def back_low(kept, grad):
    return (low(grad),)
low.defvjp(low_keep, low_pass)
low_back.defvjp(back_keep, back_low)
EPS = 1e-05
HIGH = lax.Precision.HIGHEST

def matmul(left, right):
    return jnp.dot(left, right, precision=HIGH, preferred_element_type=jnp.float32)

def layer_norm(values, gain):
    center = values - lax.optimization_barrier(jnp.mean(values, axis=-1, keepdims=True))
    spread = lax.optimization_barrier(jnp.mean(center * center, axis=-1, keepdims=True))
    return center * lax.rsqrt(spread + EPS) * gain

def block_mix(values, weight):
    row_count, col_count = values.shape
    group = weight.shape[0]
    grouped = values.reshape(row_count, col_count // group, group)
    table = weight.reshape(group, col_count // group, group)
    return jnp.einsum('lgj,jgi->lgi', grouped, table, precision=HIGH).reshape(row_count, col_count)

def seq_layout(positions, lengths):
    starts = jnp.cumsum(lengths) - lengths
    segment = lax.optimization_barrier(jnp.sum((positions[:, None] >= starts[None, :]).astype(jnp.int32), axis=1)) - 1
    starting = jnp.any(positions[:, None] == starts[None, :], axis=1)
    return (segment, starting)

def conv_masks(first, row_count, kernel, lengths, segment):
    ext_pos = first - (kernel - 1) + jnp.arange(row_count + kernel - 1, dtype=jnp.int32)
    ext_seg, unused = seq_layout(ext_pos, lengths)
    return jnp.stack([(ext_seg[tap:tap + row_count] == segment).astype(jnp.float32) for tap in range(kernel)])

def front(mixed, rim_rows, conv_w, conv_b, qkv_w, gate_w, same_seq):
    row_count = mixed.shape[0]
    kernel = conv_w.shape[0]
    padded = jnp.concatenate([rim_rows, mixed], axis=0)
    conv = jnp.broadcast_to(conv_b, mixed.shape)
    for tap in range(kernel):
        conv = conv + conv_w[tap] * padded[tap:tap + row_count] * same_seq[tap][:, None]
    conv_act = jax.nn.silu(conv)
    queries = block_mix(conv_act, qkv_w[0])
    key_rows = block_mix(conv_act, qkv_w[1])
    val_rows = block_mix(mixed, qkv_w[2])
    stacked = jnp.stack([queries, key_rows, val_rows])
    gate_part = jnp.einsum('gci,cli->gl', gate_w, stacked, precision=HIGH)
    return (conv_act, queries, key_rows, val_rows, gate_part)

def split_heads(values, heads):
    row_count, col_count = values.shape
    return values.reshape(row_count, heads, col_count // heads).transpose(1, 0, 2)

def cell_out(queries, key_rows, val_rows, in_gate, log_keep, segment, starting, state_in):
    scaled = key_rows / math.sqrt(key_rows.shape[-1])
    running = jnp.cumsum(log_keep)
    index = jnp.arange(segment.shape[0])
    allowed = (index[:, None] >= index[None, :]) & (segment[:, None] == segment[None, :])
    expo = running[:, None] - running[None, :] + in_gate[None, :]
    weights = jnp.where(allowed, jnp.exp(jnp.where(allowed, expo, 0.0)), 0.0)
    scores = matmul(queries, scaled.T) * weights
    carried = jnp.where(jnp.cumsum(starting.astype(jnp.int32)) == 0, jnp.exp(running), 0.0)
    return matmul(scores, val_rows) + carried[:, None] * matmul(queries, state_in)

def cell_end(key_rows, val_rows, in_gate, log_keep, segment, starting):
    scaled = key_rows / math.sqrt(key_rows.shape[-1])
    running = jnp.cumsum(log_keep)
    last_seg = segment == segment[-1]
    weights = jnp.where(last_seg, jnp.exp(jnp.where(last_seg, running[-1] - running + in_gate, 0.0)), 0.0)
    weighted = scaled * weights[:, None]
    decay = jnp.where(jnp.sum(starting.astype(jnp.int32)) == 0, jnp.exp(running[-1]), 0.0)
    return (matmul(weighted.T, val_rows), decay)

def finish(hidden, conv_act, outgate, gn_gain, skip):
    center = hidden - lax.optimization_barrier(jnp.mean(hidden, axis=-1, keepdims=True))
    spread = lax.optimization_barrier(jnp.mean(center * center, axis=-1, keepdims=True))
    normed = center * lax.rsqrt(spread + EPS)
    heads, row_count, head_dim = normed.shape
    flat = normed.transpose(1, 0, 2).reshape(row_count, heads * head_dim) * gn_gain
    return (flat + skip * conv_act) * jax.nn.silu(outgate)

def reference(stream, ln_gain, up_x, up_z, conv_w, conv_b, qkv_w, gate_w, gate_bias, gn_gain, skip, down_w, cotangent, lengths):
    positions = jnp.arange(TOKENS, dtype=jnp.int32)
    segment, starting = seq_layout(positions, lengths)
    same_seq = conv_masks(0, TOKENS, KW, lengths, segment)
    block_len = math.gcd(TOKENS, 512)
    block_count = TOKENS // block_len

    def blocks(values):
        return values.reshape(NH, block_count, block_len, values.shape[-1]).transpose(1, 0, 2, 3)

    def gate_blocks(values):
        return values.reshape(NH, block_count, block_len).transpose(1, 0, 2)

    def step(state_in, inputs):
        query_blk, key_blk, value_blk, in_blk, keep_blk, seg_blk, start_blk = inputs
        hidden = jax.vmap(cell_out, in_axes=(0, 0, 0, 0, 0, None, None, 0))(query_blk, key_blk, value_blk, in_blk, keep_blk, seg_blk, start_blk, state_in)
        state_end, decay = jax.vmap(cell_end, in_axes=(0, 0, 0, 0, None, None))(key_blk, value_blk, in_blk, keep_blk, seg_blk, start_blk)
        return (decay[:, None, None] * state_in + state_end, hidden)

    def mix_cells(queries, key_rows, val_rows, gates):
        inputs = (blocks(split_heads(queries, NH)), blocks(split_heads(key_rows, NH)), blocks(split_heads(val_rows, NH)), gate_blocks(gates[0]), gate_blocks(jax.nn.log_sigmoid(gates[1])), segment.reshape(block_count, block_len), starting.reshape(block_count, block_len))
        init = jnp.zeros((NH, DH, DH), jnp.float32)
        unused, hidden = lax.scan(jax.checkpoint(step), init, inputs)
        return hidden.transpose(1, 0, 2, 3).reshape(NH, TOKENS, DH)

    def forward(stream32, ln_gain, up_x, up_z, conv_w, conv_b, qkv_w, gate_w, gate_bias, gn_gain, skip, down_w):
        normed = layer_norm(stream32, ln_gain)
        mixed = matmul(normed, up_x)
        outgate = matmul(normed, up_z)
        rim_rows = jnp.zeros((KW - 1, INNER), jnp.float32)
        conv_act, queries, key_rows, val_rows, gate_part = front(mixed, rim_rows, conv_w, conv_b, qkv_w, gate_w, same_seq)
        gate_rows = gate_part.reshape(2, NH, TOKENS)
        gates = jnp.stack([gate_rows[0], gate_rows[1] + gate_bias[:, None]])
        hidden = mix_cells(queries, key_rows, val_rows, gates)
        gated = finish(hidden, conv_act, outgate, gn_gain, skip)
        branch = matmul(gated, down_w)
        return (stream32 + branch, branch)
    stream32 = stream.astype(jnp.float32)
    (result, branch), pull = jax.vjp(forward, stream32, ln_gain, up_x, up_z, conv_w, conv_b, qkv_w, gate_w, gate_bias, gn_gain, skip, down_w)
    grads = pull((cotangent.astype(jnp.float32), jnp.zeros_like(branch)))
    rms_pair = jnp.sqrt(jnp.stack([jnp.mean(result * result), jnp.mean(branch * branch)]))
    return (result.astype(jnp.bfloat16), rms_pair, grads[0], grads[2], grads[3], grads[11], grads[1], grads[4], grads[5], grads[6], grads[7], grads[8], grads[9], grads[10])
```

```python
import functools
import math

import jax
import jax.numpy as jnp
from jax import lax
from jax.experimental import pallas as pl
from jax.experimental.pallas import tpu as pltpu
from jax.sharding import PartitionSpec as P

EPS = 1e-05
F32, BF16, I16, I32 = jnp.float32, jnp.bfloat16, jnp.int16, jnp.int32
HALO = 16
CT = 256
UNIT = math.log(2.0) / 256.0
NN = (((1,), (0,)), ((), ()))
NT = (((1,), (1,)), ((), ()))
TN = (((0,), (0,)), ((), ()))
SEGS = 4


def iota(shape, dim):
    return lax.broadcasted_iota(I32, shape, dim)


def split(a):
    hi = a.astype(BF16)
    return hi, (a - hi.astype(F32)).astype(BF16)


def mm(a, b, dims):
    return lax.dot_general(a, b, dims, preferred_element_type=F32)


def mm3(a, b, dims):
    return mm(a[0], b[0], dims) + (mm(a[0], b[1], dims) + mm(a[1], b[0], dims))


def to_row(col, width):
    rows = col.shape[0]
    same = iota((rows, width), 0) == iota((rows, width), 1)
    return jnp.sum(jnp.where(same, col, 0.0), axis=0, keepdims=True)


def to_col(row, rows):
    width = row.shape[1]
    same = iota((rows, width), 0) == iota((rows, width), 1)
    return jnp.sum(jnp.where(same, row, 0.0), axis=1, keepdims=True)


def tile(ct):
    return slice(ct * CT, (ct + 1) * CT)


def up(n, to):
    return (n + to - 1) // to * to


def seg_at(first, shape, dim, sc):
    p = first + iota(shape, dim)
    total = jnp.zeros(shape, I32)
    for i in range(SEGS):
        total = total + jnp.where(p >= sc[2 + i], 1, 0)
    return total


def quantize(get, pay, rows, nt):
    amax = jnp.zeros((rows, 1), F32)
    for ct in range(nt):
        amax = jnp.maximum(amax, jnp.max(jnp.abs(get(ct)), axis=1, keepdims=True))
    code = jnp.ceil(jnp.log(jnp.maximum(amax, 1e-30) * (1.0 / 32767.0)) * (1.0 / UNIT))
    inv = jnp.exp(code * (-UNIT))
    for ct in range(nt):
        q = jnp.floor(get(ct) * inv + 0.5)
        q = jnp.minimum(jnp.maximum(q, -32767.0), 32767.0)
        pay[0:rows, tile(ct)] = q.astype(I32).astype(I16)
    width = up(rows, 128)
    pay[rows : rows + 16, :] = jnp.zeros((16, nt * CT), I16)
    row = to_row(code, width)
    pay[rows : rows + 16, 0:width] = jnp.broadcast_to(row, (16, width)).astype(I32).astype(I16)


def scales_of(codes, rows):
    row = codes.astype(I32).astype(F32)[0:1, :]
    return jnp.exp(to_col(row, rows) * UNIT)


def conv_masks(base, rows, kw, sc):
    here = seg_at(base, (rows, 1), 0, sc)
    out = []
    for tap in range(kw):
        there = seg_at(base - (kw - 1) + tap, (rows, 1), 0, sc)
        out.append(jnp.where(there == here, 1.0, 0.0))
    return out


def conv_tile(ext, ct, cw, cb, masks):
    kw, rows = len(masks), masks[0].shape[0]
    total = jnp.broadcast_to(cb[:, tile(ct)], (rows, CT))
    for tap in range(kw):
        at = HALO - (kw - 1) + tap
        total = total + cw[tap : tap + 1, tile(ct)] * (ext[at : at + rows, tile(ct)] * masks[tap])
    return total


def sigmoid(v):
    return 1.0 / (1.0 + jnp.exp(-v))


def weight_of(allowed, expo):
    return jnp.where(allowed, jnp.exp(jnp.where(allowed, expo, 0.0)), 0.0)


def call(kernel, ins, outs, grid=None, in_specs=None, out_specs=None, scratch=(), aliases=None, macs=0):
    whole = pl.BlockSpec(memory_space=pltpu.VMEM)
    if in_specs is None:
        in_specs = [None] * len(ins)
    if out_specs is None:
        out_specs = [None] * len(outs)
    in_specs = [whole if s is None else s for s in in_specs]
    out_specs = [whole if s is None else s for s in out_specs]
    size = sum(math.prod(a.shape) * a.dtype.itemsize for a in list(ins) + list(outs))
    return pl.pallas_call(
        kernel,
        out_shape=[jax.ShapeDtypeStruct(o.shape, o.dtype) for o in outs],
        grid=() if grid is None else grid,
        in_specs=in_specs,
        out_specs=out_specs,
        scratch_shapes=list(scratch),
        input_output_aliases=aliases or {},
        compiler_params=pltpu.CompilerParams(vmem_limit_bytes=48 * 1024 * 1024),
        cost_estimate=pl.CostEstimate(flops=2 * macs, bytes_accessed=size, transcendentals=0),
    )(*ins)


def S(shape, dtype=F32):
    return jax.ShapeDtypeStruct(shape, dtype)


SMEM = pl.BlockSpec(memory_space=pltpu.SMEM)


def prep_kernel(w, bh, bl):
    for m in range(w.shape[0]):
        for ct in range(w.shape[2] // CT):
            t = w[m, :, tile(ct)]
            r, c = iota((CT, CT), 0), iota((CT, CT), 1)
            group = w.shape[1]
            first = c - lax.rem(c, group)
            out = jnp.zeros((CT, CT), F32)
            for j in range(group):
                out = jnp.where(r == first + j, jnp.broadcast_to(t[j : j + 1, :], (CT, CT)), out)
            hi, lo = split(out)
            bh[m, ct], bl[m, ct] = hi, lo


def proj_kernel(send, x, w, g, *refs):
    out, stat = refs[0], refs[1]
    pay = refs[2] if send else None
    acc, cs, mu, rs = refs[-4:]
    k, last = pl.program_id(0), pl.num_programs(0) - 1
    rows, width = x.shape
    nt = w.shape[1] // CT

    @pl.when(k == 0)
    def _():
        total = jnp.zeros((rows, 1), F32)
        for i in range(width // CT):
            total = total + jnp.sum(x[:, tile(i)].astype(F32), axis=1, keepdims=True)
        mean = total * (1.0 / width)
        total = jnp.zeros((rows, 1), F32)
        for i in range(width // CT):
            d = x[:, tile(i)].astype(F32) - mean
            total = total + jnp.sum(d * d, axis=1, keepdims=True)
        mu[...] = mean
        rs[...] = lax.rsqrt(total * (1.0 / width) + EPS)
        acc[...] = jnp.zeros_like(acc)
        cs[...] = jnp.zeros_like(cs)

    gain = to_col(g[0], CT)
    xt = x[:, pl.ds(pl.multiple_of(k * CT, CT), CT)]
    for ct in range(nt):
        wt = w[:, tile(ct)] * gain
        hi, lo = split(wt)
        acc[:, tile(ct)] += mm(xt, hi, NN) + mm(xt, lo, NN)
        cs[:, tile(ct)] += jnp.sum(wt, axis=0, keepdims=True)

    @pl.when(k == last)
    def _():
        for ct in range(nt):
            out[:, tile(ct)] = (acc[:, tile(ct)] - mu[...] * cs[:, tile(ct)]) * rs[...]
        lane = iota((rows, 128), 1)
        stat[...] = jnp.where(lane == 0, mu[...], rs[...])
        if send:
            quantize(lambda ct: out[:, tile(ct)], pay, rows, nt)


def proj(x, w, gain, send):
    rows, width = x.shape
    cols = w.shape[1]
    g = gain.reshape(width // CT, 1, CT)
    outs = [S((rows, cols)), S((rows, 128))] + ([S((rows + 16, cols), I16)] if send else [])
    return call(
        functools.partial(proj_kernel, send),
        [x, w, g],
        outs,
        grid=(width // CT,),
        in_specs=[
            pl.BlockSpec((rows, width), lambda k: (0, 0)),
            pl.BlockSpec((CT, cols), lambda k: (k, 0)),
            pl.BlockSpec((1, 1, CT), lambda k: (k, 0, 0)),
        ],
        out_specs=[pl.BlockSpec(o.shape, lambda k: (0, 0)) for o in outs],
        scratch=[
            pltpu.VMEM((rows, cols), F32),
            pltpu.VMEM((1, cols), F32),
            pltpu.VMEM((rows, 1), F32),
            pltpu.VMEM((rows, 1), F32),
        ],
        macs=2 * rows * width * cols,
    )


def dgated_kernel(g, w, out):
    hi, lo = split(w[...])
    out[...] = mm(g[...], hi, NT) + mm(g[...], lo, NT)


def dgated(g, w):
    rows, width = g.shape
    cols = w.shape[0]
    return call(
        dgated_kernel,
        [g, w],
        [S((rows, cols))],
        grid=(cols // CT,),
        in_specs=[
            pl.BlockSpec((rows, width), lambda i: (0, 0)),
            pl.BlockSpec((CT, width), lambda i: (i, 0)),
        ],
        out_specs=[pl.BlockSpec((rows, CT), lambda i: (0, i))],
        macs=2 * rows * width * cols,
    )[0]


def front_kernel(sc, ext, bh, bl, cw, cb, gw, act, qh, ql, kh, kl, vh, vl, gates):
    rows = act.shape[0]
    nt = act.shape[1] // CT
    masks = conv_masks(sc[0] * rows, rows, cw.shape[0], sc)
    total = jnp.zeros((16, rows), F32)
    for ct in range(nt):
        c = conv_tile(ext, ct, cw, cb, masks)
        a = c * sigmoid(c)
        act[:, tile(ct)] = a
        a2 = split(a)
        m2 = split(ext[HALO : HALO + rows, tile(ct)])
        for m, (src, oh, ol) in enumerate(((a2, qh, ql), (a2, kh, kl), (m2, vh, vl))):
            y = split(mm3(src, (bh[m, ct], bl[m, ct]), NN))
            oh[:, tile(ct)], ol[:, tile(ct)] = y
            total = total + mm3(split(gw[m, :, tile(ct)]), y, NT)
    gates[...] = total[0:8, :]


def gate_kernel(sc, parts, bias, out):
    heads = parts.shape[0]
    width = parts.shape[2]
    rows8 = parts[0]
    for h in range(1, heads):
        rows8 = rows8 + parts[h]
    hd = sc[1]
    r = iota((8, width), 0)
    gi = jnp.sum(jnp.where(r == hd, rows8, 0.0), axis=0, keepdims=True)
    gf = jnp.sum(jnp.where(r == hd + heads, rows8, 0.0), axis=0, keepdims=True)
    b = jnp.float32(0.0)
    for h in range(heads):
        b = jnp.where(hd == h, bias[h], b)
    gf = gf + b
    u = jnp.exp(-jnp.abs(gf))
    w = 1.0 + u
    log1p = jnp.where(w == 1.0, u, jnp.log(w) * (u / jnp.where(w == 1.0, 1.0, w - 1.0)))
    keep = jnp.minimum(gf, 0.0) - log1p
    leave = jnp.where(gf >= 0.0, u, 1.0) / w
    upto = iota((width, width), 1) <= iota((width, width), 0)
    run = to_row(jnp.sum(jnp.where(upto, keep, 0.0), axis=1, keepdims=True), width)
    end = jnp.sum(keep, axis=1, keepdims=True)
    vals = [gi - run + end, run, jnp.broadcast_to(end, (1, width)), leave, gi, gi - run]
    res = jnp.zeros((8, width), F32)
    for i, v in enumerate(vals):
        res = jnp.where(r == i, v, res)
    out[...] = res


def between(gv, n, dist, later):
    total = jnp.zeros((1, gv.shape[2]), F32)
    for s in range(1, n - 1):
        total = total + jnp.where(s < dist, gv[n - s if later else s, 2:3, :], 0.0)
    return total


def local_kernel(sc, qh, ql, kh, kl, vh, vl, gv, hid):
    rows, cols = hid.shape
    nt = cols // CT
    s = jnp.zeros((rows, rows), F32)
    for ct in range(nt):
        s = s + mm3((qh[:, tile(ct)], ql[:, tile(ct)]), (kh[:, tile(ct)], kl[:, tile(ct)]), NT)
    base = sc[0] * rows
    allowed = (iota((rows, rows), 0) >= iota((rows, rows), 1)) & (
        seg_at(base, (rows, 1), 0, sc) == seg_at(base, (1, rows), 1, sc)
    )
    w = weight_of(allowed, to_col(gv[1:2, :], rows) + gv[5:6, :])
    p = split(s * (1.0 / math.sqrt(cols)) * w)
    for ct in range(nt):
        hid[:, tile(ct)] = mm3(p, (vh[:, tile(ct)], vl[:, tile(ct)]), NN)


def block_kernel(n, slot, first, *refs):
    sc, pay, qh, ql, gv, bh, bl, cw, cb, hid_in = refs[:10]
    hid, ah, al, vh, vl, ext = refs[-6:]
    rows, cols = hid.shape
    nt = cols // CT
    me, src = sc[0], sc[6 + slot]
    scale = scales_of(pay[HALO + rows : 2 * HALO + rows, 0 : up(HALO + rows, 128)], HALO + rows)
    for ct in range(nt):
        ext[:, tile(ct)] = pay[0 : HALO + rows, tile(ct)].astype(I32).astype(F32) * scale
    masks = conv_masks(src * rows, rows, cw.shape[0], sc)

    def act(ct):
        c = conv_tile(ext, ct, cw, cb, masks)
        return split(c * sigmoid(c))

    @pl.when(src < me)
    def _():
        s = jnp.zeros((rows, rows), F32)
        for ct in range(nt):
            k2 = split(mm3(act(ct), (bh[1, ct], bl[1, ct]), NN))
            ah[0, :, tile(ct)], al[0, :, tile(ct)] = k2
            m2 = split(ext[HALO : HALO + rows, tile(ct)])
            v2 = split(mm3(m2, (bh[2, ct], bl[2, ct]), NN))
            vh[0, :, tile(ct)], vl[0, :, tile(ct)] = v2
            s = s + mm3((qh[:, tile(ct)], ql[:, tile(ct)]), k2, NT)
        w = pair_weight(n, sc, gv, me, src, rows)
        p = split(s * (1.0 / math.sqrt(cols)) * w)
        for ct in range(nt):
            hid[:, tile(ct)] = hid_in[:, tile(ct)] + mm3(
                p, (vh[0, :, tile(ct)], vl[0, :, tile(ct)]), NN
            )

    @pl.when(src > me)
    def _():
        for ct in range(nt):
            q2 = split(mm3(act(ct), (bh[0, ct], bl[0, ct]), NN))
            ah[0, :, tile(ct)], al[0, :, tile(ct)] = q2
        hid[...] = hid_in[...]


def pair_weight(n, sc, gv, me, src, rows):
    at = lax.rem(me - src + n, n)
    allowed = seg_at(me * rows, (rows, 1), 0, sc) == seg_at(src * rows, (1, rows), 1, sc)
    expo = to_col(gv[0, 1:2, :], rows) + (between(gv, n, me - src, False) + gv[at, 0:1, :])
    return weight_of(allowed, expo)


def finish_kernel(hid, act, z, dg, gn, sk, st, gh, gl, zh, zl, dh, dl, dact, rowtot, sums, payd, payg, payz, buf, norm):
    rows, cols = hid.shape
    nt = cols // CT
    total = jnp.zeros((rows, 1), F32)
    for ct in range(nt):
        total = total + jnp.sum(hid[:, tile(ct)], axis=1, keepdims=True)
    mean = total * (1.0 / cols)
    total = jnp.zeros((rows, 1), F32)
    for ct in range(nt):
        d = hid[:, tile(ct)] - mean
        total = total + jnp.sum(d * d, axis=1, keepdims=True)
    rstd = lax.rsqrt(total * (1.0 / cols) + EPS)
    m1 = jnp.zeros((rows, 1), F32)
    m2 = jnp.zeros((rows, 1), F32)
    xm, xr = st[:, 0:1], st[:, 1:2]
    r8 = iota((8, CT), 0)
    for ct in range(nt):
        t = tile(ct)
        n = (hid[:, t] - mean) * rstd
        a = act[:, t]
        full = n * gn[:, t] + sk[:, t] * a
        zz = z[:, t]
        sg = sigmoid(zz)
        gate = zz * sg
        gated = full * gate
        buf[0, :, t] = gated
        gh[:, t], gl[:, t] = split(gated)
        dgt = dg[:, t]
        da = dgt * gate
        dz = dgt * full * (sg * (1.0 + zz * (1.0 - sg)))
        zh[:, t], zl[:, t] = split(dz)
        dzr = dz * xr
        buf[1, :, t] = dzr
        dact[:, t] = da * sk[:, t]
        dn = da * gn[:, t]
        buf[2, :, t] = dn
        norm[:, t] = n
        m1 = m1 + jnp.sum(dn, axis=1, keepdims=True)
        m2 = m2 + jnp.sum(dn * n, axis=1, keepdims=True)
        s0 = jnp.sum(da * n, axis=0, keepdims=True)
        s1 = jnp.sum(da * a, axis=0, keepdims=True)
        s2 = jnp.sum(dzr * xm, axis=0, keepdims=True)
        sums[:, t] = jnp.where(r8 == 0, s0, jnp.where(r8 == 1, s1, jnp.where(r8 == 2, s2, 0.0)))
    m1, m2 = m1 * (1.0 / cols), m2 * (1.0 / cols)
    total = jnp.zeros((rows, 1), F32)
    for ct in range(nt):
        t = tile(ct)
        d = rstd * (buf[2, :, t] - m1 - norm[:, t] * m2)
        buf[2, :, t] = d
        dh[:, t], dl[:, t] = split(d)
        total = total + jnp.sum(d * hid[:, t], axis=1, keepdims=True)
    rowtot[...] = jnp.broadcast_to(total, rowtot.shape)
    quantize(lambda ct: buf[2, :, tile(ct)], payd, rows, nt)
    quantize(lambda ct: buf[0, :, tile(ct)], payg, rows, nt)
    quantize(lambda ct: buf[1, :, tile(ct)], payz, rows, nt)


def branch_kernel(gh, gl, w, out):
    out[...] = mm3((gh[...], gl[...]), split(w[...]), NN)


def branch_of(gh, gl, w):
    rows, cols = gh.shape
    width = w.shape[1]
    return call(
        branch_kernel,
        [gh, gl, w],
        [S((rows, width))],
        grid=(width // CT,),
        in_specs=[
            pl.BlockSpec((rows, cols), lambda i: (0, 0)),
            pl.BlockSpec((rows, cols), lambda i: (0, 0)),
            pl.BlockSpec((cols, CT), lambda i: (0, i)),
        ],
        out_specs=[pl.BlockSpec((rows, CT), lambda i: (0, i))],
        macs=3 * rows * width * cols,
    )[0]


def local_back_kernel(sc, qh, ql, kh, kl, vh, vl, dh, dl, gv, dq, dk, dv, col):
    rows, cols = dq.shape
    nt = cols // CT
    st = jnp.zeros((rows, rows), F32)
    dpt = jnp.zeros((rows, rows), F32)
    for ct in range(nt):
        t = tile(ct)
        st = st + mm3((kh[:, t], kl[:, t]), (qh[:, t], ql[:, t]), NT)
        dpt = dpt + mm3((vh[:, t], vl[:, t]), (dh[:, t], dl[:, t]), NT)
    base = sc[0] * rows
    allowed = (iota((rows, rows), 1) >= iota((rows, rows), 0)) & (
        seg_at(base, (rows, 1), 0, sc) == seg_at(base, (1, rows), 1, sc)
    )
    w = weight_of(allowed, gv[1:2, :] + to_col(gv[5:6, :], rows))
    scaled = w * (1.0 / math.sqrt(cols))
    pt = st * scaled
    dst = dpt * scaled
    col[...] = jnp.broadcast_to(jnp.sum(dpt * pt, axis=1, keepdims=True), col.shape)
    pt2, dst2, ds2 = split(pt), split(dst), split(dst.T)
    for ct in range(nt):
        t = tile(ct)
        dv[:, t] = mm3(pt2, (dh[:, t], dl[:, t]), NN)
        dk[:, t] = mm3(dst2, (qh[:, t], ql[:, t]), NN)
        dq[:, t] = mm3(ds2, (kh[:, t], kl[:, t]), NN)


def earlier_kernel(n, sc, ah, al, bh, bl, dh, dl, qh, ql, gv, dq_in, dq, vec):
    rows, cols = dq.shape
    nt = cols // CT
    i = pl.program_id(0)
    me, src = sc[0], sc[6 + i]

    @pl.when(i == 0)
    def _():
        dq[...] = dq_in[...]
        vec[...] = jnp.zeros_like(vec)

    @pl.when(src < me)
    def _():
        dp = jnp.zeros((rows, rows), F32)
        for ct in range(nt):
            t = tile(ct)
            dp = dp + mm3((dh[:, t], dl[:, t]), (bh[0, :, t], bl[0, :, t]), NT)
        ds = split(dp * pair_weight(n, sc, gv, me, src, rows) * (1.0 / math.sqrt(cols)))
        total = jnp.zeros((rows, 1), F32)
        for ct in range(nt):
            t = tile(ct)
            part = mm3(ds, (ah[0, :, t], al[0, :, t]), NN)
            dq[:, t] += part
            q = qh[:, t].astype(F32) + ql[:, t].astype(F32)
            total = total + jnp.sum(part * q, axis=1, keepdims=True)
        flow = jnp.sum(total, axis=0, keepdims=True)
        lane = iota(vec.shape, 1)
        vec[...] += jnp.where((lane > src) & (lane < me), flow, 0.0)


def earlier(n, sc, bufs, dh, dl, qh, ql, gv, dq_in):
    rows, cols = dq_in.shape
    fixed2 = pl.BlockSpec((rows, cols), lambda i: (0, 0))
    moving = pl.BlockSpec((1, rows, cols), lambda i: (i, 0, 0))
    return call(
        functools.partial(earlier_kernel, n),
        [sc, *bufs, dh, dl, qh, ql, gv, dq_in],
        [S((rows, cols)), S((8, 128))],
        grid=(n - 1,),
        in_specs=[SMEM] + [moving] * 4 + [fixed2] * 4 + [pl.BlockSpec(gv.shape, lambda i: (0, 0, 0)), fixed2],
        out_specs=[fixed2, pl.BlockSpec((8, 128), lambda i: (0, 0))],
        macs=(n - 1) * 6 * rows * rows * cols // 2,
    )


def later_kernel(n, slot, sc, pay, ah, al, kh, kl, vh, vl, gv, dk_in, dv_in, col_in, dk, dv, col, ph, pl_):
    rows, cols = dk.shape
    nt = cols // CT
    me, src = sc[0], sc[6 + slot]

    @pl.when(src < me)
    def _():
        dk[...] = dk_in[...]
        dv[...] = dv_in[...]
        col[...] = col_in[...]

    @pl.when(src > me)
    def _():
        scale = scales_of(pay[rows : rows + 16, 0:rows], rows)
        st = jnp.zeros((rows, rows), F32)
        dpt = jnp.zeros((rows, rows), F32)
        for ct in range(nt):
            t = tile(ct)
            d2 = split(pay[0:rows, t].astype(I32).astype(F32) * scale)
            ph[:, t], pl_[:, t] = d2
            st = st + mm3((kh[:, t], kl[:, t]), (ah[0, :, t], al[0, :, t]), NT)
            dpt = dpt + mm3((vh[:, t], vl[:, t]), d2, NT)
        at = lax.rem(me - src + n, n)
        allowed = seg_at(me * rows, (rows, 1), 0, sc) == seg_at(src * rows, (1, rows), 1, sc)
        expo = to_col(gv[0, 0:1, :], rows) + (between(gv, n, src - me, True) + gv[at, 1:2, :])
        scaled = weight_of(allowed, expo) * (1.0 / math.sqrt(cols))
        pt = st * scaled
        col[...] = col_in[...] + jnp.sum(dpt * pt, axis=1, keepdims=True)
        pt2, dst2 = split(pt), split(dpt * scaled)
        for ct in range(nt):
            t = tile(ct)
            dv[:, t] = dv_in[:, t] + mm3(pt2, (ph[:, t], pl_[:, t]), NN)
            dk[:, t] = dk_in[:, t] + mm3(dst2, (ah[0, :, t], al[0, :, t]), NN)


def gate_back_kernel(sc, col_here, col_later, rowtot, gv, vec, out):
    rows = rowtot.shape[0]
    here, later = col_here[:, 0:1], col_later[:, 0:1]
    t, p = iota((rows, rows), 1), iota((rows, rows), 0)
    val = to_row(rowtot[:, 0:1] - here, rows)
    dlk = jnp.sum(jnp.where(t >= p, val, 0.0), axis=1, keepdims=True)
    dlk = dlk + jnp.sum(jnp.where(t < p, to_row(later, rows), 0.0), axis=1, keepdims=True)
    lane = iota((1, 128), 1)
    dlk = dlk + jnp.sum(jnp.where(lane == sc[0], vec[0:1, :], 0.0), axis=1, keepdims=True)
    r = iota((8, rows), 0)
    d_in = to_row(here + later, rows)
    d_f = to_row(dlk, rows) * gv[3:4, :]
    out[...] = jnp.where(r == 0, d_in, jnp.where(r == 1, d_f, 0.0))


def back_kernel(sc, ext, act, dact, dq, dk1, dk2, dv1, dv2, qh, ql, kh, kl, vh, vl, bh, bl, cw, cb, gw, dg, dm, rim, pack, dcs):
    rows, cols = act.shape
    nt = cols // CT
    kw = cw.shape[0]
    heads = dg.shape[0]
    base = sc[0] * rows
    masks = conv_masks(base, rows, kw, sc)
    ext_rows = HALO + rows
    here = seg_at(base - HALO, (ext_rows, 1), 0, sc)
    back_masks = []
    for tap in range(kw):
        there = seg_at(base - HALO + kw - 1 - tap, (ext_rows, 1), 0, sc)
        back_masks.append(jnp.where(there == here, 1.0, 0.0))
    r16 = iota((16, rows), 0)
    g = jnp.zeros((16, rows), F32)
    for h in range(heads):
        g = jnp.where(r16 == h, dg[h, 0:1, :], g)
        g = jnp.where(r16 == heads + h, dg[h, 1:2, :], g)
    g2 = split(g)
    pack[...] = jnp.zeros_like(pack)
    bias = to_row(jnp.sum(g, axis=1, keepdims=True), 128)
    pack[41:42, 0:128] = bias
    group = 4
    sub = iota((CT, CT), 0)
    lane = iota((CT, CT), 1)
    first = lane - lax.rem(lane, group)
    dcs[0:HALO, :] = jnp.zeros((HALO, CT), F32)
    dcs[HALO + rows : 2 * HALO + rows, :] = jnp.zeros((HALO, CT), F32)
    for ct in range(nt):
        t = tile(ct)
        a2 = split(act[:, t])
        m2 = split(ext[HALO : HALO + rows, t])
        grads = (dq[:, t], dk1[:, t] + dk2[:, t], dv1[:, t] + dv2[:, t])
        stored = ((qh, ql), (kh, kl), (vh, vl))
        back = []
        for m in range(3):
            d2 = split(grads[m] + mm3(g2, split(gw[m, :, t]), TN))
            back.append(mm3(d2, (bh[m, ct], bl[m, ct]), NT))
            gate_rows = mm3(g2, (stored[m][0][:, t], stored[m][1][:, t]), NN)
            pack[17 + 8 * m : 25 + 8 * m, t] = gate_rows[0:8, :]
            outer = mm3(a2 if m < 2 else m2, d2, TN)
            for j in range(group):
                pack[5 + group * m + j : 6 + group * m + j, t] = jnp.sum(
                    jnp.where(sub == first + j, outer, 0.0), axis=0, keepdims=True
                )
        c = conv_tile(ext, ct, cw, cb, masks)
        sg = sigmoid(c)
        dc = (dact[:, t] + back[0] + back[1]) * (sg * (1.0 + c * (1.0 - sg)))
        pack[4:5, t] = jnp.sum(dc, axis=0, keepdims=True)
        for tap in range(kw):
            at = HALO - (kw - 1) + tap
            pack[tap : tap + 1, t] = jnp.sum(dc * (ext[at : at + rows, t] * masks[tap]), axis=0, keepdims=True)
        dcs[HALO : HALO + rows, :] = dc
        dext = jnp.zeros((ext_rows, CT), F32)
        for tap in range(kw):
            at = kw - 1 - tap
            dext = dext + cw[tap : tap + 1, t] * (dcs[at : at + ext_rows, :] * back_masks[tap])
        rim[:, t] = dext[0:HALO, :]
        dm[:, t] = dext[HALO:, :] + back[2]


def send_kernel(dm, rim, st, mh, ml, pay, ux, buf):
    rows, cols = dm.shape
    nt = cols // CT
    xm, xr = st[:, 0:1], st[:, 1:2]
    for ct in range(nt):
        t = tile(ct)
        buf[:, t] = dm[:, t]
        buf[rows - HALO : rows, t] = dm[rows - HALO : rows, t] + rim[:, t]
        d = buf[:, t]
        mh[:, t], ml[:, t] = split(d)
        d = d * xr
        buf[:, t] = d
        ux[:, t] = jnp.broadcast_to(jnp.sum(d * xm, axis=0, keepdims=True), (8, CT))
    quantize(lambda ct: buf[:, tile(ct)], pay, rows, nt)


def dnorm_kernel(mh, ml, zh, zl, wx, wz, g, x, st, out, ln):
    gain = to_col(g[0], CT)
    a = mm3((zh[...], zl[...]), split(wz[...] * gain), NT)
    a = a + mm3((mh[...], ml[...]), split(wx[...] * gain), NT)
    out[...] = a
    xhat = (x[...].astype(F32) - st[:, 0:1]) * st[:, 1:2]
    ln[0] = jnp.sum(a * xhat, axis=0, keepdims=True) / g[0]


def dnorm(mh, ml, zh, zl, wx, wz, gain, x, st):
    rows, cols = mh.shape
    width = wx.shape[0]
    fixed = pl.BlockSpec((rows, cols), lambda i: (0, 0))
    moving = pl.BlockSpec((CT, cols), lambda i: (i, 0))
    g = gain.reshape(width // CT, 1, CT)
    gspec = pl.BlockSpec((1, 1, CT), lambda i: (i, 0, 0))
    out, ln = call(
        dnorm_kernel,
        [mh, ml, zh, zl, wx, wz, g, x, st],
        [S((rows, width)), S((width // CT, 1, CT))],
        grid=(width // CT,),
        in_specs=[fixed] * 4 + [moving] * 2 + [gspec, pl.BlockSpec((rows, CT), lambda i: (0, i)), pl.BlockSpec((rows, 128), lambda i: (0, 0))],
        out_specs=[pl.BlockSpec((rows, CT), lambda i: (0, i)), gspec],
        macs=6 * rows * width * cols,
    )
    return out, ln.reshape(width)


def wgrad_kernel(left, pay, codes, out):
    m = left.shape[0]
    rows = left.shape[2]
    total = jnp.zeros(out.shape, F32)
    for s in range(m):
        scale = scales_of(codes[s], rows)
        hi, lo = split(pay[s].astype(I32).astype(F32) * scale)
        total = total + (mm(left[s], hi, NN) + mm(left[s], lo, NN))
    out[...] = total


def wgrad(left, half, pay):
    m, both, rows = left.shape
    feats = both // 2
    cols = pay.shape[2]
    return call(
        wgrad_kernel,
        [left, pay, pay],
        [S((feats, cols))],
        grid=(cols // CT,),
        in_specs=[
            pl.BlockSpec((m, feats, rows), lambda i: (0, half, 0)),
            pl.BlockSpec((m, rows, CT), lambda i: (0, 0, i)),
            pl.BlockSpec((m, 16, rows), lambda i: (0, rows // 16, 0)),
        ],
        out_specs=[pl.BlockSpec((feats, CT), lambda i: (0, i))],
        macs=2 * m * feats * rows * cols,
    )[0]


def shifted(a, by):
    n = lax.axis_size("seq")
    return lax.ppermute(a, "seq", [(i, (i + by) % n) for i in range(n)])


def swapped(a, axis, bit):
    n = lax.axis_size(axis)
    return lax.ppermute(a, axis, [(i, i ^ bit) for i in range(n)])


def sum_over(a, axis):
    bit = 1
    while bit < lax.axis_size(axis):
        a = a + swapped(a, axis, bit)
        bit *= 2
    return a


def gather_runs(pay):
    n = lax.axis_size("seq")
    if n != 8:
        return [shifted(pay, s) for s in range(1, n)]
    half = pay.shape[0] // 2
    x = swapped(pay, "seq", 1)
    above, below = shifted(pay, -2), shifted(pay, 2)
    from_above = shifted(jnp.concatenate([above[:half], x[:half]]), -2)
    from_below = shifted(jnp.concatenate([below[half:], x[:half]]), 2)
    from_side = swapped(jnp.concatenate([above[half:], below[half:]]), "seq", 1)
    x_above = jnp.concatenate([from_above[half:], from_side[:half]])
    x_below = jnp.concatenate([from_below[half:], from_side[half:]])
    across = jnp.concatenate([from_above[:half], from_below[:half]])
    return [x, above, below, x_above, x_below, across, swapped(across, "seq", 1)]


def sources(me, n):
    if n != 8:
        return [lax.rem(me - s + n, n) for s in range(1, n)]
    z, x = me // 2, lax.rem(me, 2)

    def at(dz, dx):
        return lax.rem(z + dz, 4) * 2 + (1 - x if dx else x)

    return [at(0, 1), at(1, 0), at(3, 0), at(1, 1), at(3, 1), at(2, 0), at(2, 1)]


def gather_ring(pay):
    m = lax.axis_size("seq") // 2
    if m != 4:
        return jnp.stack([pay] + [shifted(pay, 2 * s) for s in range(1, m)])
    half = up(pay.shape[0] // 2, 16)
    below, above = shifted(pay, 2), shifted(pay, -2)
    across = jnp.concatenate([shifted(below[:half], 2), shifted(above[half:], -2)])
    return jnp.stack([pay, below, across, above])


def halves(a, bit_set):
    half = a.shape[0] // 2
    keep = lax.dynamic_slice_in_dim(a, jnp.where(bit_set, half, 0), half, 0)
    give = lax.dynamic_slice_in_dim(a, jnp.where(bit_set, 0, half), half, 0)
    return keep, give


def scatter_heads(a, bits):
    for bit, bit_set in bits:
        keep, give = halves(a, bit_set)
        a = keep + swapped(give, "head", bit)
    return a


def join_heads(a, bits):
    for bit, bit_set in reversed(bits):
        other = swapped(a, "head", bit)
        a = jnp.where(bit_set, jnp.concatenate([other, a]), jnp.concatenate([a, other]))
    return a


def per_device(
    stream,
    ln_gain,
    up_x,
    up_z,
    conv_w,
    conv_b,
    qkv_w,
    gate_w,
    gate_bias,
    gn_gain,
    skip,
    down_w,
    cotangent,
    lengths,
):
    rows, width = stream.shape
    cols = up_x.shape[1]
    kw = conv_w.shape[0]
    heads = gate_w.shape[0] // 2
    n = lax.axis_size("seq")
    m = n // 2
    me, hd = lax.axis_index("seq"), lax.axis_index("head")
    starts = jnp.cumsum(lengths) - lengths
    order = sources(me, n)
    sc = jnp.concatenate([jnp.stack([me, hd]), starts, jnp.stack(order)]).astype(I32)
    cb, gn, sk = conv_b.reshape(1, cols), gn_gain.reshape(1, cols), skip.reshape(1, cols)
    gw = jnp.pad(gate_w.transpose(1, 0, 2), ((0, 0), (0, 16 - 2 * heads), (0, 0)))
    tall = S((rows, cols))
    tall16 = S((rows, cols), BF16)

    halo = lax.ppermute(stream[rows - HALO :], "seq", [(i, i + 1) for i in range(n - 1)])
    outgate, stat = proj(stream, up_z, ln_gain, False)
    mixed, _, pay = proj(jnp.concatenate([halo, stream]), up_x, ln_gain, True)
    runs = gather_runs(pay)

    nt = cols // CT
    bh, bl = call(prep_kernel, [qkv_w], [S((3, nt, CT, CT), BF16)] * 2)
    act, qh, ql, kh, kl, vh, vl, gate_part = call(
        front_kernel,
        [sc, mixed, bh, bl, conv_w, cb, gw],
        [tall] + [tall16] * 6 + [S((8, rows))],
        in_specs=[SMEM] + [None] * 6,
        macs=9 * rows * cols * CT,
    )
    gate_parts = lax.all_gather(gate_part, "head")
    (gv,) = call(
        gate_kernel, [sc, gate_parts, gate_bias], [S((8, rows))], in_specs=[SMEM, None, SMEM]
    )
    gvs = jnp.stack([gv] + [shifted(gv, s) for s in range(1, n)])

    feats = width // m
    both = jnp.concatenate(
        [stream.T.reshape(m, feats, rows), cotangent.T.reshape(m, feats, rows)], axis=1
    )
    ring = me // 2
    left = jnp.stack(
        [
            shifted(lax.dynamic_index_in_dim(both, lax.rem(ring + s, m), 0, False), 2 * s)
            if s
            else lax.dynamic_index_in_dim(both, ring, 0, False)
            for s in range(m)
        ]
    )

    dgate = dgated(cotangent, down_w)
    (hid,) = call(
        local_kernel,
        [sc, qh, ql, kh, kl, vh, vl, gv],
        [tall],
        in_specs=[SMEM] + [None] * 7,
        macs=6 * rows * rows * cols,
    )
    bufs = None
    buf_shape = S((n - 1, rows, cols), BF16)
    for slot in range(n - 1):
        ins = [sc, runs[slot], qh, ql, gvs, bh, bl, conv_w, cb, hid]
        specs = [SMEM] + [None] * 9
        aliases = {9: 0}
        if bufs is not None:
            ins += bufs
            specs += [pl.BlockSpec(memory_space=pl.ANY)] * 4
            aliases.update({10 + i: 1 + i for i in range(4)})
        place = pl.BlockSpec((1, rows, cols), lambda i, slot=slot: (slot, 0, 0))
        hid, *bufs = call(
            functools.partial(block_kernel, n, slot, bufs is None),
            ins,
            [tall] + [buf_shape] * 4,
            grid=(1,),
            in_specs=specs,
            out_specs=[None] + [place] * 4,
            scratch=[pltpu.VMEM((HALO + rows, cols), F32)],
            aliases=aliases,
            macs=6 * rows * rows * cols,
        )

    gh, gl, zh, zl, dh, dl, dact, rowtot, sums, payd, payg, payz = call(
        finish_kernel,
        [hid, act, outgate, dgate, gn, sk, stat],
        [tall16] * 6 + [tall, S((rows, 128)), S((8, cols))] + [S((rows + 16, cols), I16)] * 3,
        scratch=[pltpu.VMEM((3, rows, cols), F32), pltpu.VMEM((rows, cols), F32)],
    )
    back_runs = gather_runs(payd)

    bits = [(1, lax.rem(hd, 2) == 1), (2, hd // 2 == 1)]
    share = rows // 4
    first = jnp.where(bits[0][1], rows // 2, 0) + jnp.where(bits[1][1], share, 0)
    x_share = lax.dynamic_slice_in_dim(stream, first, share, 0).astype(F32)
    branch = scatter_heads(branch_of(gh, gl, down_w), bits)
    result = x_share + branch
    output = join_heads(result.astype(BF16), bits)
    squares = jnp.stack([jnp.sum(result * result), jnp.sum(branch * branch)])

    dq, dk1, dv1, col_here = call(
        local_back_kernel,
        [sc, qh, ql, kh, kl, vh, vl, dh, dl, gv],
        [tall] * 3 + [S((rows, 128))],
        in_specs=[SMEM] + [None] * 9,
        macs=15 * rows * rows * cols,
    )
    dq, vec = earlier(n, sc, bufs, dh, dl, qh, ql, gvs, dq)
    vec = sum_over(vec, "seq")
    dk2, dv2, col_later = jnp.zeros((rows, cols)), jnp.zeros((rows, cols)), jnp.zeros((rows, 128))
    for slot in range(n - 1):
        place = pl.BlockSpec((1, rows, cols), lambda i, slot=slot: (slot, 0, 0))
        dk2, dv2, col_later = call(
            functools.partial(later_kernel, n, slot),
            [sc, back_runs[slot], bufs[0], bufs[1], kh, kl, vh, vl, gvs, dk2, dv2, col_later],
            [tall, tall, S((rows, 128))],
            grid=(1,),
            in_specs=[SMEM, None, place, place] + [None] * 8,
            scratch=[pltpu.VMEM((rows, cols), BF16)] * 2,
            aliases={9: 0, 10: 1, 11: 2},
            macs=6 * rows * rows * cols,
        )
    (dgates,) = call(
        gate_back_kernel,
        [sc, col_here, col_later, rowtot, gv, vec],
        [S((8, rows))],
        in_specs=[SMEM] + [None] * 5,
    )
    dgates = lax.all_gather(dgates, "head")
    dm, rim, pack = call(
        back_kernel,
        [sc, mixed, act, dact, dq, dk1, dk2, dv1, dv2, qh, ql, kh, kl, vh, vl, bh, bl, conv_w, cb, gw, dgates],
        [tall, S((HALO, cols)), S((48, cols))],
        in_specs=[SMEM] + [None] * 20,
        scratch=[pltpu.VMEM((2 * HALO + rows, CT), F32)],
        macs=30 * rows * cols * CT,
    )
    rim = lax.ppermute(rim, "seq", [(i + 1, i) for i in range(n - 1)])
    mh, ml, paym, ux = call(
        send_kernel,
        [dm, rim, stat],
        [tall16] * 2 + [S((rows + 16, cols), I16), S((8, cols))],
        scratch=[pltpu.VMEM((rows, cols), F32)],
    )

    dnormed, ln_part = dnorm(mh, ml, zh, zl, up_x, up_z, ln_gain, stream, stat)
    dn = scatter_heads(dnormed, bits)
    center = x_share - jnp.mean(x_share, axis=-1, keepdims=True)
    rstd = lax.rsqrt(jnp.mean(center * center, axis=-1, keepdims=True) + EPS)
    xhat = center * rstd
    dx = rstd * (
        dn
        - jnp.mean(dn, axis=-1, keepdims=True)
        - xhat * jnp.mean(dn * xhat, axis=-1, keepdims=True)
    )
    g_share = lax.dynamic_slice_in_dim(cotangent, first, share, 0).astype(F32)
    grad_stream = join_heads(g_share + dx, bits)

    def finish_grad(half, pay):
        part = wgrad(left, half, gather_ring(pay))
        keep, give = halves(part, lax.rem(me, 2) == 1)
        return keep + swapped(give, "seq", 1)

    grad_down = finish_grad(1, payg).T
    raw_z = finish_grad(0, payz)
    raw_x = finish_grad(0, paym)

    extra = jnp.zeros((1, cols)).at[0, :2].set(squares)
    small = jnp.concatenate([pack, sums, ux[:1], ln_part.reshape(width // cols, cols), extra])
    small = sum_over(small, "seq")
    tail = sum_over(small[57:], "head")
    lns = width // cols
    grad_ln = tail[:lns].reshape(width)
    rms_pair = jnp.sqrt(tail[lns, :2] / (rows * n * width))
    gain_here = lax.dynamic_slice_in_dim(ln_gain, me * (width // n), width // n, 0)[:, None]
    grad_up_x = gain_here * (raw_x - small[56:57])
    grad_up_z = gain_here * (raw_z - small[50:51])
    return (
        output,
        rms_pair,
        grad_stream,
        grad_up_x,
        grad_up_z,
        grad_down,
        grad_ln,
        small[0:kw],
        small[4],
        small[5:17].reshape(3, 4, cols),
        small[17:41].reshape(3, 2 * heads, cols).transpose(1, 0, 2),
        small[41, heads : 2 * heads],
        small[48],
        small[49],
    )


def solution(mesh):
    return jax.shard_map(
        per_device,
        mesh=mesh,
        in_specs=(
            P("seq", None),
            P(),
            P(None, "head"),
            P(None, "head"),
            P(None, "head"),
            P("head"),
            P(None, None, "head"),
            P(None, None, "head"),
            P(),
            P("head"),
            P("head"),
            P("head", None),
            P("seq", None),
            P(),
        ),
        out_specs=(
            P("seq", None),
            P(),
            P("seq", None),
            P("seq", "head"),
            P("seq", "head"),
            P("head", "seq"),
            P(),
            P(None, "head"),
            P("head"),
            P(None, None, "head"),
            P(None, None, "head"),
            P(),
            P("head"),
            P("head"),
        ),
        check_vma=False,
    )
```

```python
import functools
import math

import jax
import jax.numpy as jnp
from jax import lax
from jax.experimental import pallas as pl
from jax.experimental.pallas import tpu as pltpu
from jax.sharding import PartitionSpec as P

EPS = 1e-05
F32, BF16, I16, I32 = jnp.float32, jnp.bfloat16, jnp.int16, jnp.int32
HALO = 16
CT = 256
UNIT = math.log(2.0) / 256.0
NN = (((1,), (0,)), ((), ()))
NT = (((1,), (1,)), ((), ()))
TN = (((0,), (0,)), ((), ()))
SEGS = 4


def iota(shape, dim):
    return lax.broadcasted_iota(I32, shape, dim)


def split(a):
    hi = a.astype(BF16)
    return hi, (a - hi.astype(F32)).astype(BF16)


def mm(a, b, dims):
    return lax.dot_general(a, b, dims, preferred_element_type=F32)


def mm3(a, b, dims):
    return mm(a[0], b[0], dims) + (mm(a[0], b[1], dims) + mm(a[1], b[0], dims))


def to_row(col, width):
    rows = col.shape[0]
    same = iota((rows, width), 0) == iota((rows, width), 1)
    return jnp.sum(jnp.where(same, col, 0.0), axis=0, keepdims=True)


def to_col(row, rows):
    width = row.shape[1]
    same = iota((rows, width), 0) == iota((rows, width), 1)
    return jnp.sum(jnp.where(same, row, 0.0), axis=1, keepdims=True)


def tile(ct):
    return slice(ct * CT, (ct + 1) * CT)


def up(n, to):
    return (n + to - 1) // to * to


def seg_at(first, shape, dim, sc):
    p = first + iota(shape, dim)
    total = jnp.zeros(shape, I32)
    for i in range(SEGS):
        total = total + jnp.where(p >= sc[2 + i], 1, 0)
    return total


def quantize(get, pay, rows, nt, inside):
    amax = jnp.zeros((rows, 1), F32)
    for ct in range(nt):
        amax = jnp.maximum(amax, jnp.max(jnp.abs(get(ct)), axis=1, keepdims=True))
    code = jnp.ceil(jnp.log(jnp.maximum(amax, 1e-30) * (1.0 / 32767.0)) * (1.0 / UNIT))
    inv = jnp.exp(code * (-UNIT))
    for ct in range(nt):
        q = jnp.floor(get(ct) * inv + 0.5)
        q = jnp.minimum(jnp.maximum(q, -32767.0), 32767.0)
        pay[0:rows, tile(ct)] = q.astype(I32).astype(I16)
    width = up(rows, 128)
    codes = jnp.broadcast_to(to_row(code, width), (16, width)).astype(I32)
    if inside:
        old = pay[0:16, 0:width].astype(I32)
        pay[0:16, 0:width] = jnp.where(iota((16, width), 0) == 0, codes, old).astype(I16)
    else:
        pay[rows : rows + 16, :] = jnp.zeros((16, nt * CT), I16)
        pay[rows : rows + 16, 0:width] = codes.astype(I16)


def scales_of(codes, rows):
    row = codes.astype(I32).astype(F32)[0:1, :]
    return jnp.exp(to_col(row, rows) * UNIT)


def conv_masks(base, rows, kw, sc):
    here = seg_at(base, (rows, 1), 0, sc)
    out = []
    for tap in range(kw):
        there = seg_at(base - (kw - 1) + tap, (rows, 1), 0, sc)
        out.append(jnp.where(there == here, 1.0, 0.0))
    return out


def conv_tile(ext, ct, cw, cb, masks):
    kw, rows = len(masks), masks[0].shape[0]
    total = jnp.broadcast_to(cb[:, tile(ct)], (rows, CT))
    for tap in range(kw):
        at = HALO - (kw - 1) + tap
        total = total + cw[tap : tap + 1, tile(ct)] * (ext[at : at + rows, tile(ct)] * masks[tap])
    return total


def sigmoid(v):
    return 1.0 / (1.0 + jnp.exp(-v))


def weight_of(allowed, expo):
    return jnp.where(allowed, jnp.exp(jnp.where(allowed, expo, 0.0)), 0.0)


def call(kernel, ins, outs, grid=(1,), in_specs=None, out_specs=None, scratch=(), aliases=None, macs=0, weight=10):
    def spec_of(spec, a):
        if spec is not None:
            return spec
        zeros = (0,) * len(a.shape)
        return pl.BlockSpec(a.shape, lambda *i: zeros, pipeline_mode=pl.Buffered(1))

    in_specs = [spec_of(s, a) for s, a in zip(in_specs or [None] * len(ins), ins)]
    out_specs = [spec_of(s, a) for s, a in zip(out_specs or [None] * len(outs), outs)]
    size = sum(math.prod(a.shape) * a.dtype.itemsize for a in list(ins) + list(outs))
    base = kernel.func if isinstance(kernel, functools.partial) else kernel
    return pl.pallas_call(
        kernel,
        name=base.__name__,
        out_shape=[jax.ShapeDtypeStruct(o.shape, o.dtype) for o in outs],
        grid=grid,
        in_specs=in_specs,
        out_specs=out_specs,
        scratch_shapes=list(scratch),
        input_output_aliases=aliases or {},
        compiler_params=pltpu.CompilerParams(vmem_limit_bytes=48 * 1024 * 1024),
        cost_estimate=pl.CostEstimate(
            flops=2 * weight * macs + weight // 10 * 10**9, bytes_accessed=size, transcendentals=0
        ),
    )(*ins)


def S(shape, dtype=F32):
    return jax.ShapeDtypeStruct(shape, dtype)


SMEM = pl.BlockSpec(memory_space=pltpu.SMEM)


def prep_kernel(w, bh, bl):
    for m in range(w.shape[0]):
        for ct in range(w.shape[2] // CT):
            t = w[m, :, tile(ct)]
            r, c = iota((CT, CT), 0), iota((CT, CT), 1)
            group = w.shape[1]
            first = c - lax.rem(c, group)
            out = jnp.zeros((CT, CT), F32)
            for j in range(group):
                out = jnp.where(r == first + j, jnp.broadcast_to(t[j : j + 1, :], (CT, CT)), out)
            hi, lo = split(out)
            bh[m, ct], bl[m, ct] = hi, lo


def proj_kernel(send, x, w, g, *refs):
    out, stat = refs[0], refs[1]
    gc = refs[-1]
    k, last = pl.program_id(0), pl.num_programs(0) - 1
    rows, width = x.shape
    wide = w.shape[1]

    @pl.when(k == 0)
    def _():
        total = jnp.zeros((rows, 1), F32)
        for i in range(width // CT):
            gc[i * CT : (i + 1) * CT, :] = jnp.broadcast_to(to_col(g[:, tile(i)], CT), (CT, 128))
            total = total + jnp.sum(x[:, tile(i)].astype(F32), axis=1, keepdims=True)
        mean = total * (1.0 / width)
        total = jnp.zeros((rows, 1), F32)
        for i in range(width // CT):
            d = x[:, tile(i)].astype(F32) - mean
            total = total + jnp.sum(d * d, axis=1, keepdims=True)
        rstd = lax.rsqrt(total * (1.0 / width) + EPS)
        stat[...] = jnp.where(iota((rows, 128), 1) == 0, mean, rstd)

    acc = jnp.zeros((rows, wide), F32)
    for i in range(width // CT):
        hi, lo = split(w[i * CT : (i + 1) * CT, :] * gc[i * CT : (i + 1) * CT, 0:1])
        xt = x[:, tile(i)]
        acc = acc + (mm(xt, hi, NN) + mm(xt, lo, NN))
    at = pl.ds(pl.multiple_of(k * wide, wide), wide)
    out[:, at] = (acc - stat[:, 0:1] * acc[0:1, :]) * stat[:, 1:2]
    if send:

        @pl.when(k == last)
        def _():
            quantize(lambda ct: out[:, tile(ct)], refs[2], rows, out.shape[1] // CT, True)


def proj(x, w, gain, send):
    rows, width = x.shape
    cols = w.shape[1]
    wide = min(cols, 512)
    outs = [S((rows, cols)), S((rows, 128))] + ([S((rows, cols), I16)] if send else [])
    return call(
        functools.partial(proj_kernel, send),
        [x, w, gain.reshape(1, width)],
        outs,
        grid=(cols // wide,),
        in_specs=[
            pl.BlockSpec((rows, width), lambda k: (0, 0)),
            pl.BlockSpec((width, wide), lambda k: (0, k)),
            pl.BlockSpec((1, width), lambda k: (0, 0)),
        ],
        out_specs=[pl.BlockSpec(o.shape, lambda k: (0, 0)) for o in outs],
        scratch=[pltpu.VMEM((width, 128), F32)],
        weight=1,
        macs=2 * rows * width * cols,
    )


def dgated_kernel(g, w, out):
    acc = None
    for i in range(w.shape[1] // CT):
        hi, lo = split(w[:, tile(i)])
        part = mm(g[:, tile(i)], hi, NT) + mm(g[:, tile(i)], lo, NT)
        acc = part if acc is None else acc + part
    out[...] = acc


def dgated(g, w):
    rows, width = g.shape
    cols = w.shape[0]
    wide = min(cols, 512)
    return call(
        dgated_kernel,
        [g, w],
        [S((rows, cols))],
        grid=(cols // wide,),
        in_specs=[
            pl.BlockSpec((rows, width), lambda i: (0, 0)),
            pl.BlockSpec((wide, width), lambda i: (i, 0)),
        ],
        out_specs=[pl.BlockSpec((rows, wide), lambda i: (0, i))],
        macs=2 * rows * width * cols,
        weight=1,
    )[0]


def front_kernel(sc, ext, bh, bl, cw, cb, gw, act, qh, ql, kh, kl, vh, vl, ph, pl_, gates):
    rows = act.shape[0]
    nt = act.shape[1] // CT
    masks = conv_masks(sc[0] * rows, rows, cw.shape[0], sc)
    total = jnp.zeros((16, rows), F32)
    for ct in range(nt):
        c = conv_tile(ext, ct, cw, cb, masks)
        a = c * sigmoid(c)
        act[:, tile(ct)] = a
        a2 = split(a)
        m2 = split(ext[HALO : HALO + rows, tile(ct)])
        for m, (src, oh, ol) in enumerate(((a2, qh, ql), (a2, kh, kl), (m2, vh, vl))):
            y = split(mm3(src, (bh[m, ct], bl[m, ct]), NN))
            oh[:, tile(ct)], ol[:, tile(ct)] = y
            total = total + mm3(split(gw[m, :, tile(ct)]), y, NT)
            if m == 0:
                ph[:, tile(ct)], pl_[:, tile(ct)] = split(mm3(y, (bh[1, ct], bl[1, ct]), NT))
    gates[...] = total[0:8, :]


def gate_kernel(sc, parts, bias, out):
    heads = bias.shape[0]
    width = parts.shape[1]
    rows8 = parts[...]
    hd = sc[1]
    r = iota((8, width), 0)
    gi = jnp.sum(jnp.where(r == hd, rows8, 0.0), axis=0, keepdims=True)
    gf = jnp.sum(jnp.where(r == hd + heads, rows8, 0.0), axis=0, keepdims=True)
    b = jnp.float32(0.0)
    for h in range(heads):
        b = jnp.where(hd == h, bias[h], b)
    gf = gf + b
    u = jnp.exp(-jnp.abs(gf))
    w = 1.0 + u
    log1p = jnp.where(w == 1.0, u, jnp.log(w) * (u / jnp.where(w == 1.0, 1.0, w - 1.0)))
    keep = jnp.minimum(gf, 0.0) - log1p
    leave = jnp.where(gf >= 0.0, u, 1.0) / w
    upto = iota((width, width), 1) <= iota((width, width), 0)
    run = to_row(jnp.sum(jnp.where(upto, keep, 0.0), axis=1, keepdims=True), width)
    end = jnp.sum(keep, axis=1, keepdims=True)
    vals = [gi - run + end, run, jnp.broadcast_to(end, (1, width)), leave, gi, gi - run]
    res = jnp.zeros((8, width), F32)
    for i, v in enumerate(vals):
        res = jnp.where(r == i, v, res)
    out[...] = res


def between(gv, me, low, high):
    total = jnp.zeros((1, gv.shape[2]), F32)
    for t in range(1, gv.shape[0]):
        run = jnp.bitwise_xor(me, t)
        total = total + jnp.where((run > low) & (run < high), gv[t, 2:3, :], 0.0)
    return total


def local_kernel(sc, qh, ql, kh, kl, vh, vl, gv, hid):
    rows, cols = hid.shape
    nt = cols // CT
    s = jnp.zeros((rows, rows), F32)
    for ct in range(nt):
        s = s + mm3((qh[:, tile(ct)], ql[:, tile(ct)]), (kh[:, tile(ct)], kl[:, tile(ct)]), NT)
    base = sc[0] * rows
    allowed = (iota((rows, rows), 0) >= iota((rows, rows), 1)) & (
        seg_at(base, (rows, 1), 0, sc) == seg_at(base, (1, rows), 1, sc)
    )
    w = weight_of(allowed, to_col(gv[1:2, :], rows) + gv[5:6, :])
    p = split(s * (1.0 / math.sqrt(cols)) * w)
    for ct in range(nt):
        hid[:, tile(ct)] = mm3(p, (vh[:, tile(ct)], vl[:, tile(ct)]), NN)


def block_kernel(count, slot, *refs):
    sc, pays, refs = refs[0], refs[1 : 1 + count], refs[1 + count :]
    ph, pl_, gv, cw, cb = refs[:5]
    u_in = refs[5] if slot else None
    u, ah, al, mh, ml, ext = refs[-6:]
    rows, cols = u.shape
    nt = cols // CT
    i = pl.program_id(0)
    me, src = sc[0], sc[6 + slot + i]
    long = HALO + rows

    @pl.when(i == 0)
    def _():
        u[...] = u_in[...] if slot else jnp.zeros_like(u)

    for b, pay in enumerate(pays):

        @pl.when((i == b) & (src != me))
        def _(pay=pay):
            scale = scales_of(pay[0:16, 0 : up(long, 128)], long)
            for ct in range(nt):
                ext[:, tile(ct)] = pay[:, tile(ct)].astype(I32).astype(F32) * scale

    @pl.when(src != me)
    def _():
        masks = conv_masks(src * rows, rows, cw.shape[0], sc)
        for ct in range(nt):
            c = conv_tile(ext, ct, cw, cb, masks)
            ah[0, :, tile(ct)], al[0, :, tile(ct)] = split(c * sigmoid(c))

    @pl.when(src < me)
    def _():
        s = jnp.zeros((rows, rows), F32)
        for ct in range(nt):
            t = tile(ct)
            mh[0, :, t], ml[0, :, t] = split(ext[HALO:long, t])
            s = s + mm3((ph[:, t], pl_[:, t]), (ah[0, :, t], al[0, :, t]), NT)
        w = pair_weight(sc, gv, me, src, rows)
        p = split(s * (1.0 / math.sqrt(cols)) * w)
        for ct in range(nt):
            t = tile(ct)
            u[:, t] += mm3(p, (mh[0, :, t], ml[0, :, t]), NN)


def pair_weight(sc, gv, me, src, rows):
    allowed = seg_at(me * rows, (rows, 1), 0, sc) == seg_at(src * rows, (1, rows), 1, sc)
    row = between(gv, me, src, me) + gv[jnp.bitwise_xor(me, src), 0:1, :]
    return weight_of(allowed, to_col(gv[0, 1:2, :], rows) + row)


def finish_kernel(hid_in, u, bh, bl, act, z, dg, gn, sk, st, gh, gl, zh, zl, dh, dl, dact, rowtot, sums, payd, pays, buf, norm, hid):
    rows, cols = hid.shape
    nt = cols // CT
    total = jnp.zeros((rows, 1), F32)
    for ct in range(nt):
        t = tile(ct)
        h = hid_in[:, t] + mm3(split(u[:, t]), (bh[2, ct], bl[2, ct]), NN)
        hid[:, t] = h
        total = total + jnp.sum(h, axis=1, keepdims=True)
    mean = total * (1.0 / cols)
    total = jnp.zeros((rows, 1), F32)
    for ct in range(nt):
        d = hid[:, tile(ct)] - mean
        total = total + jnp.sum(d * d, axis=1, keepdims=True)
    rstd = lax.rsqrt(total * (1.0 / cols) + EPS)
    m1 = jnp.zeros((rows, 1), F32)
    m2 = jnp.zeros((rows, 1), F32)
    xm, xr = st[HALO : HALO + rows, 0:1], st[HALO : HALO + rows, 1:2]
    r8 = iota((8, CT), 0)
    for ct in range(nt):
        t = tile(ct)
        n = (hid[:, t] - mean) * rstd
        a = act[:, t]
        full = n * gn[:, t] + sk[:, t] * a
        zz = z[HALO : HALO + rows, t]
        sg = sigmoid(zz)
        gate = zz * sg
        gated = full * gate
        buf[0, :, t] = gated
        gh[:, t], gl[:, t] = split(gated)
        dgt = dg[:, t]
        da = dgt * gate
        dz = dgt * full * (sg * (1.0 + zz * (1.0 - sg)))
        zh[:, t], zl[:, t] = split(dz)
        dzr = dz * xr
        buf[1, :, t] = dzr
        dact[:, t] = da * sk[:, t]
        dn = da * gn[:, t]
        buf[2, :, t] = dn
        norm[:, t] = n
        m1 = m1 + jnp.sum(dn, axis=1, keepdims=True)
        m2 = m2 + jnp.sum(dn * n, axis=1, keepdims=True)
        s0 = jnp.sum(da * n, axis=0, keepdims=True)
        s1 = jnp.sum(da * a, axis=0, keepdims=True)
        s2 = jnp.sum(dzr * xm, axis=0, keepdims=True)
        sums[:, t] = jnp.where(r8 == 0, s0, jnp.where(r8 == 1, s1, jnp.where(r8 == 2, s2, 0.0)))
    m1, m2 = m1 * (1.0 / cols), m2 * (1.0 / cols)
    total = jnp.zeros((rows, 1), F32)
    for ct in range(nt):
        t = tile(ct)
        d = rstd * (buf[2, :, t] - m1 - norm[:, t] * m2)
        buf[2, :, t] = d
        dh[:, t], dl[:, t] = split(d)
        total = total + jnp.sum(d * hid[:, t], axis=1, keepdims=True)
    rowtot[...] = jnp.broadcast_to(total, rowtot.shape)
    quantize(lambda ct: buf[2, :, tile(ct)], payd, rows, nt, False)
    quantize(lambda ct: buf[0, :, tile(ct)], pays.at[0], rows, nt, False)
    quantize(lambda ct: buf[1, :, tile(ct)], pays.at[1], rows, nt, False)


def branch_kernel(gh, gl, w, out):
    acc = None
    for i in range(w.shape[0] // CT):
        part = mm3((gh[:, tile(i)], gl[:, tile(i)]), split(w[i * CT : (i + 1) * CT, :]), NN)
        acc = part if acc is None else acc + part
    out[...] = acc


def branch_of(gh, gl, w):
    rows, cols = gh.shape
    width = w.shape[1]
    wide = 512
    return call(
        branch_kernel,
        [gh, gl, w],
        [S((rows, width))],
        grid=(width // wide,),
        in_specs=[
            pl.BlockSpec((rows, cols), lambda i: (0, 0)),
            pl.BlockSpec((rows, cols), lambda i: (0, 0)),
            pl.BlockSpec((cols, wide), lambda i: (0, i)),
        ],
        out_specs=[pl.BlockSpec((rows, wide), lambda i: (0, i))],
        macs=3 * rows * width * cols,
    )[0]


def local_back_kernel(sc, qh, ql, kh, kl, vh, vl, dh, dl, gv, bh, bl, dq, dk, dv, col, rh, rl, eh, el):
    rows, cols = dq.shape
    nt = cols // CT
    st = jnp.zeros((rows, rows), F32)
    dpt = jnp.zeros((rows, rows), F32)
    for ct in range(nt):
        t = tile(ct)
        st = st + mm3((kh[:, t], kl[:, t]), (qh[:, t], ql[:, t]), NT)
        dpt = dpt + mm3((vh[:, t], vl[:, t]), (dh[:, t], dl[:, t]), NT)
        rh[:, t], rl[:, t] = split(mm3((kh[:, t], kl[:, t]), (bh[0, ct], bl[0, ct]), NT))
        eh[:, t], el[:, t] = split(mm3((dh[:, t], dl[:, t]), (bh[2, ct], bl[2, ct]), NT))
    base = sc[0] * rows
    allowed = (iota((rows, rows), 1) >= iota((rows, rows), 0)) & (
        seg_at(base, (rows, 1), 0, sc) == seg_at(base, (1, rows), 1, sc)
    )
    w = weight_of(allowed, gv[1:2, :] + to_col(gv[5:6, :], rows))
    scaled = w * (1.0 / math.sqrt(cols))
    pt = st * scaled
    dst = dpt * scaled
    col[...] = jnp.broadcast_to(jnp.sum(dpt * pt, axis=1, keepdims=True), col.shape)
    pt2, dst2, ds2 = split(pt), split(dst), split(dst.T)
    for ct in range(nt):
        t = tile(ct)
        dv[:, t] = mm3(pt2, (dh[:, t], dl[:, t]), NN)
        dk[:, t] = mm3(dst2, (qh[:, t], ql[:, t]), NN)
        dq[:, t] = mm3(ds2, (kh[:, t], kl[:, t]), NN)


def earlier_kernel(sc, ah, al, mh, ml, eh, el, ph, pl_, gv, bh, bl, dq_in, pay_in, dq, pay, acc, vec):
    rows, cols = dq.shape
    nt = cols // CT
    i, last = pl.program_id(0), pl.num_programs(0) - 1
    me, src = sc[0], sc[6 + i]

    @pl.when(i == 0)
    def _():
        acc[...] = jnp.zeros_like(acc)
        vec[...] = jnp.zeros_like(vec)

    @pl.when(src < me)
    def _():
        dp = jnp.zeros((rows, rows), F32)
        for ct in range(nt):
            t = tile(ct)
            dp = dp + mm3((eh[:, t], el[:, t]), (mh[0, :, t], ml[0, :, t]), NT)
        ds = split(dp * pair_weight(sc, gv, me, src, rows) * (1.0 / math.sqrt(cols)))
        total = jnp.zeros((rows, 1), F32)
        for ct in range(nt):
            t = tile(ct)
            part = mm3(ds, (ah[0, :, t], al[0, :, t]), NN)
            acc[:, t] += part
            p = ph[:, t].astype(F32) + pl_[:, t].astype(F32)
            total = total + jnp.sum(part * p, axis=1, keepdims=True)
        flow = jnp.sum(total, axis=0, keepdims=True)
        lane = iota(vec.shape, 1)
        vec[...] += jnp.where((lane > src) & (lane < me), flow, 0.0)

    @pl.when(i == last)
    def _():
        for ct in range(nt):
            t = tile(ct)
            dq[:, t] = dq_in[:, t] + mm3(split(acc[:, t]), (bh[1, ct], bl[1, ct]), NN)
        v = vec[0:1, :]
        top = jnp.maximum(jnp.max(jnp.abs(v), axis=1, keepdims=True), 1e-30)
        code = jnp.ceil(jnp.log(top * (1.0 / 32000.0)) * (1.0 / UNIT))
        v = v * jnp.exp(code * (-UNIT))
        whole = jnp.floor(v)
        digits = [whole, jnp.floor((v - whole) * 32767.0 + 0.5), jnp.broadcast_to(code, v.shape)]
        r = iota((16, 128), 0)
        out = pay_in[:, 0:128].astype(I32)
        for k, d in enumerate(digits):
            out = jnp.where(r == k + 1, d.astype(I32), out)
        pay[...] = pay_in[...]
        pay[:, 0:128] = out.astype(I16)


def earlier(n, sc, bufs, e2, p2, gv, bh, bl, dq_in, pay):
    rows, cols = dq_in.shape
    moving = pl.BlockSpec((1, rows, cols), lambda i: (i, 0, 0))
    codes = pl.BlockSpec((16, cols), lambda i: (rows // 16, 0))
    return call(
        earlier_kernel,
        [sc, *bufs, *e2, *p2, gv, bh, bl, dq_in, pay],
        [S((rows, cols)), pay],
        grid=(n - 1,),
        in_specs=[SMEM] + [moving] * 4 + [None] * 8 + [codes],
        out_specs=[None, codes],
        scratch=[pltpu.VMEM((rows, cols), F32), pltpu.VMEM((8, 128), F32)],
        aliases={13: 1},
        weight=0,
        macs=(n - 1) * 6 * rows * rows * cols // 2,
    )


def pick(slots, i):
    out = slots[0]
    for b, slot in enumerate(slots[1:]):
        out = jnp.where(i == b + 1, slot, out)
    return out


def later_kernel(slots, *refs):
    count = len(slots)
    sc, pays, refs = refs[0], refs[1 : 1 + count], refs[1 + count :]
    ah, al, rh, rl, vh, vl, gv = refs[:7]
    e_in, dv_in, col_in, flow_in = refs[7:11] if len(refs) == 17 else (None, refs[7], None, None)
    e, dv, col, flow, ph, pl_ = refs[-6:]
    rows, cols = e.shape
    nt = cols // CT
    i = pl.program_id(0)
    me, src = sc[0], sc[6 + pick(slots, i)]

    @pl.when(i == 0)
    def _():
        e[...] = jnp.zeros_like(e) if e_in is None else e_in[...]
        dv[...] = dv_in[...]
        col[...] = jnp.zeros_like(col) if col_in is None else col_in[...]
        flow[...] = jnp.zeros_like(flow) if flow_in is None else flow_in[...]

    for b, pay in enumerate(pays):

        @pl.when((src > me) & (i == b))
        def _(pay=pay):
            scale = scales_of(pay[rows : rows + 16, 0:rows], rows)
            for ct in range(nt):
                t = tile(ct)
                ph[:, t], pl_[:, t] = split(pay[0:rows, t].astype(I32).astype(F32) * scale)
            d = pay[rows : rows + 16, 0:128].astype(I32).astype(F32)
            v = (d[1:2, :] + d[2:3, :] * (1.0 / 32767.0)) * jnp.exp(d[3:4, :] * UNIT)
            v = jnp.where(iota((1, 128), 1) == me, v, 0.0)
            flow[...] += jnp.sum(v, axis=1, keepdims=True)

    @pl.when(src > me)
    def _():
        st = jnp.zeros((rows, rows), F32)
        dpt = jnp.zeros((rows, rows), F32)
        for ct in range(nt):
            t = tile(ct)
            st = st + mm3((rh[:, t], rl[:, t]), (ah[0, :, t], al[0, :, t]), NT)
            dpt = dpt + mm3((vh[:, t], vl[:, t]), (ph[:, t], pl_[:, t]), NT)
        allowed = seg_at(me * rows, (rows, 1), 0, sc) == seg_at(src * rows, (1, rows), 1, sc)
        row = between(gv, me, me, src) + gv[jnp.bitwise_xor(me, src), 1:2, :]
        w = weight_of(allowed, to_col(gv[0, 0:1, :], rows) + row)
        scaled = w * (1.0 / math.sqrt(cols))
        pt = st * scaled
        col[...] += jnp.sum(dpt * pt, axis=1, keepdims=True)
        pt2, dst2 = split(pt), split(dpt * scaled)
        for ct in range(nt):
            t = tile(ct)
            dv[:, t] += mm3(pt2, (ph[:, t], pl_[:, t]), NN)
            e[:, t] += mm3(dst2, (ah[0, :, t], al[0, :, t]), NN)


def gate_back_kernel(sc, col_here, col_later, rowtot, gv, flow, out):
    rows = rowtot.shape[0]
    here, later = col_here[:, 0:1], col_later[:, 0:1]
    t, p = iota((rows, rows), 1), iota((rows, rows), 0)
    val = to_row(rowtot[:, 0:1] - here, rows)
    dlk = jnp.sum(jnp.where(t >= p, val, 0.0), axis=1, keepdims=True)
    dlk = dlk + jnp.sum(jnp.where(t < p, to_row(later, rows), 0.0), axis=1, keepdims=True)
    dlk = dlk + flow[0:1, 0:1]
    r = iota((8, rows), 0)
    d_in = to_row(here + later, rows)
    d_f = to_row(dlk, rows) * gv[3:4, :]
    out[...] = jnp.where(r == sc[1], d_in, jnp.where(r == sc[1] + out.shape[0] // 2, d_f, 0.0))


def back_kernel(sc, ext, dact, dq, dk, e, dv, bh, bl, cw, cb, gw, dg, dm, rim, d0h, d0l, d1h, d1l, d2h, d2l, dco, dcs):
    rows = dq.shape[0]
    kw = cw.shape[0]
    base = sc[0] * rows
    masks = conv_masks(base, rows, kw, sc)
    long = HALO + rows
    here = seg_at(base - HALO, (long, 1), 0, sc)
    back_masks = []
    for tap in range(kw):
        there = seg_at(base - HALO + kw - 1 - tap, (long, 1), 0, sc)
        back_masks.append(jnp.where(there == here, 1.0, 0.0))
    g2 = split(jnp.concatenate([dg[...], jnp.zeros((8, rows), F32)], axis=0))
    dcs[0:HALO, :] = jnp.zeros((HALO, CT), F32)
    dcs[long : HALO + long, :] = jnp.zeros((HALO, CT), F32)
    dk_all = dk[...] + mm3(split(e[...]), (bh[0, 0], bl[0, 0]), NN)
    grads = (dq[...], dk_all, dv[...])
    kept = ((d0h, d0l), (d1h, d1l), (d2h, d2l))
    back = []
    for m in range(3):
        d2 = split(grads[m] + mm3(g2, split(gw[m]), TN))
        kept[m][0][...], kept[m][1][...] = d2
        back.append(mm3(d2, (bh[m, 0], bl[m, 0]), NT))
    c = conv_tile(ext, 0, cw, cb, masks)
    sg = sigmoid(c)
    dc = (dact[...] + back[0] + back[1]) * (sg * (1.0 + c * (1.0 - sg)))
    dco[...] = dc
    dcs[HALO:long, :] = dc
    dext = jnp.zeros((long, CT), F32)
    for tap in range(kw):
        at = kw - 1 - tap
        dext = dext + cw[tap : tap + 1, :] * (dcs[at : at + long, :] * back_masks[tap])
    rim[...] = dext[0:HALO, :]
    dm[...] = dext[HALO:, :] + back[2]


def small_kernel(sc, ext, act, dc, d0h, d0l, d1h, d1l, d2h, d2l, qh, ql, kh, kl, vh, vl, dg, cw, pack):
    rows = act.shape[0]
    kw = cw.shape[0]
    masks = conv_masks(sc[0] * rows, rows, kw, sc)
    long = HALO + rows
    g = jnp.concatenate([dg[...], jnp.zeros((8, rows), F32)], axis=0)
    g2 = split(g)
    pack[...] = jnp.zeros_like(pack)
    pack[41:42, 0:128] = to_row(jnp.sum(g, axis=1, keepdims=True), 128)
    group = 4
    sub, lane = iota((CT, CT), 0), iota((CT, CT), 1)
    diagonal = (sub - lax.rem(sub, group)) == (lane - lax.rem(lane, group))
    a2 = split(act[...])
    m2 = split(ext[HALO:long, :])
    grads = ((d0h, d0l), (d1h, d1l), (d2h, d2l))
    stored = ((qh, ql), (kh, kl), (vh, vl))
    for m in range(3):
        gate_rows = mm3(g2, (stored[m][0][...], stored[m][1][...]), NN)
        pack[17 + 8 * m : 25 + 8 * m, :] = gate_rows[0:8, :]
        d2 = (grads[m][0][...], grads[m][1][...])
        outer = jnp.where(diagonal, mm3(a2 if m < 2 else m2, d2, TN), 0.0)
        eight = outer[0:8, :]
        for r in range(1, CT // 8):
            eight = eight + outer[8 * r : 8 * r + 8, :]
        pack[5 + group * m : 5 + group * (m + 1), :] = eight[0:4, :] + eight[4:8, :]
    d = dc[...]
    pack[4:5, :] = jnp.sum(d, axis=0, keepdims=True)
    for tap in range(kw):
        at = HALO - (kw - 1) + tap
        pack[tap : tap + 1, :] = jnp.sum(d * (ext[at : at + rows, :] * masks[tap]), axis=0, keepdims=True)


def by_columns(kernel, ins, outs, scratch=(), macs=0, fixed=(), weight=10):
    def spec(a, index=None):
        if index == 0:
            return SMEM
        if index in fixed:
            return None
        if len(a.shape) == 2:
            return pl.BlockSpec((a.shape[0], CT), lambda i: (0, i))
        if len(a.shape) == 3:
            return pl.BlockSpec((a.shape[0], a.shape[1], CT), lambda i: (0, 0, i))
        return pl.BlockSpec((a.shape[0], 1, CT, CT), lambda i: (0, i, 0, 0))

    return call(
        kernel,
        ins,
        outs,
        grid=(outs[0].shape[1] // CT,),
        in_specs=[spec(a, k) for k, a in enumerate(ins)],
        out_specs=[spec(o) for o in outs],
        scratch=scratch,
        macs=macs,
        weight=weight,
    )


def send_kernel(dm, rim, st, mh, ml, pay, ux, buf):
    rows, cols = dm.shape
    nt = cols // CT
    xm, xr = st[HALO : HALO + rows, 0:1], st[HALO : HALO + rows, 1:2]
    for ct in range(nt):
        t = tile(ct)
        buf[:, t] = dm[:, t]
        buf[rows - HALO : rows, t] = dm[rows - HALO : rows, t] + rim[:, t]
        d = buf[:, t]
        mh[:, t], ml[:, t] = split(d)
        d = d * xr
        buf[:, t] = d
        ux[:, t] = jnp.broadcast_to(jnp.sum(d * xm, axis=0, keepdims=True), (8, CT))
    quantize(lambda ct: buf[:, tile(ct)], pay, rows, nt, False)


def part_kernel(ah, al, w, g, out):
    out[...] = mm3((ah[...], al[...]), split(w[...] * to_col(g[0], CT)), NT)


def dnorm_kernel(sc, ah, al, w, g, other, x, st, keep, give, ln, buf):
    a = other[...] + mm3((ah[...], al[...]), split(w[...] * to_col(g[0], CT)), NT)
    rows = a.shape[0]
    buf[...] = a
    q = rows // 4
    mine = lax.rem(sc[1], 2)
    for half in range(2):
        at = pl.multiple_of(half * 2 * q + mine * q, q)
        keep[half * q : half * q + q, :] = buf[pl.ds(at, q), :]
        at = pl.multiple_of(half * 2 * q + (1 - mine) * q, q)
        give[half * q : half * q + q, :] = buf[pl.ds(at, q), :]
    xhat = (x[...].astype(F32) - st[HALO : HALO + rows, 0:1]) * st[HALO : HALO + rows, 1:2]
    ln[0] = jnp.sum(a * xhat, axis=0, keepdims=True) / g[0]


def dnorm_z(ah, al, w, gain):
    rows, cols = ah.shape
    width = w.shape[0]
    return call(
        part_kernel,
        [ah, al, w, gain.reshape(width // CT, 1, CT)],
        [S((rows, width))],
        grid=(width // CT,),
        in_specs=[None] * 2
        + [pl.BlockSpec((CT, cols), lambda i: (i, 0)), pl.BlockSpec((1, 1, CT), lambda i: (i, 0, 0))],
        out_specs=[pl.BlockSpec((rows, CT), lambda i: (0, i))],
        macs=3 * rows * width * cols,
    )[0]


def dnorm(sc, ah, al, w, gain, other, x, st):
    rows, cols = ah.shape
    width = w.shape[0]
    gspec = pl.BlockSpec((1, 1, CT), lambda i: (i, 0, 0))
    wide = pl.BlockSpec((rows, CT), lambda i: (0, i))
    half = pl.BlockSpec((rows // 2, CT), lambda i: (0, i))
    return call(
        dnorm_kernel,
        [sc, ah, al, w, gain.reshape(width // CT, 1, CT), other, x, st],
        [S((rows // 2, width)), S((rows // 2, width)), S((width // CT, 1, CT))],
        grid=(width // CT,),
        in_specs=[SMEM, None, None, pl.BlockSpec((CT, cols), lambda i: (i, 0)), gspec, wide, wide, None],
        out_specs=[half, half, gspec],
        scratch=[pltpu.VMEM((rows, CT), F32)],
        macs=3 * rows * width * cols,
    )


def second_kernel(sc, a, b, keep, give):
    q = keep.shape[0]
    mine = sc[1] // 2
    at = pl.multiple_of(mine * q, q)
    keep[...] = a[pl.ds(at, q), :] + b[pl.ds(at, q), :]
    at = pl.multiple_of((1 - mine) * q, q)
    give[...] = a[pl.ds(at, q), :] + b[pl.ds(at, q), :]


def norm_back_kernel(sc, a, b, x, g, out):
    q, width = out.shape
    at = pl.multiple_of(sc[1] * q, q)
    xs = x[pl.ds(at, q), :].astype(F32)
    dn = a[...] + b[...]
    c = xs - jnp.mean(xs, axis=1, keepdims=True)
    rstd = lax.rsqrt(jnp.mean(c * c, axis=1, keepdims=True) + EPS)
    xhat = c * rstd
    m1 = jnp.mean(dn, axis=1, keepdims=True)
    m2 = jnp.mean(dn * xhat, axis=1, keepdims=True)
    out[...] = g[pl.ds(at, q), :].astype(F32) + rstd * (dn - m1 - xhat * m2)


def left_kernel(sc, x, g, *outs):
    m = len(outs)
    hf = outs[0].shape[1]
    ring, kind, half = sc[0] // 2, lax.rem(sc[1], 2), sc[1] // 2
    for s, out in enumerate(outs):
        at = lax.rem(ring - s + m, m) * (2 * hf) + half * hf
        cols = pl.ds(pl.multiple_of(at, hf), hf)

        @pl.when(kind == 0)
        def _(out=out, cols=cols):
            out[...] = x[:, cols]

        @pl.when(kind == 1)
        def _(out=out, cols=cols):
            out[...] = g[:, cols]


def join_kernel(sc, own, a, b, c, out):
    q = own.shape[0]
    for bits, part in enumerate((own, a, b, c)):
        at = pl.multiple_of(jnp.bitwise_xor(sc[1], bits) * q, q)
        out[pl.ds(at, q), :] = part[...]


def wgrad_kernel(m, kinds, sc, left, *refs):
    count = len(refs) // 2 - 1
    pays, codes = refs[:count], refs[count : 2 * count]
    keep, pay, buf = refs[2 * count :]
    rows = left.shape[2]
    hf = left.shape[3]
    kind = pick(kinds, pl.program_id(0))
    ct, last = pl.program_id(1), pl.num_programs(1) - 1
    odd = lax.rem(sc[0], 2)
    ring = sc[0] // 2
    mine, other = odd * 2 + kind, (1 - odd) * 2 + kind

    def slots(refs):
        every = [r[0].astype(I32) for r in refs]
        if m != 4:
            return every
        own, down1, up1, down2, up2, three = every
        far = jnp.where(ring == m - 1, three, 0)
        near = jnp.where(ring == 0, three, 0)
        return [own, down1 + far, down2 + up2, up1 + near]

    a = jnp.zeros((hf, CT), F32)
    b = jnp.zeros((hf, CT), F32)
    for s, (q, c) in enumerate(zip(slots(pays), slots(codes))):
        hi, lo = split(q.astype(F32) * jnp.exp(to_col(c.astype(F32)[0:1, :], rows) * UNIT))
        a = a + (mm(left[mine, s], hi, TN) + mm(left[mine, s], lo, TN))
        b = b + (mm(left[other, s], hi, TN) + mm(left[other, s], lo, TN))
    keep[0] = a
    buf[:, pl.ds(pl.multiple_of(ct * CT, CT), CT)] = b

    @pl.when(ct == last)
    def _():
        quantize(lambda c: buf[:, tile(c)], pay.at[0], hf, buf.shape[1] // CT, False)


def wgrad(sc, left, kinds, pays):
    _, m, rows, hf = left.shape
    cols = pays[0].shape[2]
    count = len(kinds)
    return call(
        functools.partial(wgrad_kernel, m, kinds),
        [sc, left, *pays, *pays],
        [S((count, hf, cols)), S((count, hf + 16, cols), I16)],
        grid=(count, cols // CT),
        in_specs=[SMEM, None]
        + [pl.BlockSpec((1, rows, CT), lambda p, i: (p, 0, i))] * len(pays)
        + [pl.BlockSpec((1, 16, rows), lambda p, i: (p, rows // 16, 0))] * len(pays),
        out_specs=[
            pl.BlockSpec((1, hf, CT), lambda p, i: (p, 0, i)),
            pl.BlockSpec((1, hf + 16, cols), lambda p, i: (p, 0, 0)),
        ],
        scratch=[pltpu.VMEM((hf, cols), F32)],
        macs=4 * count * m * hf * rows * cols,
    )


def received(pay, ct, rows):
    return pay[0:rows, tile(ct)].astype(I32).astype(F32)


def down_kernel(keep, pay, out):
    rows, cols = keep.shape[1:]
    scale = scales_of(pay[0, rows : rows + 16, 0 : up(rows, 128)], rows)
    for ct in range(cols // CT):
        t = keep[0, :, tile(ct)] + received(pay.at[0], ct, rows) * scale
        out[tile(ct), :] = t.T


def up_kernel(which, keep, pay, gain, u, out):
    rows, cols = out.shape
    scale = scales_of(pay[which, rows : rows + 16, 0 : up(rows, 128)], rows)
    g = to_col(gain[...], rows)
    for ct in range(cols // CT):
        t = keep[which, :, tile(ct)] + received(pay.at[which], ct, rows) * scale
        out[:, tile(ct)] = g * (t - u[:, tile(ct)])


def shifted(a, by):
    n = lax.axis_size("seq")
    return lax.ppermute(a, "seq", [(i, (i + by) % n) for i in range(n)])


def swapped(a, axis, bit):
    n = lax.axis_size(axis)
    return lax.ppermute(a, axis, [(i, i ^ bit) for i in range(n)])


def sum_over(a, axis):
    bit = 1
    while bit < lax.axis_size(axis):
        a = a + swapped(a, axis, bit)
        bit *= 2
    return a


def moved(a, pairs):
    return lax.ppermute(a, "seq", pairs)


def gather_runs(pay):
    n = lax.axis_size("seq")
    if n != 8:
        return [shifted(pay, s) for s in range(1, n)], lambda last: []
    x, above, below = swapped(pay, "seq", 1), shifted(pay, -2), shifted(pay, 2)

    def rest(last):
        across = shifted(pay, 4)
        return [across] + [swapped(a, "seq", 1) for a in (above, below, across)]

    return [x, above, below], rest


def gather_later(pay, steps):
    n = lax.axis_size("seq")
    if n != 8:
        for step in steps:
            step(pay)
        return [(list(range(n - 1)), [shifted(pay, s) for s in range(1, n)])]
    one = moved(pay, [(i, i - 2) for i in range(2, 8)])
    x = moved(pay, [(i, i - 1) for i in range(1, 8, 2)])
    done = steps[0](pay)
    two = moved(after(one, done), [(i, i - 2) for i in range(2, 6)])
    x_one = moved(after(one, done), [(i, i ^ 1) for i in range(6)])
    done = steps[1](done)
    three = moved(after(two, done), [(i, i - 2) for i in range(2, 4)])
    x_two = moved(after(two, done), [(i, i ^ 1) for i in range(4)])
    x_three = moved(three, [(0, 1), (1, 0)])
    return [([0, 1], [x, one]), ([4, 3], [x_one, two]), ([6, 2, 5], [x_two, three, x_three])]


def gather_xor(a):
    a = a[None]
    bit = 1
    while bit < lax.axis_size("seq"):
        a = jnp.concatenate([a, swapped(a, "seq", bit)])
        bit *= 2
    return a


def sources(me, n):
    if n != 8:
        return [lax.rem(me - s + n, n) for s in range(1, n)]
    z, x = me // 2, lax.rem(me, 2)

    def at(dz, dx):
        return lax.rem(z + dz, 4) * 2 + (1 - x if dx else x)

    return [at(0, 1), at(1, 0), at(3, 0), at(2, 0), at(1, 1), at(3, 1), at(2, 1)]


def ring_first(pay):
    m = lax.axis_size("seq") // 2
    if m != 4:
        return [shifted(pay, -2 * s) for s in range(1, m)]
    return [moved(pay, [(i + 2, i) for i in range(6)]), moved(pay, [(i, i + 2) for i in range(6)])]


def ring_second(got):
    if len(got) != 2:
        return got
    down1, up1 = got
    down2 = moved(down1, [(i, i - 2) for i in range(2, 6)])
    return [down1, up1, down2, moved(up1, [(i, i + 2) for i in range(2, 6)])]


def ring_third(got):
    if len(got) != 4:
        return got
    return got + [moved(got[2] + got[3], [(2, 0), (3, 1), (4, 6), (5, 7)])]


def after(array, *others):
    if isinstance(array, list):
        return list(lax.optimization_barrier((*array, *others))[: len(array)])
    return lax.optimization_barrier((array, *others))[0]


def per_device(
    stream,
    ln_gain,
    up_x,
    up_z,
    conv_w,
    conv_b,
    qkv_w,
    gate_w,
    gate_bias,
    gn_gain,
    skip,
    down_w,
    cotangent,
    lengths,
):
    rows, width = stream.shape
    cols = up_x.shape[1]
    kw = conv_w.shape[0]
    heads = gate_w.shape[0] // 2
    n = lax.axis_size("seq")
    m = n // 2
    me, hd = lax.axis_index("seq"), lax.axis_index("head")
    starts = jnp.cumsum(lengths) - lengths
    order = sources(me, n)
    sc = jnp.concatenate([jnp.stack([me, hd]), starts, jnp.stack(order)]).astype(I32)
    cb, gn, sk = conv_b.reshape(1, cols), gn_gain.reshape(1, cols), skip.reshape(1, cols)
    gw = jnp.pad(gate_w.transpose(1, 0, 2), ((0, 0), (0, 16 - 2 * heads), (0, 0)))
    tall = S((rows, cols))
    tall16 = S((rows, cols), BF16)

    hf = width // m // 2
    if hf % 128 == 0:
        slices = call(
            left_kernel,
            [sc, stream, cotangent],
            [S((rows, hf), BF16)] * m,
            in_specs=[SMEM, None, None],
            weight=0,
        )
    else:
        chosen = jnp.where(lax.rem(hd, 2) == 1, cotangent, stream)
        at = [lax.rem(me // 2 - k + m, m) * (2 * hf) + hd // 2 * hf for k in range(m)]
        slices = [lax.dynamic_slice_in_dim(chosen, a, hf, 1) for a in at]
    left = jnp.stack([shifted(a, -2 * k) if k else a for k, a in enumerate(slices)])

    halo = lax.ppermute(stream[rows - HALO :], "seq", [(i, i + 1) for i in range(n - 1)])
    nt = cols // CT
    bh, bl = call(prep_kernel, [qkv_w], [S((3, nt, CT, CT), BF16)] * 2)
    x_ext = after(jnp.concatenate([jnp.ones((1, width), BF16), halo[1:], stream]), bh)
    mixed, stat, pay = proj(x_ext, up_x, ln_gain, True)
    first_runs, rest_runs = gather_runs(pay)

    act, qh, ql, kh, kl, vh, vl, ph, pl_, gate_part = call(
        front_kernel,
        [after(sc, left), mixed, bh, bl, conv_w, cb, gw],
        [tall] + [tall16] * 8 + [S((8, rows))],
        in_specs=[SMEM] + [None] * 6,
        weight=1,
        macs=12 * rows * cols * CT,
    )
    (gv,) = call(
        gate_kernel,
        [sc, sum_over(gate_part, "head"), gate_bias],
        [S((8, rows))],
        in_specs=[SMEM, None, SMEM],
        weight=0,
    )
    gvs = gather_xor(gv)

    outgate = proj(after(x_ext, gate_part), up_z, ln_gain, False)[0]
    dgate = dgated(after(cotangent, gate_part), down_w)
    (hid,) = call(
        local_kernel,
        [sc, qh, ql, kh, kl, vh, vl, gv],
        [tall],
        in_specs=[SMEM] + [None] * 7,
        macs=6 * rows * rows * cols,
        weight=1,
    )
    rest = rest_runs(gvs)
    runs = [first_runs, rest[:3], rest[3:]]
    u, bufs = None, []
    slot = 0
    for pays in filter(None, runs):
        count = len(pays)
        ins = [sc, *pays, ph, pl_, gvs, conv_w, cb]
        specs = [SMEM] + [None] * (count + 5)
        aliases = {}
        if slot:
            ins += [u, *bufs]
            specs += [None] + [pl.BlockSpec(memory_space=pl.ANY)] * 4
            aliases = {6 + count + i: i for i in range(5)}
        place = pl.BlockSpec((1, rows, cols), lambda i, slot=slot: (slot + i, 0, 0))
        u, *bufs = call(
            functools.partial(block_kernel, count, slot),
            ins,
            [tall] + [S((n - 1, rows, cols), BF16)] * 4,
            grid=(count,),
            in_specs=specs,
            out_specs=[None] + [place] * 4,
            scratch=[pltpu.VMEM((HALO + rows, cols), F32)],
            aliases=aliases,
            macs=count * 6 * rows * rows * cols,
            weight=1,
        )
        slot += count

    left = lax.all_gather(left, "head")
    gh, gl, zh, zl, dh, dl, dact, rowtot, sums, payd, pays = call(
        finish_kernel,
        [hid, u, bh, bl, act, outgate, dgate, gn, sk, stat],
        [tall16] * 6
        + [tall, S((rows, 128)), S((8, cols)), S((rows + 16, cols), I16), S((2, rows + 16, cols), I16)],
        scratch=[pltpu.VMEM((3, rows, cols), F32)] + [pltpu.VMEM((rows, cols), F32)] * 2,
        macs=3 * rows * cols * CT,
    )

    dq, dk, dv, col_here, rh, rl, eh, el = call(
        local_back_kernel,
        [after(sc, left), qh, ql, kh, kl, vh, vl, dh, dl, gv, bh, bl],
        [tall] * 3 + [S((rows, 128))] + [tall16] * 4,
        in_specs=[SMEM] + [None] * 11,
        weight=0,
        macs=15 * rows * rows * cols,
    )
    dq, payd = earlier(n, sc, bufs, (eh, el), (ph, pl_), gvs, bh, bl, dq, payd)
    early = ring_first(pays)
    beside = []

    def step_norm(last):
        beside.append(dnorm_z(after(zh, last, *early), zl, up_z, ln_gain))
        return beside[0]

    def step_branch(last):
        beside.append(branch_of(after(gh, last), gl, down_w))
        return beside[1]

    back_runs = gather_later(payd, (step_norm, step_branch))
    early = ring_second(after(early, back_runs[-1 if n != 8 else -2][1][-1], beside[1]))
    dn_z, branch = beside
    share = rows // 4
    first = hd * share
    x_share = lax.dynamic_slice_in_dim(stream, first, share, 0).astype(F32)
    branch = lax.psum_scatter(branch, "head", scatter_dimension=0, tiled=True)
    result = x_share + branch
    output = lax.all_gather(result.astype(BF16), "head", axis=0, tiled=True)
    squares = jnp.stack([jnp.sum(result * result), jnp.sum(branch * branch)])

    state = None
    for step, (slots, payloads) in enumerate(back_runs):
        count = len(slots)
        place = pl.BlockSpec((1, rows, cols), lambda i, slots=slots: (pick(slots, i), 0, 0))
        ins = [sc, *payloads, bufs[0], bufs[1], rh, rl, vh, vl, gvs]
        ins += [dv] if state is None else state
        at = 8 + count
        state = call(
            functools.partial(later_kernel, slots),
            ins,
            [tall, tall, S((rows, 128)), S((8, 128))],
            grid=(count,),
            in_specs=[SMEM] + [None] * count + [place, place] + [None] * (len(ins) - count - 3),
            scratch=[pltpu.VMEM((rows, cols), BF16)] * 2,
            aliases={at: 1} if state is None else {at + k: k for k in range(4)},
            macs=count * 6 * rows * rows * cols,
            weight=10 if step < len(back_runs) - 1 else 0,
        )
    e, dv, col_later, flow = state
    (dgates,) = call(
        gate_back_kernel,
        [after(sc, *early), col_here, col_later, rowtot, gv, flow],
        [S((8, rows))],
        in_specs=[SMEM] + [None] * 5,
        weight=0,
    )
    early = ring_third(after(early, e))
    dgates = sum_over(dgates, "head")
    dm, rim, *kept = by_columns(
        back_kernel,
        [after(sc, result), mixed, dact, dq, dk, e, dv, bh, bl, conv_w, cb, gw, dgates],
        [tall, S((HALO, cols))] + [tall16] * 6 + [tall],
        scratch=[pltpu.VMEM((2 * HALO + rows, CT), F32)],
        macs=30 * rows * cols * CT,
        fixed=(12,),
    )
    rim = lax.ppermute(rim, "seq", [(i + 1, i) for i in range(n - 1)])
    (pack,) = by_columns(
        small_kernel,
        [after(sc, *early), mixed, act, kept[6], *kept[:6], qh, ql, kh, kl, vh, vl, dgates, conv_w],
        [S((48, cols))],
        macs=30 * rows * cols * CT,
        fixed=(16,),
    )
    mh, ml, paym, ux = call(
        send_kernel,
        [dm, rim, after(stat, pack)],
        [tall16] * 2 + [S((rows + 16, cols), I16), S((8, cols))],
        scratch=[pltpu.VMEM((rows, cols), F32)],
        weight=0,
    )
    late = first_late = ring_first(paym[None])

    keep_early, give_early = wgrad(after(sc, paym), left, (1, 0), [pays] + early)
    got_early = swapped(give_early, "seq", 1)
    late = ring_second(after(late, keep_early))
    keep, give, ln_part = dnorm(after(sc, keep_early, *first_late), mh, ml, up_x, ln_gain, dn_z, stream, stat)
    extra = jnp.zeros((1, cols)).at[0, :2].set(squares)
    small = jnp.concatenate([pack, sums, ux[:1], ln_part.reshape(width // cols, cols), extra])
    first_sum = small + swapped(small, "seq", 1)
    keep, give = call(
        second_kernel,
        [sc, keep, swapped(after(give, *late), "head", 1)],
        [S((share, width))] * 2,
        in_specs=[SMEM, None, None],
    )
    late = ring_third(late)
    small, bit = after(first_sum, give), 2
    while bit < n // 2:
        small = small + swapped(small, "seq", bit)
        bit *= 2
    keep_x, give_x = wgrad(after(sc, small), left, (0,), [paym[None]] + late)
    got_x = swapped(give_x, "seq", 1)
    small = small + swapped(small, "seq", bit)
    (grad_share,) = call(
        norm_back_kernel,
        [after(sc, keep_x), keep, swapped(give, "head", 2), stream, cotangent],
        [S((share, width))],
        in_specs=[SMEM] + [None] * 4,
    )
    grad_other = swapped(grad_share, "head", 2)
    (grad_stream,) = call(
        join_kernel,
        [sc, grad_share, swapped(grad_share, "head", 1), grad_other, swapped(grad_other, "head", 1)],
        [S((rows, width))],
        in_specs=[SMEM] + [None] * 4,
    )
    (grad_down,) = call(down_kernel, [after(keep_early, keep_x), got_early], [S((cols, hf))])
    tail = sum_over(after(small[57:], keep_x), "head")
    lns = width // cols
    grad_ln = tail[:lns].reshape(width)
    rms_pair = jnp.sqrt(tail[lns, :2] / (rows * n * width))
    gain_here = lax.dynamic_slice_in_dim(ln_gain, me * hf, hf, 0)[None]
    (grad_up_z,) = call(
        functools.partial(up_kernel, 1), [keep_early, got_early, gain_here, small[50:51]], [S((hf, cols))]
    )
    (grad_up_x,) = call(
        functools.partial(up_kernel, 0), [keep_x, got_x, gain_here, small[56:57]], [S((hf, cols))]
    )
    return (
        output,
        rms_pair,
        grad_stream,
        grad_up_x,
        grad_up_z,
        grad_down,
        grad_ln,
        small[0:kw],
        small[4],
        small[5:17].reshape(3, 4, cols),
        small[17:41].reshape(3, 2 * heads, cols).transpose(1, 0, 2),
        small[41, heads : 2 * heads],
        small[48],
        small[49],
    )


def solution(mesh):
    return jax.shard_map(
        per_device,
        mesh=mesh,
        in_specs=(
            P("seq", None),
            P(),
            P(None, "head"),
            P(None, "head"),
            P(None, "head"),
            P("head"),
            P(None, None, "head"),
            P(None, None, "head"),
            P(),
            P("head"),
            P("head"),
            P("head", None),
            P("seq", None),
            P(),
        ),
        out_specs=(
            P("seq", None),
            P(),
            P("seq", None),
            P("seq", "head"),
            P("seq", "head"),
            P("head", "seq"),
            P(),
            P(None, "head"),
            P("head"),
            P(None, None, "head"),
            P(None, None, "head"),
            P(),
            P("head"),
            P("head"),
        ),
        check_vma=False,
    )
```

```python
import functools
import math

import jax
import jax.numpy as jnp
from jax import lax
from jax.experimental import pallas as pl
from jax.experimental.pallas import tpu as pltpu
from jax.sharding import PartitionSpec as P

EPS = 1e-05
F32, BF16, I16, I32 = jnp.float32, jnp.bfloat16, jnp.int16, jnp.int32
HALO = 16
CT = 256
UNIT = math.log(2.0) / 256.0
NN = (((1,), (0,)), ((), ()))
NT = (((1,), (1,)), ((), ()))
TN = (((0,), (0,)), ((), ()))
SEGS = 4


def iota(shape, dim):
    return lax.broadcasted_iota(I32, shape, dim)


def split(a):
    hi = a.astype(BF16)
    return hi, (a - hi.astype(F32)).astype(BF16)


def mm(a, b, dims):
    return lax.dot_general(a, b, dims, preferred_element_type=F32)


def mm3(a, b, dims):
    return mm(a[0], b[0], dims) + (mm(a[0], b[1], dims) + mm(a[1], b[0], dims))


def to_row(col, width):
    rows = col.shape[0]
    same = iota((rows, width), 0) == iota((rows, width), 1)
    return jnp.sum(jnp.where(same, col, 0.0), axis=0, keepdims=True)


def to_col(row, rows):
    width = row.shape[1]
    same = iota((rows, width), 0) == iota((rows, width), 1)
    return jnp.sum(jnp.where(same, row, 0.0), axis=1, keepdims=True)


def tile(ct):
    return slice(ct * CT, (ct + 1) * CT)


def up(n, to):
    return (n + to - 1) // to * to


def seg_at(first, shape, dim, sc):
    p = first + iota(shape, dim)
    total = jnp.zeros(shape, I32)
    for i in range(SEGS):
        total = total + jnp.where(p >= sc[2 + i], 1, 0)
    return total


def quantize(get, pay, rows, nt, inside):
    amax = jnp.zeros((rows, 1), F32)
    for ct in range(nt):
        amax = jnp.maximum(amax, jnp.max(jnp.abs(get(ct)), axis=1, keepdims=True))
    code = jnp.ceil(jnp.log(jnp.maximum(amax, 1e-30) * (1.0 / 32767.0)) * (1.0 / UNIT))
    inv = jnp.exp(code * (-UNIT))
    for ct in range(nt):
        q = jnp.floor(get(ct) * inv + 0.5)
        q = jnp.minimum(jnp.maximum(q, -32767.0), 32767.0)
        pay[0:rows, tile(ct)] = q.astype(I32).astype(I16)
    width = up(rows, 128)
    codes = jnp.broadcast_to(to_row(code, width), (16, width)).astype(I32)
    if inside:
        old = pay[0:16, 0:width].astype(I32)
        pay[0:16, 0:width] = jnp.where(iota((16, width), 0) == 0, codes, old).astype(I16)
    else:
        pay[rows : rows + 16, :] = jnp.zeros((16, nt * CT), I16)
        pay[rows : rows + 16, 0:width] = codes.astype(I16)


def scales_of(codes, rows):
    row = codes.astype(I32).astype(F32)[0:1, :]
    return jnp.exp(to_col(row, rows) * UNIT)


def conv_masks(base, rows, kw, sc):
    here = seg_at(base, (rows, 1), 0, sc)
    out = []
    for tap in range(kw):
        there = seg_at(base - (kw - 1) + tap, (rows, 1), 0, sc)
        out.append(jnp.where(there == here, 1.0, 0.0))
    return out


def conv_tile(ext, ct, cw, cb, masks):
    kw, rows = len(masks), masks[0].shape[0]
    total = jnp.broadcast_to(cb[:, tile(ct)], (rows, CT))
    for tap in range(kw):
        at = HALO - (kw - 1) + tap
        total = total + cw[tap : tap + 1, tile(ct)] * (ext[at : at + rows, tile(ct)] * masks[tap])
    return total


def sigmoid(v):
    return 1.0 / (1.0 + jnp.exp(-v))


def weight_of(allowed, expo):
    return jnp.where(allowed, jnp.exp(jnp.where(allowed, expo, 0.0)), 0.0)


def call(kernel, ins, outs, grid=(1,), in_specs=None, out_specs=None, scratch=(), aliases=None, macs=0, weight=10):
    def spec_of(spec, a):
        if spec is not None:
            return spec
        zeros = (0,) * len(a.shape)
        return pl.BlockSpec(a.shape, lambda *i: zeros, pipeline_mode=pl.Buffered(1))

    in_specs = [spec_of(s, a) for s, a in zip(in_specs or [None] * len(ins), ins)]
    out_specs = [spec_of(s, a) for s, a in zip(out_specs or [None] * len(outs), outs)]
    size = sum(math.prod(a.shape) * a.dtype.itemsize for a in list(ins) + list(outs))
    base = kernel.func if isinstance(kernel, functools.partial) else kernel
    last = base in (join_kernel, up_kernel, down_kernel)
    need = (20 if lax.axis_size("seq") != 8 else 10 if last else 3) * 1024 * 1024
    need += sum(math.prod(c.shape) * c.dtype.itemsize for c in scratch)
    for spec, a in zip(in_specs + out_specs, list(ins) + list(outs)):
        if spec.block_shape is not None and spec.pipeline_mode is None:
            need += 2 * math.prod(spec.block_shape) * a.dtype.itemsize
    return pl.pallas_call(
        kernel,
        name=base.__name__,
        out_shape=[jax.ShapeDtypeStruct(o.shape, o.dtype) for o in outs],
        grid=grid,
        in_specs=in_specs,
        out_specs=out_specs,
        scratch_shapes=list(scratch),
        input_output_aliases=aliases or {},
        compiler_params=pltpu.CompilerParams(vmem_limit_bytes=need),
        cost_estimate=pl.CostEstimate(
            flops=2 * weight * macs + weight // 10 * 10**9, bytes_accessed=size, transcendentals=0
        ),
    )(*ins)


def S(shape, dtype=F32):
    return jax.ShapeDtypeStruct(shape, dtype)


SMEM = pl.BlockSpec(memory_space=pltpu.SMEM)


def prep_kernel(w, bh, bl):
    for m in range(w.shape[0]):
        for ct in range(w.shape[2] // CT):
            t = w[m, :, tile(ct)]
            r, c = iota((CT, CT), 0), iota((CT, CT), 1)
            group = w.shape[1]
            first = c - lax.rem(c, group)
            out = jnp.zeros((CT, CT), F32)
            for j in range(group):
                out = jnp.where(r == first + j, jnp.broadcast_to(t[j : j + 1, :], (CT, CT)), out)
            hi, lo = split(out)
            bh[m, ct], bl[m, ct] = hi, lo


def proj_kernel(send, x, w, g, *refs):
    out, stat = refs[0], refs[1]
    gc = refs[-1]
    k, last = pl.program_id(0), pl.num_programs(0) - 1
    rows, width = x.shape
    wide = w.shape[1]

    @pl.when(k == 0)
    def _():
        total = jnp.zeros((rows, 1), F32)
        for i in range(width // CT):
            gc[i * CT : (i + 1) * CT, :] = jnp.broadcast_to(to_col(g[:, tile(i)], CT), (CT, 128))
            total = total + jnp.sum(x[:, tile(i)].astype(F32), axis=1, keepdims=True)
        mean = total * (1.0 / width)
        total = jnp.zeros((rows, 1), F32)
        for i in range(width // CT):
            d = x[:, tile(i)].astype(F32) - mean
            total = total + jnp.sum(d * d, axis=1, keepdims=True)
        rstd = lax.rsqrt(total * (1.0 / width) + EPS)
        stat[...] = jnp.where(iota((rows, 128), 1) == 0, mean, rstd)

    acc = jnp.zeros((rows, wide), F32)
    for i in range(width // CT):
        hi, lo = split(w[i * CT : (i + 1) * CT, :] * gc[i * CT : (i + 1) * CT, 0:1])
        xt = x[:, tile(i)]
        acc = acc + (mm(xt, hi, NN) + mm(xt, lo, NN))
    at = pl.ds(pl.multiple_of(k * wide, wide), wide)
    out[:, at] = (acc - stat[:, 0:1] * acc[0:1, :]) * stat[:, 1:2]
    if send:

        @pl.when(k == last)
        def _():
            quantize(lambda ct: out[:, tile(ct)], refs[2], rows, out.shape[1] // CT, True)


def proj(x, w, gain, send):
    rows, width = x.shape
    cols = w.shape[1]
    wide = min(cols, 512)
    outs = [S((rows, cols)), S((rows, 128))] + ([S((rows, cols), I16)] if send else [])
    return call(
        functools.partial(proj_kernel, send),
        [x, w, gain.reshape(1, width)],
        outs,
        grid=(cols // wide,),
        in_specs=[
            pl.BlockSpec((rows, width), lambda k: (0, 0)),
            pl.BlockSpec((width, wide), lambda k: (0, k)),
            pl.BlockSpec((1, width), lambda k: (0, 0)),
        ],
        out_specs=[pl.BlockSpec(o.shape, lambda k: (0, 0)) for o in outs],
        scratch=[pltpu.VMEM((width, 128), F32)],
        macs=2 * rows * width * cols,
    )


def dgated_kernel(g, w, out):
    acc = None
    for i in range(w.shape[1] // CT):
        hi, lo = split(w[:, tile(i)])
        part = mm(g[:, tile(i)], hi, NT) + mm(g[:, tile(i)], lo, NT)
        acc = part if acc is None else acc + part
    out[...] = acc


def dgated(g, w):
    rows, width = g.shape
    cols = w.shape[0]
    wide = min(cols, 512)
    return call(
        dgated_kernel,
        [g, w],
        [S((rows, cols))],
        grid=(cols // wide,),
        in_specs=[
            pl.BlockSpec((rows, width), lambda i: (0, 0)),
            pl.BlockSpec((wide, width), lambda i: (i, 0)),
        ],
        out_specs=[pl.BlockSpec((rows, wide), lambda i: (0, i))],
        macs=2 * rows * width * cols,
    )[0]


def front_kernel(sc, ext, bh, bl, cw, cb, gw, act, qh, ql, kh, kl, vh, vl, ph, pl_, gates):
    rows = act.shape[0]
    nt = act.shape[1] // CT
    masks = conv_masks(sc[0] * rows, rows, cw.shape[0], sc)
    total = jnp.zeros((16, rows), F32)
    for ct in range(nt):
        c = conv_tile(ext, ct, cw, cb, masks)
        a = c * sigmoid(c)
        act[:, tile(ct)] = a
        a2 = split(a)
        m2 = split(ext[HALO : HALO + rows, tile(ct)])
        for m, (src, oh, ol) in enumerate(((a2, qh, ql), (a2, kh, kl), (m2, vh, vl))):
            y = split(mm3(src, (bh[m, ct], bl[m, ct]), NN))
            oh[:, tile(ct)], ol[:, tile(ct)] = y
            total = total + mm3(split(gw[m, :, tile(ct)]), y, NT)
            if m == 0:
                ph[:, tile(ct)], pl_[:, tile(ct)] = split(mm3(y, (bh[1, ct], bl[1, ct]), NT))
    gates[...] = total[0:8, :]


def gate_kernel(sc, parts, bias, out):
    heads = bias.shape[0]
    width = parts.shape[1]
    rows8 = parts[...]
    hd = sc[1]
    r = iota((8, width), 0)
    gi = jnp.sum(jnp.where(r == hd, rows8, 0.0), axis=0, keepdims=True)
    gf = jnp.sum(jnp.where(r == hd + heads, rows8, 0.0), axis=0, keepdims=True)
    b = jnp.float32(0.0)
    for h in range(heads):
        b = jnp.where(hd == h, bias[h], b)
    gf = gf + b
    u = jnp.exp(-jnp.abs(gf))
    w = 1.0 + u
    log1p = jnp.where(w == 1.0, u, jnp.log(w) * (u / jnp.where(w == 1.0, 1.0, w - 1.0)))
    keep = jnp.minimum(gf, 0.0) - log1p
    leave = jnp.where(gf >= 0.0, u, 1.0) / w
    upto = iota((width, width), 1) <= iota((width, width), 0)
    run = to_row(jnp.sum(jnp.where(upto, keep, 0.0), axis=1, keepdims=True), width)
    end = jnp.sum(keep, axis=1, keepdims=True)
    vals = [gi - run + end, run, jnp.broadcast_to(end, (1, width)), leave, gi, gi - run]
    res = jnp.zeros((8, width), F32)
    for i, v in enumerate(vals):
        res = jnp.where(r == i, v, res)
    out[...] = res


def between(gv, me, low, high):
    total = jnp.zeros((1, gv.shape[2]), F32)
    for t in range(1, gv.shape[0]):
        run = jnp.bitwise_xor(me, t)
        total = total + jnp.where((run > low) & (run < high), gv[t, 2:3, :], 0.0)
    return total


def local_kernel(sc, qh, ql, kh, kl, vh, vl, gv, hid):
    rows, cols = hid.shape
    nt = cols // CT
    s = jnp.zeros((rows, rows), F32)
    for ct in range(nt):
        s = s + mm3((qh[:, tile(ct)], ql[:, tile(ct)]), (kh[:, tile(ct)], kl[:, tile(ct)]), NT)
    base = sc[0] * rows
    allowed = (iota((rows, rows), 0) >= iota((rows, rows), 1)) & (
        seg_at(base, (rows, 1), 0, sc) == seg_at(base, (1, rows), 1, sc)
    )
    w = weight_of(allowed, to_col(gv[1:2, :], rows) + gv[5:6, :])
    p = split(s * (1.0 / math.sqrt(cols)) * w)
    for ct in range(nt):
        hid[:, tile(ct)] = mm3(p, (vh[:, tile(ct)], vl[:, tile(ct)]), NN)


def block_kernel(count, slot, flip, *refs):
    sc, pays, refs = refs[0], refs[1 : 1 + count], refs[1 + count :]
    ph, pl_, gv, cw, cb = refs[:5]
    u_in = refs[5] if slot else None
    u, ah, al, mh, ml, ps, ws, ext = refs[-8:]
    rows, cols = u.shape
    nt = cols // CT
    i = pl.program_id(0)
    me, src = sc[0], sc[6 + slot + i]
    long = HALO + rows

    @pl.when(i == 0)
    def _():
        u[...] = u_in[...] if slot else jnp.zeros_like(u)

    for b, pay in enumerate(pays):

        place = jnp.where(me // 2 == 2, 3 - b, b) if flip and b else b

        @pl.when((i == place) & (src != me))
        def _(pay=pay):
            scale = scales_of(pay[0:16, 0 : up(long, 128)], long)
            for ct in range(nt):
                ext[:, tile(ct)] = pay[:, tile(ct)].astype(I32).astype(F32) * scale

    @pl.when(src != me)
    def _():
        masks = conv_masks(src * rows, rows, cw.shape[0], sc)
        for ct in range(nt):
            c = conv_tile(ext, ct, cw, cb, masks)
            ah[0, :, tile(ct)], al[0, :, tile(ct)] = split(c * sigmoid(c))

    @pl.when(src < me)
    def _():
        s = jnp.zeros((rows, rows), F32)
        for ct in range(nt):
            t = tile(ct)
            mh[0, :, t], ml[0, :, t] = split(ext[HALO:long, t])
            s = s + mm3((ph[:, t], pl_[:, t]), (ah[0, :, t], al[0, :, t]), NT)
        w = pair_weight(sc, gv, me, src, rows) * (1.0 / math.sqrt(cols))
        s = s * w
        ws[0], ps[0] = w, s
        p = split(s)
        for ct in range(nt):
            t = tile(ct)
            u[:, t] += mm3(p, (mh[0, :, t], ml[0, :, t]), NN)


def pair_weight(sc, gv, me, src, rows):
    allowed = seg_at(me * rows, (rows, 1), 0, sc) == seg_at(src * rows, (1, rows), 1, sc)
    row = between(gv, me, src, me) + gv[jnp.bitwise_xor(me, src), 0:1, :]
    return weight_of(allowed, to_col(gv[0, 1:2, :], rows) + row)


def finish_kernel(hid_in, u, bh, bl, act, z, dg, gn, sk, st, gh, gl, zh, zl, dh, dl, eh, el, dact, rowtot, sums, payd, pays, buf, norm, hid):
    rows, cols = hid.shape
    nt = cols // CT
    total = jnp.zeros((rows, 1), F32)
    for ct in range(nt):
        t = tile(ct)
        h = hid_in[:, t] + mm3(split(u[:, t]), (bh[2, ct], bl[2, ct]), NN)
        hid[:, t] = h
        total = total + jnp.sum(h, axis=1, keepdims=True)
    mean = total * (1.0 / cols)
    total = jnp.zeros((rows, 1), F32)
    for ct in range(nt):
        d = hid[:, tile(ct)] - mean
        total = total + jnp.sum(d * d, axis=1, keepdims=True)
    rstd = lax.rsqrt(total * (1.0 / cols) + EPS)
    m1 = jnp.zeros((rows, 1), F32)
    m2 = jnp.zeros((rows, 1), F32)
    xm, xr = st[HALO : HALO + rows, 0:1], st[HALO : HALO + rows, 1:2]
    r8 = iota((8, CT), 0)
    for ct in range(nt):
        t = tile(ct)
        n = (hid[:, t] - mean) * rstd
        a = act[:, t]
        full = n * gn[:, t] + sk[:, t] * a
        zz = z[HALO : HALO + rows, t]
        sg = sigmoid(zz)
        gate = zz * sg
        gated = full * gate
        buf[0, :, t] = gated
        gh[:, t], gl[:, t] = split(gated)
        dgt = dg[:, t]
        da = dgt * gate
        dz = dgt * full * (sg * (1.0 + zz * (1.0 - sg)))
        zh[:, t], zl[:, t] = split(dz)
        dzr = dz * xr
        buf[1, :, t] = dzr
        dact[:, t] = da * sk[:, t]
        dn = da * gn[:, t]
        buf[2, :, t] = dn
        norm[:, t] = n
        m1 = m1 + jnp.sum(dn, axis=1, keepdims=True)
        m2 = m2 + jnp.sum(dn * n, axis=1, keepdims=True)
        s0 = jnp.sum(da * n, axis=0, keepdims=True)
        s1 = jnp.sum(da * a, axis=0, keepdims=True)
        s2 = jnp.sum(dzr * xm, axis=0, keepdims=True)
        sums[:, t] = jnp.where(r8 == 0, s0, jnp.where(r8 == 1, s1, jnp.where(r8 == 2, s2, 0.0)))
    m1, m2 = m1 * (1.0 / cols), m2 * (1.0 / cols)
    total = jnp.zeros((rows, 1), F32)
    for ct in range(nt):
        t = tile(ct)
        d = rstd * (buf[2, :, t] - m1 - norm[:, t] * m2)
        buf[2, :, t] = d
        d2 = split(d)
        dh[:, t], dl[:, t] = d2
        eh[:, t], el[:, t] = split(mm3(d2, (bh[2, ct], bl[2, ct]), NT))
        total = total + jnp.sum(d * hid[:, t], axis=1, keepdims=True)
    rowtot[...] = jnp.broadcast_to(total, rowtot.shape)
    quantize(lambda ct: buf[2, :, tile(ct)], payd, rows, nt, False)
    quantize(lambda ct: buf[0, :, tile(ct)], pays.at[0], rows, nt, False)
    quantize(lambda ct: buf[1, :, tile(ct)], pays.at[1], rows, nt, False)


def part_rows(a, buf, sc, keep, give):
    buf[...] = a
    q = a.shape[0] // 4
    mine = lax.rem(sc[1], 2)
    for half in range(2):
        at = pl.multiple_of(half * 2 * q + mine * q, q)
        keep[half * q : half * q + q, :] = buf[pl.ds(at, q), :]
        at = pl.multiple_of(half * 2 * q + (1 - mine) * q, q)
        give[half * q : half * q + q, :] = buf[pl.ds(at, q), :]


def branch_kernel(sc, gh, gl, w, keep, give, buf):
    acc = None
    for i in range(w.shape[0] // CT):
        part = mm3((gh[:, tile(i)], gl[:, tile(i)]), split(w[i * CT : (i + 1) * CT, :]), NN)
        acc = part if acc is None else acc + part
    part_rows(acc, buf, sc, keep, give)


def branch_of(sc, gh, gl, w):
    rows, cols = gh.shape
    width = w.shape[1]
    wide = 512
    half = pl.BlockSpec((rows // 2, wide), lambda i: (0, i))
    return call(
        branch_kernel,
        [sc, gh, gl, w],
        [S((rows // 2, width))] * 2,
        grid=(width // wide,),
        in_specs=[SMEM, None, None, pl.BlockSpec((cols, wide), lambda i: (0, i))],
        out_specs=[half, half],
        scratch=[pltpu.VMEM((rows, wide), F32)],
        macs=3 * rows * width * cols,
    )


def result_kernel(sc, a, b, x, out, squares):
    q = out.shape[0]
    branch = a[...] + b[...]
    result = x[pl.ds(pl.multiple_of(sc[1] * q, q), q), :].astype(F32) + branch
    out[...] = result.astype(BF16)
    r2 = jnp.sum(jnp.sum(result * result, axis=1, keepdims=True), axis=0, keepdims=True)
    b2 = jnp.sum(jnp.sum(branch * branch, axis=1, keepdims=True), axis=0, keepdims=True)
    lane = iota(squares.shape, 1)
    squares[...] = jnp.where(lane == 0, r2, jnp.where(lane == 1, b2, 0.0))


def local_back(sc, qh, ql, kh, kl, vh, vl, dh, dl, gv, bh, bl, dq_in, dq, dk, dv, col, rh, rl):
    rows, cols = dq.shape
    nt = cols // CT
    st = jnp.zeros((rows, rows), F32)
    dpt = jnp.zeros((rows, rows), F32)
    for ct in range(nt):
        t = tile(ct)
        st = st + mm3((kh[:, t], kl[:, t]), (qh[:, t], ql[:, t]), NT)
        dpt = dpt + mm3((vh[:, t], vl[:, t]), (dh[:, t], dl[:, t]), NT)
        rh[:, t], rl[:, t] = split(mm3((kh[:, t], kl[:, t]), (bh[0, ct], bl[0, ct]), NT))
    base = sc[0] * rows
    allowed = (iota((rows, rows), 1) >= iota((rows, rows), 0)) & (
        seg_at(base, (rows, 1), 0, sc) == seg_at(base, (1, rows), 1, sc)
    )
    w = weight_of(allowed, gv[1:2, :] + to_col(gv[5:6, :], rows))
    scaled = w * (1.0 / math.sqrt(cols))
    pt = st * scaled
    dst = dpt * scaled
    col[...] = jnp.broadcast_to(jnp.sum(dpt * pt, axis=1, keepdims=True), col.shape)
    pt2, dst2, ds2 = split(pt), split(dst), split(dst.T)
    for ct in range(nt):
        t = tile(ct)
        dv[:, t] = mm3(pt2, (dh[:, t], dl[:, t]), NN)
        dk[:, t] = mm3(dst2, (qh[:, t], ql[:, t]), NN)
        dq[:, t] = dq_in[:, t] + mm3(ds2, (kh[:, t], kl[:, t]), NN)


def flow_kernel(sc, mh, ml, ps, ws, eh, el, pay_in, dsh, dsl, pay, vec):
    rows = eh.shape[0]
    nt = eh.shape[1] // CT
    i, last = pl.program_id(0), pl.num_programs(0) - 1
    me, src = sc[0], sc[6 + i]

    @pl.when(i == 0)
    def _():
        vec[...] = jnp.zeros_like(vec)

    @pl.when(src < me)
    def _():
        dp = jnp.zeros((rows, rows), F32)
        for ct in range(nt):
            t = tile(ct)
            dp = dp + mm3((eh[:, t], el[:, t]), (mh[0, :, t], ml[0, :, t]), NT)
        dsh[0], dsl[0] = split(dp * ws[0])
        flow = jnp.sum(dp * ps[0], axis=0, keepdims=True)
        flow = jnp.sum(flow, axis=1, keepdims=True)
        lane = iota(vec.shape, 1)
        vec[...] += jnp.where((lane > src) & (lane < me), flow, 0.0)

    @pl.when(i == last)
    def _():
        v = vec[0:1, :]
        top = jnp.maximum(jnp.max(jnp.abs(v), axis=1, keepdims=True), 1e-30)
        code = jnp.ceil(jnp.log(top * (1.0 / 32000.0)) * (1.0 / UNIT))
        v = v * jnp.exp(code * (-UNIT))
        whole = jnp.floor(v)
        digits = [whole, jnp.floor((v - whole) * 32767.0 + 0.5), jnp.broadcast_to(code, v.shape)]
        r = iota((16, 128), 0)
        out = pay_in[:, 0:128].astype(I32)
        for k, d in enumerate(digits):
            out = jnp.where(r == k + 1, d.astype(I32), out)
        pay[...] = pay_in[...]
        pay[:, 0:128] = out.astype(I16)


def flows(sc, bufs, e2, pay):
    mh, ml, ps, ws = bufs[2:]
    slots, rows, cols = mh.shape
    moving = pl.BlockSpec((1, rows, cols), lambda i: (i, 0, 0))
    square = pl.BlockSpec((1, rows, rows), lambda i: (i, 0, 0))
    codes = pl.BlockSpec((16, cols), lambda i: (rows // 16, 0))
    return call(
        flow_kernel,
        [sc, mh, ml, ps, ws, *e2, pay],
        [S((slots, rows, rows), BF16)] * 2 + [pay],
        grid=(slots,),
        in_specs=[SMEM] + [moving] * 2 + [square] * 2 + [None] * 2 + [codes],
        out_specs=[square, square, codes],
        scratch=[pltpu.VMEM((8, 128), F32)],
        aliases={7: 2},
        weight=0,
        macs=slots * 3 * rows * rows * cols // 2,
    )


def earlier_kernel(sc, ah, al, dsh, dsl, bh, bl, dq, acc):
    nt = dq.shape[1] // CT
    i, last = pl.program_id(0), pl.num_programs(0) - 1

    @pl.when(i == 0)
    def _():
        acc[...] = jnp.zeros_like(acc)

    @pl.when(sc[6 + i] < sc[0])
    def _():
        ds = (dsh[0], dsl[0])
        for ct in range(nt):
            t = tile(ct)
            acc[:, t] += mm3(ds, (ah[0, :, t], al[0, :, t]), NN)

    @pl.when(i == last)
    def _():
        for ct in range(nt):
            t = tile(ct)
            dq[:, t] = mm3(split(acc[:, t]), (bh[1, ct], bl[1, ct]), NN)


def earlier(sc, bufs, ds, bh, bl):
    slots, rows, cols = bufs[0].shape
    moving = pl.BlockSpec((1, rows, cols), lambda i: (i, 0, 0))
    square = pl.BlockSpec((1, rows, rows), lambda i: (i, 0, 0))
    return call(
        earlier_kernel,
        [sc, *bufs[:2], *ds, bh, bl],
        [S((rows, cols))],
        grid=(slots,),
        in_specs=[SMEM] + [moving] * 2 + [square] * 2 + [None] * 2,
        scratch=[pltpu.VMEM((rows, cols), F32)],
        weight=0,
        macs=slots * 3 * rows * rows * cols // 2,
    )[0]


def pick(slots, i):
    out = slots[0]
    for b, slot in enumerate(slots[1:]):
        out = jnp.where(i == b + 1, slot, out)
    return out


def later_kernel(slots, *refs):
    count = len(slots)
    sc, pays, refs = refs[0], refs[1 : 1 + count], refs[1 + count :]
    ah, al, rh, rl, vh, vl, gv = refs[:7]
    e_in, dv_in, col_in, flow_in = refs[7:11] if len(refs) == 17 else (None, refs[7], None, None)
    e, dv, col, flow, ph, pl_ = refs[-6:]
    rows, cols = e.shape
    nt = cols // CT
    i = pl.program_id(0)
    me, src = sc[0], sc[6 + pick(slots, i)]

    @pl.when(i == 0)
    def _():
        e[...] = jnp.zeros_like(e) if e_in is None else e_in[...]
        dv[...] = dv_in[...]
        col[...] = jnp.zeros_like(col) if col_in is None else col_in[...]
        flow[...] = jnp.zeros_like(flow) if flow_in is None else flow_in[...]

    for b, pay in enumerate(pays):

        @pl.when((src > me) & (i == b))
        def _(pay=pay):
            scale = scales_of(pay[rows : rows + 16, 0:rows], rows)
            for ct in range(nt):
                t = tile(ct)
                ph[:, t], pl_[:, t] = split(pay[0:rows, t].astype(I32).astype(F32) * scale)
            d = pay[rows : rows + 16, 0:128].astype(I32).astype(F32)
            v = (d[1:2, :] + d[2:3, :] * (1.0 / 32767.0)) * jnp.exp(d[3:4, :] * UNIT)
            v = jnp.where(iota((1, 128), 1) == me, v, 0.0)
            flow[...] += jnp.sum(v, axis=1, keepdims=True)

    @pl.when(src > me)
    def _():
        st = jnp.zeros((rows, rows), F32)
        dpt = jnp.zeros((rows, rows), F32)
        for ct in range(nt):
            t = tile(ct)
            st = st + mm3((rh[:, t], rl[:, t]), (ah[0, :, t], al[0, :, t]), NT)
            dpt = dpt + mm3((vh[:, t], vl[:, t]), (ph[:, t], pl_[:, t]), NT)
        allowed = seg_at(me * rows, (rows, 1), 0, sc) == seg_at(src * rows, (1, rows), 1, sc)
        row = between(gv, me, me, src) + gv[jnp.bitwise_xor(me, src), 1:2, :]
        w = weight_of(allowed, to_col(gv[0, 0:1, :], rows) + row)
        scaled = w * (1.0 / math.sqrt(cols))
        pt = st * scaled
        col[...] += jnp.sum(dpt * pt, axis=1, keepdims=True)
        pt2, dst2 = split(pt), split(dpt * scaled)
        for ct in range(nt):
            t = tile(ct)
            dv[:, t] += mm3(pt2, (ph[:, t], pl_[:, t]), NN)
            e[:, t] += mm3(dst2, (ah[0, :, t], al[0, :, t]), NN)


def gate_back_kernel(sc, col_here, col_later, rowtot, gv, flow, out):
    rows = rowtot.shape[0]
    here, later = col_here[:, 0:1], col_later[:, 0:1]
    t, p = iota((rows, rows), 1), iota((rows, rows), 0)
    val = to_row(rowtot[:, 0:1] - here, rows)
    dlk = jnp.sum(jnp.where(t >= p, val, 0.0), axis=1, keepdims=True)
    dlk = dlk + jnp.sum(jnp.where(t < p, to_row(later, rows), 0.0), axis=1, keepdims=True)
    dlk = dlk + flow[0:1, 0:1]
    r = iota((8, rows), 0)
    d_in = to_row(here + later, rows)
    d_f = to_row(dlk, rows) * gv[3:4, :]
    out[...] = jnp.where(r == sc[1], d_in, jnp.where(r == sc[1] + out.shape[0] // 2, d_f, 0.0))


def back_kernel(sc, ext, dact, dq, dk, e, dv, bh, bl, cw, cb, gw, dg, dm, rim, d0h, d0l, d1h, d1l, d2h, d2l, dco, dcs):
    rows = dq.shape[0]
    kw = cw.shape[0]
    base = sc[0] * rows
    masks = conv_masks(base, rows, kw, sc)
    long = HALO + rows
    here = seg_at(base - HALO, (long, 1), 0, sc)
    back_masks = []
    for tap in range(kw):
        there = seg_at(base - HALO + kw - 1 - tap, (long, 1), 0, sc)
        back_masks.append(jnp.where(there == here, 1.0, 0.0))
    g2 = split(jnp.concatenate([dg[...], jnp.zeros((8, rows), F32)], axis=0))
    dcs[0:HALO, :] = jnp.zeros((HALO, CT), F32)
    dcs[long : HALO + long, :] = jnp.zeros((HALO, CT), F32)
    dk_all = dk[...] + mm3(split(e[...]), (bh[0, 0], bl[0, 0]), NN)
    grads = (dq[...], dk_all, dv[...])
    kept = ((d0h, d0l), (d1h, d1l), (d2h, d2l))
    back = []
    for m in range(3):
        d2 = split(grads[m] + mm3(g2, split(gw[m]), TN))
        kept[m][0][...], kept[m][1][...] = d2
        back.append(mm3(d2, (bh[m, 0], bl[m, 0]), NT))
    c = conv_tile(ext, 0, cw, cb, masks)
    sg = sigmoid(c)
    dc = (dact[...] + back[0] + back[1]) * (sg * (1.0 + c * (1.0 - sg)))
    dco[...] = dc
    dcs[HALO:long, :] = dc
    dext = jnp.zeros((long, CT), F32)
    for tap in range(kw):
        at = kw - 1 - tap
        dext = dext + cw[tap : tap + 1, :] * (dcs[at : at + long, :] * back_masks[tap])
    rim[...] = dext[0:HALO, :]
    dm[...] = dext[HALO:, :] + back[2]


def small_kernel(sc, ext, act, dc, d0h, d0l, d1h, d1l, d2h, d2l, qh, ql, kh, kl, vh, vl, dg, cw, pack):
    rows = act.shape[0]
    kw = cw.shape[0]
    masks = conv_masks(sc[0] * rows, rows, kw, sc)
    long = HALO + rows
    g = jnp.concatenate([dg[...], jnp.zeros((8, rows), F32)], axis=0)
    g2 = split(g)
    pack[...] = jnp.zeros_like(pack)
    pack[41:42, 0:128] = to_row(jnp.sum(g, axis=1, keepdims=True), 128)
    group = 4
    sub, lane = iota((CT, CT), 0), iota((CT, CT), 1)
    diagonal = (sub - lax.rem(sub, group)) == (lane - lax.rem(lane, group))
    a2 = split(act[...])
    m2 = split(ext[HALO:long, :])
    grads = ((d0h, d0l), (d1h, d1l), (d2h, d2l))
    stored = ((qh, ql), (kh, kl), (vh, vl))
    for m in range(3):
        gate_rows = mm3(g2, (stored[m][0][...], stored[m][1][...]), NN)
        pack[17 + 8 * m : 25 + 8 * m, :] = gate_rows[0:8, :]
        d2 = (grads[m][0][...], grads[m][1][...])
        outer = jnp.where(diagonal, mm3(a2 if m < 2 else m2, d2, TN), 0.0)
        eight = outer[0:8, :]
        for r in range(1, CT // 8):
            eight = eight + outer[8 * r : 8 * r + 8, :]
        pack[5 + group * m : 5 + group * (m + 1), :] = eight[0:4, :] + eight[4:8, :]
    d = dc[...]
    pack[4:5, :] = jnp.sum(d, axis=0, keepdims=True)
    for tap in range(kw):
        at = HALO - (kw - 1) + tap
        pack[tap : tap + 1, :] = jnp.sum(d * (ext[at : at + rows, :] * masks[tap]), axis=0, keepdims=True)


def by_columns(kernel, ins, outs, scratch=(), macs=0, fixed=(), weight=10):
    def spec(a, index=None):
        if index == 0:
            return SMEM
        if index in fixed:
            return None
        if len(a.shape) == 2:
            return pl.BlockSpec((a.shape[0], CT), lambda i: (0, i))
        if len(a.shape) == 3:
            return pl.BlockSpec((a.shape[0], a.shape[1], CT), lambda i: (0, 0, i))
        return pl.BlockSpec((a.shape[0], 1, CT, CT), lambda i: (0, i, 0, 0))

    return call(
        kernel,
        ins,
        outs,
        grid=(outs[0].shape[1] // CT,),
        in_specs=[spec(a, k) for k, a in enumerate(ins)],
        out_specs=[spec(o) for o in outs],
        scratch=scratch,
        macs=macs,
        weight=weight,
    )


def send_kernel(dm, rim, st, mh, ml, pay, ux, buf):
    rows, cols = dm.shape
    nt = cols // CT
    xm, xr = st[HALO : HALO + rows, 0:1], st[HALO : HALO + rows, 1:2]
    for ct in range(nt):
        t = tile(ct)
        buf[:, t] = dm[:, t]
        buf[rows - HALO : rows, t] = dm[rows - HALO : rows, t] + rim[:, t]
        d = buf[:, t]
        mh[:, t], ml[:, t] = split(d)
        d = d * xr
        buf[:, t] = d
        ux[:, t] = jnp.broadcast_to(jnp.sum(d * xm, axis=0, keepdims=True), (8, CT))
    quantize(lambda ct: buf[:, tile(ct)], pay, rows, nt, False)


def beside_kernel(sc, *refs):
    ins, (zh, zl, w, g), outs, out = refs[:12], refs[12:16], refs[16:22], refs[22]

    @pl.when(pl.program_id(0) == 0)
    def _():
        local_back(sc, *ins, *outs)

    out[...] = mm3((zh[...], zl[...]), split(w[...] * to_col(g[0], CT)), NT)


def beside(sc, locals_in, zh, zl, w, gain):
    rows, cols = zh.shape
    width = w.shape[0]
    return call(
        beside_kernel,
        [sc, *locals_in, zh, zl, w, gain.reshape(width // CT, 1, CT)],
        [S((rows, cols))] * 3 + [S((rows, 128))] + [S((rows, cols), BF16)] * 2 + [S((rows, width))],
        grid=(width // CT,),
        in_specs=[SMEM]
        + [None] * 14
        + [pl.BlockSpec((CT, cols), lambda i: (i, 0)), pl.BlockSpec((1, 1, CT), lambda i: (i, 0, 0))],
        out_specs=[None] * 6 + [pl.BlockSpec((rows, CT), lambda i: (0, i))],
        macs=3 * rows * width * cols,
        weight=10,
    )


def dnorm_kernel(sc, ah, al, w, g, other, x, st, keep, give, ln, buf):
    a = other[...] + mm3((ah[...], al[...]), split(w[...] * to_col(g[0], CT)), NT)
    part_rows(a, buf, sc, keep, give)
    rows = a.shape[0]
    xhat = (x[...].astype(F32) - st[HALO : HALO + rows, 0:1]) * st[HALO : HALO + rows, 1:2]
    ln[0] = jnp.sum(a * xhat, axis=0, keepdims=True) / g[0]


def dnorm(sc, ah, al, w, gain, other, x, st):
    rows, cols = ah.shape
    width = w.shape[0]
    gspec = pl.BlockSpec((1, 1, CT), lambda i: (i, 0, 0))
    wide = pl.BlockSpec((rows, CT), lambda i: (0, i))
    half = pl.BlockSpec((rows // 2, CT), lambda i: (0, i))
    return call(
        dnorm_kernel,
        [sc, ah, al, w, gain.reshape(width // CT, 1, CT), other, x, st],
        [S((rows // 2, width)), S((rows // 2, width)), S((width // CT, 1, CT))],
        grid=(width // CT,),
        in_specs=[SMEM, None, None, pl.BlockSpec((CT, cols), lambda i: (i, 0)), gspec, wide, wide, None],
        out_specs=[half, half, gspec],
        scratch=[pltpu.VMEM((rows, CT), F32)],
        macs=3 * rows * width * cols,
    )


def second_kernel(sc, a, b, keep, give):
    q = keep.shape[0]
    mine = sc[1] // 2
    at = pl.multiple_of(mine * q, q)
    keep[...] = a[pl.ds(at, q), :] + b[pl.ds(at, q), :]
    at = pl.multiple_of((1 - mine) * q, q)
    give[...] = a[pl.ds(at, q), :] + b[pl.ds(at, q), :]


def norm_back_kernel(sc, a, b, x, g, out):
    q, width = out.shape
    at = pl.multiple_of(sc[1] * q, q)
    xs = x[pl.ds(at, q), :].astype(F32)
    dn = a[...] + b[...]
    c = xs - jnp.mean(xs, axis=1, keepdims=True)
    rstd = lax.rsqrt(jnp.mean(c * c, axis=1, keepdims=True) + EPS)
    xhat = c * rstd
    m1 = jnp.mean(dn, axis=1, keepdims=True)
    m2 = jnp.mean(dn * xhat, axis=1, keepdims=True)
    out[...] = g[pl.ds(at, q), :].astype(F32) + rstd * (dn - m1 - xhat * m2)


def left_kernel(sc, x, g, *outs):
    m = len(outs)
    wide = outs[0].shape[1]
    ring, kind = sc[0] // 2, lax.rem(sc[1], 2)
    for s, out in enumerate(outs):
        cols = pl.ds(pl.multiple_of(lax.rem(ring - s + m, m) * wide, wide), wide)

        @pl.when(kind == 0)
        def _(out=out, cols=cols):
            out[...] = x[:, cols]

        @pl.when(kind == 1)
        def _(out=out, cols=cols):
            out[...] = g[:, cols]


def join_kernel(sc, own, a, b, c, out):
    q = own.shape[0]
    for bits, part in enumerate((own, a, b, c)):
        at = pl.multiple_of(jnp.bitwise_xor(sc[1], bits) * q, q)
        out[pl.ds(at, q), :] = part[...]


def wgrad_kernel(m, kinds, sc, *refs):
    parts, refs = refs[:2], refs[2:]
    count = len(refs) // 2 - 2
    pays, codes = refs[:count], refs[count : 2 * count]
    keep, pay, buf, left = refs[2 * count :]
    rows, hf = left.shape[3:]
    kind = pick(kinds, pl.program_id(0))
    ct, last = pl.program_id(1), pl.num_programs(1) - 1
    odd = lax.rem(sc[0], 2)
    ring = sc[0] // 2
    mine, other = left.at[kind, odd], left.at[kind, 1 - odd]

    @pl.when((pl.program_id(0) == 0) & (ct == 0))
    def _():
        for bits, part in enumerate(parts):
            at = jnp.bitwise_xor(lax.rem(sc[1], 2), bits)
            for half in range(2):
                left[at, half] = part[:, :, half * hf : (half + 1) * hf]

    def slots(refs):
        every = [r[0].astype(I32) for r in refs]
        if m != 4:
            return every
        own, down1, up1, down2, up2, three = every
        far = jnp.where(ring == m - 1, three, 0)
        near = jnp.where(ring == 0, three, 0)
        return [own, down1 + far, down2 + up2, up1 + near]

    a = jnp.zeros((hf, CT), F32)
    b = jnp.zeros((hf, CT), F32)
    for s, (q, c) in enumerate(zip(slots(pays), slots(codes))):
        hi, lo = split(q.astype(F32) * jnp.exp(to_col(c.astype(F32)[0:1, :], rows) * UNIT))
        a = a + (mm(mine[s], hi, TN) + mm(mine[s], lo, TN))
        b = b + (mm(other[s], hi, TN) + mm(other[s], lo, TN))
    keep[0] = a
    buf[:, pl.ds(pl.multiple_of(ct * CT, CT), CT)] = b

    @pl.when(ct == last)
    def _():
        quantize(lambda c: buf[:, tile(c)], pay.at[0], hf, buf.shape[1] // CT, False)


def wgrad(sc, left, kinds, pays):
    m, rows, hf = left[0].shape
    hf = hf // 2
    cols = pays[0].shape[2]
    count = len(kinds)
    return call(
        functools.partial(wgrad_kernel, m, kinds),
        [sc, *left, *pays, *pays],
        [S((count, hf, cols)), S((count, hf + 16, cols), I16)],
        grid=(count, cols // CT),
        in_specs=[SMEM] + [None] * 2
        + [pl.BlockSpec((1, rows, CT), lambda p, i: (p, 0, i))] * len(pays)
        + [pl.BlockSpec((1, 16, rows), lambda p, i: (p, rows // 16, 0))] * len(pays),
        out_specs=[
            pl.BlockSpec((1, hf, CT), lambda p, i: (p, 0, i)),
            pl.BlockSpec((1, hf + 16, cols), lambda p, i: (p, 0, 0)),
        ],
        scratch=[pltpu.VMEM((hf, cols), F32), pltpu.VMEM((2, 2, m, rows, hf), BF16)],
        macs=4 * count * m * hf * rows * cols,
    )


def received(pay, ct, rows):
    return pay[0:rows, tile(ct)].astype(I32).astype(F32)


def down_kernel(keep, pay, out):
    rows, cols = keep.shape[1:]
    scale = scales_of(pay[0, rows : rows + 16, 0 : up(rows, 128)], rows)
    for ct in range(cols // CT):
        t = keep[0, :, tile(ct)] + received(pay.at[0], ct, rows) * scale
        out[tile(ct), :] = t.T


def up_kernel(which, keep, pay, gain, u, out):
    rows, cols = out.shape
    scale = scales_of(pay[which, rows : rows + 16, 0 : up(rows, 128)], rows)
    g = to_col(gain[...], rows)
    for ct in range(cols // CT):
        t = keep[which, :, tile(ct)] + received(pay.at[which], ct, rows) * scale
        out[:, tile(ct)] = g * (t - u[:, tile(ct)])


def shifted(a, by):
    n = lax.axis_size("seq")
    return lax.ppermute(a, "seq", [(i, (i + by) % n) for i in range(n)])


def swapped(a, axis, bit):
    n = lax.axis_size(axis)
    return lax.ppermute(a, axis, [(i, i ^ bit) for i in range(n)])


def sum_over(a, axis):
    bit = 1
    while bit < lax.axis_size(axis):
        a = a + swapped(a, axis, bit)
        bit *= 2
    return a


def moved(a, pairs):
    return lax.ppermute(a, "seq", pairs)


def gather_runs(pay):
    n = lax.axis_size("seq")
    if n != 8:
        return [[shifted(pay, s) for s in range(1, n)]]
    z = lax.axis_index("seq") // 2
    step_up, step_down = [(i, i + 2) for i in range(6)], [(i + 2, i) for i in range(6)]
    up1, down1 = moved(pay, step_up), moved(pay, step_down)
    x = swapped(pay, "seq", 1)
    up2 = moved(jnp.where(z == 0, x, up1), step_up)
    down2 = moved(jnp.where(z == 3, x, down1), step_down)
    side = swapped(jnp.where(z < 2, down1, up1), "seq", 1)
    far = jnp.where(z < 2, down2, up2)
    three = moved(far, [(2, 0), (3, 1), (4, 6), (5, 7)])
    side2 = swapped(far, "seq", 1)
    side3 = moved(three, [(0, 1), (1, 0), (6, 7), (7, 6)])
    return [[x, up1, down1], [up2, down2, side], [side2, three], [side3, side3]]


def gather_later(pay, steps):
    n = lax.axis_size("seq")
    if n != 8:
        last = pay
        for step in steps[:2]:
            last = step(last)
        return last, [], [(list(range(n - 1)), [shifted(pay, s) for s in range(1, n)])]
    one = moved(pay, [(i, i - 2) for i in range(2, 8)])
    x = moved(pay, [(i, i - 1) for i in range(1, 8, 2)])
    done = steps[0](pay)
    two = moved(after(one, done), [(i, i - 2) for i in range(2, 6)])
    x_one = moved(after(one, done), [(i, i ^ 1) for i in range(6)])
    done = steps[1](done)
    three = moved(after(two, done), [(i, i - 2) for i in range(2, 4)])
    x_two = moved(after(two, done), [(i, i ^ 1) for i in range(4)])
    state = steps[2]([0, 2], [x, one])
    x_three = moved(after(three, state[0]), [(0, 1), (1, 0)])
    return two, state, [([5, 4], [x_one, two]), ([6, 7, 8], [x_two, three, x_three])]


def gather_xor(a):
    a = a[None]
    bit = 1
    while bit < lax.axis_size("seq"):
        a = jnp.concatenate([a, swapped(a, "seq", bit)])
        bit *= 2
    return a


def sources(me, n):
    if n != 8:
        return [lax.rem(me - s + n, n) for s in range(1, n)]
    z, x = me // 2, lax.rem(me, 2)

    def run(ring, other):
        return ring * 2 + (1 - x if other else x)

    up2 = jnp.where(z == 1, run(0, True), run(z - 2, False))
    return [
        run(z, True),
        jnp.where(z > 0, run(z - 1, False), me),
        jnp.where(z < 3, run(z + 1, False), me),
        jnp.where(z > 0, up2, me),
        jnp.where(z == 2, run(1, True), jnp.where(z < 3, run(z + 2, False), me)),
        jnp.where(z == 2, run(3, True), run(jnp.where(z < 2, z + 1, z - 1), True)),
        run(jnp.where(z < 2, z + 2, z - 2), True),
        jnp.where(z == 0, run(3, False), jnp.where(z == 3, run(0, False), me)),
        jnp.where(z == 0, run(3, True), jnp.where(z == 3, run(0, True), me)),
        me,
    ]


def ring_up(pay):
    m = lax.axis_size("seq") // 2
    if m != 4:
        return [shifted(pay, -2 * s) for s in range(1, m)]
    return [moved(pay, [(i, i + 2) for i in range(6)])]


def ring_down(pay):
    if lax.axis_size("seq") != 8:
        return []
    return [moved(pay, [(i + 2, i) for i in range(6)])]


def ring_up2(up):
    return [moved(a, [(i, i + 2) for i in range(2, 6)]) for a in up] if lax.axis_size("seq") == 8 else []


def ring_down2(down):
    return [moved(a, [(i, i - 2) for i in range(2, 6)]) for a in down]


def ring_third(up, down, up2, down2):
    last = [moved(b + a, [(2, 0), (3, 1), (4, 6), (5, 7)]) for a, b in zip(up2, down2)]
    return down + up + down2 + up2 + last


def after(array, *others):
    if isinstance(array, list):
        return list(lax.optimization_barrier((*array, *others))[: len(array)])
    return lax.optimization_barrier((array, *others))[0]


def per_device(
    stream,
    ln_gain,
    up_x,
    up_z,
    conv_w,
    conv_b,
    qkv_w,
    gate_w,
    gate_bias,
    gn_gain,
    skip,
    down_w,
    cotangent,
    lengths,
):
    rows, width = stream.shape
    cols = up_x.shape[1]
    kw = conv_w.shape[0]
    heads = gate_w.shape[0] // 2
    n = lax.axis_size("seq")
    m = n // 2
    me, hd = lax.axis_index("seq"), lax.axis_index("head")
    starts = jnp.cumsum(lengths) - lengths
    order = sources(me, n)
    sc = jnp.concatenate([jnp.stack([me, hd]), starts, jnp.stack(order)]).astype(I32)
    cb, gn, sk = conv_b.reshape(1, cols), gn_gain.reshape(1, cols), skip.reshape(1, cols)
    gw = jnp.pad(gate_w.transpose(1, 0, 2), ((0, 0), (0, 16 - 2 * heads), (0, 0)))
    tall = S((rows, cols))
    tall16 = S((rows, cols), BF16)

    hf = width // m // 2
    slices = call(
        left_kernel,
        [sc, stream, cotangent],
        [S((rows, 2 * hf), BF16)] * m,
        in_specs=[SMEM, None, None],
        weight=0,
    )
    left = [jnp.stack([shifted(a, -2 * k) if k else a for k, a in enumerate(slices)])]

    halo = lax.ppermute(stream[rows - HALO :], "seq", [(i, i + 1) for i in range(n - 1)])
    nt = cols // CT
    bh, bl = call(prep_kernel, [qkv_w], [S((3, nt, CT, CT), BF16)] * 2)
    x_ext = after(jnp.concatenate([jnp.ones((1, width), BF16), halo[1:], stream]), bh)
    mixed, stat, pay = proj(x_ext, up_x, ln_gain, True)
    runs = gather_runs(pay)
    hops = [runs[min(k, len(runs) - 1)] for k in range(3)]

    act, qh, ql, kh, kl, vh, vl, ph, pl_, gate_part = call(
        front_kernel,
        [after(sc, *left), mixed, bh, bl, conv_w, cb, gw],
        [tall] + [tall16] * 8 + [S((8, rows))],
        in_specs=[SMEM] + [None] * 6,
        macs=12 * rows * cols * CT,
    )
    (gv,) = call(
        gate_kernel,
        [after(sc, *hops[0]), sum_over(gate_part, "head"), gate_bias],
        [S((8, rows))],
        in_specs=[SMEM, None, SMEM],
        weight=0,
    )
    gvs = gather_xor(gv)

    left.append(swapped(left[0], "head", 1))
    outgate = proj(after(x_ext, gate_part, *hops[0]), up_z, ln_gain, False)[0]
    dgate = dgated(after(cotangent, outgate, *hops[1]), down_w)
    (hid,) = call(
        local_kernel,
        [sc, qh, ql, kh, kl, vh, vl, gv],
        [tall],
        in_specs=[SMEM] + [None] * 7,
        macs=6 * rows * rows * cols,
    )
    slots_all = sum(map(len, runs))
    u, bufs = None, []
    slot = 0
    for stage, pays in enumerate(runs):
        count = len(pays)
        ins = [after(sc, *hops[2]) if stage == 0 else sc, *pays, ph, pl_, gvs, conv_w, cb]
        specs = [SMEM] + [None] * (count + 5)
        aliases = {}
        if slot:
            ins += [u, *bufs]
            specs += [None] + [pl.BlockSpec(memory_space=pl.ANY)] * 6
            aliases = {6 + count + i: i for i in range(7)}
        place = pl.BlockSpec((1, rows, cols), lambda i, slot=slot: (slot + i, 0, 0))
        square = pl.BlockSpec((1, rows, rows), lambda i, slot=slot: (slot + i, 0, 0))
        u, *bufs = call(
            functools.partial(block_kernel, count, slot, n == 8 and stage == 1),
            ins,
            [tall] + [S((slots_all, rows, cols), BF16)] * 4 + [S((slots_all, rows, rows))] * 2,
            grid=(count,),
            in_specs=specs,
            out_specs=[None] + [place] * 4 + [square] * 2,
            scratch=[pltpu.VMEM((HALO + rows, cols), F32)],
            aliases=aliases,
            macs=count * 6 * rows * rows * cols,
            )
        slot += count

    gh, gl, zh, zl, dh, dl, eh, el, dact, rowtot, sums, payd, pays = call(
        finish_kernel,
        [hid, u, bh, bl, act, outgate, dgate, gn, sk, stat],
        [tall16] * 8
        + [tall, S((rows, 128)), S((8, cols)), S((rows + 16, cols), I16), S((2, rows + 16, cols), I16)],
        scratch=[pltpu.VMEM((3, rows, cols), F32)] + [pltpu.VMEM((rows, cols), F32)] * 2,
        macs=3 * rows * cols * CT,
    )

    *ds, payd = flows(sc, bufs, (eh, el), payd)
    dq = earlier(sc, bufs, ds, bh, bl)
    up = ring_up(pays)
    kept_beside = []

    def step_norm(last):
        ins = [qh, ql, kh, kl, vh, vl, dh, dl, gv, bh, bl, dq]
        kept_beside.append(beside(sc, ins, zh, zl, up_z, ln_gain))
        return kept_beside[0][-1]

    def step_branch(last):
        kept_beside.append(branch_of(after(sc, *up), after(gh, last), gl, down_w))
        return kept_beside[1][0]

    def step_later(slots, payloads, state=None, weight=10, last=()):
        last = last if state else kept_beside[1][:1]
        dv, rh, rl = kept_beside[0][2], kept_beside[0][4], kept_beside[0][5]
        count = len(slots)
        place = pl.BlockSpec((1, rows, cols), lambda i, slots=slots: (pick(slots, i), 0, 0))
        ins = [after(sc, *last), *payloads, bufs[0], bufs[1], rh, rl, vh, vl, gvs]
        ins += state or [dv]
        at = 8 + count
        return call(
            functools.partial(later_kernel, slots),
            ins,
            [tall, tall, S((rows, 128)), S((8, 128))],
            grid=(count,),
            in_specs=[SMEM] + [None] * count + [place, place] + [None] * (len(ins) - count - 3),
            scratch=[pltpu.VMEM((rows, cols), BF16)] * 2,
            aliases={at + k: k for k in range(4)} if state else {at: 1},
            macs=count * 6 * rows * rows * cols,
            weight=weight,
        )

    hop, state, back_runs = gather_later(payd, (step_norm, step_branch, step_later))
    (dq, dk, _, col_here, rh, rl, dn_z), branch = kept_beside
    share = rows // 4

    def second(keep, give, weight):
        return call(
            second_kernel,
            [sc, keep, swapped(give, "head", 1)],
            [S((share, width))] * 2,
            in_specs=[SMEM, None, None],
            weight=weight,
        )

    def join(own, last):
        other = swapped(own, "head", 2)
        parts = [own, swapped(own, "head", 1), other, swapped(other, "head", 1)]
        return call(
            join_kernel,
            [after(sc, last), *parts],
            [S((rows, width), own.dtype)],
            in_specs=[SMEM] + [None] * 4,
            weight=0,
        )[0]

    keep, give = second(*branch, 0)
    result, squares = call(
        result_kernel,
        [sc, keep, swapped(give, "head", 2), stream],
        [S((share, width), BF16), S((1, width // 2))],
        in_specs=[SMEM] + [None] * 3,
        weight=0,
    )

    down = ring_down(after(pays, hop, *state[:1]))
    up2 = ring_up2(up)
    for step, (slots, payloads) in enumerate(back_runs):
        state = step_later(slots, payloads, state, 10)
    e, dv, col_later, flow = state
    (dgates,) = call(
        gate_back_kernel,
        [after(sc, *up2, *down), col_here, col_later, rowtot, gv, flow],
        [S((8, rows))],
        in_specs=[SMEM] + [None] * 5,
        weight=0,
    )
    dgates = sum_over(dgates, "head")
    dm, rim, *kept = by_columns(
        back_kernel,
        [after(sc, result), mixed, dact, dq, dk, e, dv, bh, bl, conv_w, cb, gw, dgates],
        [tall, S((HALO, cols))] + [tall16] * 6 + [tall],
        scratch=[pltpu.VMEM((2 * HALO + rows, CT), F32)],
        macs=30 * rows * cols * CT,
        fixed=(12,),
    )
    down2 = ring_down2(down)
    early = ring_third(up, down, up2, down2)
    rim = lax.ppermute(rim, "seq", [(i + 1, i) for i in range(n - 1)])
    (pack,) = by_columns(
        small_kernel,
        [after(sc, result), mixed, act, kept[6], *kept[:6], qh, ql, kh, kl, vh, vl, dgates, conv_w],
        [S((48, cols))],
        macs=30 * rows * cols * CT,
        fixed=(16,),
        weight=0,
    )
    mh, ml, paym, ux = call(
        send_kernel,
        [dm, rim, after(stat, pack, *down2)],
        [tall16] * 2 + [S((rows + 16, cols), I16), S((8, cols))],
        scratch=[pltpu.VMEM((rows, cols), F32)],
        weight=0,
    )
    up, down = ring_up(paym[None]), ring_down(paym[None])

    keep_early, give_early = wgrad(after(sc, paym), left, (1, 0), [pays] + early)
    got_early = swapped(give_early, "seq", 1)
    keep, give, ln_part = dnorm(
        after(sc, keep_early, *up, *down), mh, ml, up_x, ln_gain, dn_z, stream, stat
    )
    far = after(up + down, keep_early)
    up2, down2 = ring_up2(far[: len(up)]), ring_down2(far[len(up) :])
    late = ring_third(up, down, up2, down2)
    keep, give = second(keep, after(give, *up2, *down2), 0)
    lns = width // cols
    tail = jnp.concatenate([ln_part.reshape(lns, cols), squares])
    tail = sum_over(after(tail, *up2, *down2), "head")
    small = jnp.concatenate([pack, sums, ux[:1], tail])
    small = small + swapped(small, "seq", 1)
    keep_x, give_x = wgrad(after(sc, small, give), left, (0,), [paym[None]] + late)
    got_x = swapped(give_x, "seq", 1)
    (grad_share,) = call(
        norm_back_kernel,
        [after(sc, keep_x), keep, swapped(give, "head", 2), stream, cotangent],
        [S((share, width))],
        in_specs=[SMEM] + [None] * 4,
        weight=0,
    )
    small, bit = after(small, keep_x, grad_share), 2
    while bit < n:
        small = small + swapped(small, "seq", bit)
        bit *= 2
    output = join(result, keep_x)
    grad_stream = join(grad_share, keep_x)
    (grad_down,) = call(
        down_kernel, [after(keep_early, keep_x), got_early], [S((cols, hf))], weight=0
    )
    tail = small[57:]
    grad_ln = tail[:lns].reshape(width)
    rms_pair = jnp.sqrt(tail[lns, :2] / (rows * n * width))
    gain_here = lax.dynamic_slice_in_dim(ln_gain, me * hf, hf, 0)[None]
    (grad_up_z,) = call(
        functools.partial(up_kernel, 1), [keep_early, got_early, gain_here, small[50:51]], [S((hf, cols))], weight=0
    )
    (grad_up_x,) = call(
        functools.partial(up_kernel, 0), [keep_x, got_x, gain_here, small[56:57]], [S((hf, cols))], weight=0
    )
    return (
        output,
        rms_pair,
        grad_stream,
        grad_up_x,
        grad_up_z,
        grad_down,
        grad_ln,
        small[0:kw],
        small[4],
        small[5:17].reshape(3, 4, cols),
        small[17:41].reshape(3, 2 * heads, cols).transpose(1, 0, 2),
        small[41, heads : 2 * heads],
        small[48],
        small[49],
    )


def solution(mesh):
    return jax.shard_map(
        per_device,
        mesh=mesh,
        in_specs=(
            P("seq", None),
            P(),
            P(None, "head"),
            P(None, "head"),
            P(None, "head"),
            P("head"),
            P(None, None, "head"),
            P(None, None, "head"),
            P(),
            P("head"),
            P("head"),
            P("head", None),
            P("seq", None),
            P(),
        ),
        out_specs=(
            P("seq", None),
            P(),
            P("seq", None),
            P("seq", "head"),
            P("seq", "head"),
            P("head", "seq"),
            P(),
            P(None, "head"),
            P("head"),
            P(None, None, "head"),
            P(None, None, "head"),
            P(),
            P("head"),
            P("head"),
        ),
        check_vma=False,
    )
```

```python
import functools
import math

import jax
import jax.numpy as jnp
from jax import lax
from jax.experimental import pallas as pl
from jax.experimental.pallas import tpu as pltpu
from jax.sharding import PartitionSpec as P

EPS = 1e-05
F32, BF16, I16, I32 = jnp.float32, jnp.bfloat16, jnp.int16, jnp.int32
HALO = 16
CT = 256
UNIT = math.log(2.0) / 256.0
NN = (((1,), (0,)), ((), ()))
NT = (((1,), (1,)), ((), ()))
TN = (((0,), (0,)), ((), ()))
SEGS = 4


def iota(shape, dim):
    return lax.broadcasted_iota(I32, shape, dim)


def split(a):
    hi = a.astype(BF16)
    return hi, (a - hi.astype(F32)).astype(BF16)


def mm(a, b, dims):
    return lax.dot_general(a, b, dims, preferred_element_type=F32)


def mm3(a, b, dims):
    return mm(a[0], b[0], dims) + (mm(a[0], b[1], dims) + mm(a[1], b[0], dims))


def to_row(col, width):
    rows = col.shape[0]
    same = iota((rows, width), 0) == iota((rows, width), 1)
    return jnp.sum(jnp.where(same, col, 0.0), axis=0, keepdims=True)


def to_col(row, rows):
    width = row.shape[1]
    same = iota((rows, width), 0) == iota((rows, width), 1)
    return jnp.sum(jnp.where(same, row, 0.0), axis=1, keepdims=True)


def tile(ct):
    return slice(ct * CT, (ct + 1) * CT)


def up(n, to):
    return (n + to - 1) // to * to


def seg_at(first, shape, dim, sc):
    p = first + iota(shape, dim)
    total = jnp.zeros(shape, I32)
    for i in range(SEGS):
        total = total + jnp.where(p >= sc[2 + i], 1, 0)
    return total


def quantize(get, pay, rows, nt, inside):
    amax = jnp.zeros((rows, 1), F32)
    for ct in range(nt):
        amax = jnp.maximum(amax, jnp.max(jnp.abs(get(ct)), axis=1, keepdims=True))
    code = jnp.ceil(jnp.log(jnp.maximum(amax, 1e-30) * (1.0 / 32767.0)) * (1.0 / UNIT))
    inv = jnp.exp(code * (-UNIT))
    for ct in range(nt):
        q = jnp.floor(get(ct) * inv + 0.5)
        q = jnp.minimum(jnp.maximum(q, -32767.0), 32767.0)
        pay[0:rows, tile(ct)] = q.astype(I32).astype(I16)
    width = up(rows, 128)
    codes = jnp.broadcast_to(to_row(code, width), (16, width)).astype(I32)
    if inside:
        old = pay[0:16, 0:width].astype(I32)
        pay[0:16, 0:width] = jnp.where(iota((16, width), 0) == 0, codes, old).astype(I16)
    else:
        pay[rows : rows + 16, :] = jnp.zeros((16, nt * CT), I16)
        pay[rows : rows + 16, 0:width] = codes.astype(I16)


def scales_of(codes, rows):
    row = codes.astype(I32).astype(F32)[0:1, :]
    return jnp.exp(to_col(row, rows) * UNIT)


def conv_masks(base, rows, kw, sc):
    here = seg_at(base, (rows, 1), 0, sc)
    out = []
    for tap in range(kw):
        there = seg_at(base - (kw - 1) + tap, (rows, 1), 0, sc)
        out.append(jnp.where(there == here, 1.0, 0.0))
    return out


def conv_tile(ext, ct, cw, cb, masks):
    kw, rows = len(masks), masks[0].shape[0]
    total = jnp.broadcast_to(cb[:, tile(ct)], (rows, CT))
    for tap in range(kw):
        at = HALO - (kw - 1) + tap
        total = total + cw[tap : tap + 1, tile(ct)] * (ext[at : at + rows, tile(ct)] * masks[tap])
    return total


def sigmoid(v):
    return 1.0 / (1.0 + jnp.exp(-v))


def weight_of(allowed, expo):
    return jnp.where(allowed, jnp.exp(jnp.where(allowed, expo, 0.0)), 0.0)


def call(kernel, ins, outs, grid=(1,), in_specs=None, out_specs=None, scratch=(), aliases=None, macs=0, weight=10):
    def spec_of(spec, a):
        if spec is not None:
            return spec
        zeros = (0,) * len(a.shape)
        return pl.BlockSpec(a.shape, lambda *i: zeros, pipeline_mode=pl.Buffered(1))

    in_specs = [spec_of(s, a) for s, a in zip(in_specs or [None] * len(ins), ins)]
    out_specs = [spec_of(s, a) for s, a in zip(out_specs or [None] * len(outs), outs)]
    size = sum(math.prod(a.shape) * a.dtype.itemsize for a in list(ins) + list(outs))
    base = kernel.func if isinstance(kernel, functools.partial) else kernel
    last = base in (join_kernel, up_kernel, down_kernel)
    need = (20 if lax.axis_size("seq") != 8 else 10 if last else 3) * 1024 * 1024
    need += sum(math.prod(c.shape) * c.dtype.itemsize for c in scratch)
    for spec, a in zip(in_specs + out_specs, list(ins) + list(outs)):
        if spec.block_shape is not None and spec.pipeline_mode is None:
            need += 2 * math.prod(spec.block_shape) * a.dtype.itemsize
    return pl.pallas_call(
        kernel,
        name=base.__name__,
        out_shape=[jax.ShapeDtypeStruct(o.shape, o.dtype) for o in outs],
        grid=grid,
        in_specs=in_specs,
        out_specs=out_specs,
        scratch_shapes=list(scratch),
        input_output_aliases=aliases or {},
        compiler_params=pltpu.CompilerParams(vmem_limit_bytes=need),
        cost_estimate=pl.CostEstimate(
            flops=2 * weight * macs + weight // 10 * 10**9, bytes_accessed=size, transcendentals=0
        ),
    )(*ins)


def S(shape, dtype=F32):
    return jax.ShapeDtypeStruct(shape, dtype)


SMEM = pl.BlockSpec(memory_space=pltpu.SMEM)


def prep_kernel(w, bh, bl):
    for m in range(w.shape[0]):
        for ct in range(w.shape[2] // CT):
            t = w[m, :, tile(ct)]
            r, c = iota((CT, CT), 0), iota((CT, CT), 1)
            group = w.shape[1]
            first = c - lax.rem(c, group)
            out = jnp.zeros((CT, CT), F32)
            for j in range(group):
                out = jnp.where(r == first + j, jnp.broadcast_to(t[j : j + 1, :], (CT, CT)), out)
            hi, lo = split(out)
            bh[m, ct], bl[m, ct] = hi, lo


def proj_kernel(send, x, w, g, *refs):
    out, stat = refs[0], refs[1]
    gc = refs[-1]
    k, last = pl.program_id(0), pl.num_programs(0) - 1
    rows, width = x.shape
    wide = w.shape[1]

    @pl.when(k == 0)
    def _():
        total = jnp.zeros((rows, 1), F32)
        for i in range(width // CT):
            gc[i * CT : (i + 1) * CT, :] = jnp.broadcast_to(to_col(g[:, tile(i)], CT), (CT, 128))
            total = total + jnp.sum(x[:, tile(i)].astype(F32), axis=1, keepdims=True)
        mean = total * (1.0 / width)
        total = jnp.zeros((rows, 1), F32)
        for i in range(width // CT):
            d = x[:, tile(i)].astype(F32) - mean
            total = total + jnp.sum(d * d, axis=1, keepdims=True)
        rstd = lax.rsqrt(total * (1.0 / width) + EPS)
        stat[...] = jnp.where(iota((rows, 128), 1) == 0, mean, rstd)

    acc = jnp.zeros((rows, wide), F32)
    for i in range(width // CT):
        hi, lo = split(w[i * CT : (i + 1) * CT, :] * gc[i * CT : (i + 1) * CT, 0:1])
        xt = x[:, tile(i)]
        acc = acc + (mm(xt, hi, NN) + mm(xt, lo, NN))
    at = pl.ds(pl.multiple_of(k * wide, wide), wide)
    out[:, at] = (acc - stat[:, 0:1] * acc[0:1, :]) * stat[:, 1:2]
    if send:

        @pl.when(k == last)
        def _():
            quantize(lambda ct: out[:, tile(ct)], refs[2], rows, out.shape[1] // CT, True)


def proj(x, w, gain, send):
    rows, width = x.shape
    cols = w.shape[1]
    wide = min(cols, 512)
    outs = [S((rows, cols)), S((rows, 128))] + ([S((rows, cols), I16)] if send else [])
    return call(
        functools.partial(proj_kernel, send),
        [x, w, gain.reshape(1, width)],
        outs,
        grid=(cols // wide,),
        in_specs=[
            pl.BlockSpec((rows, width), lambda k: (0, 0)),
            pl.BlockSpec((width, wide), lambda k: (0, k)),
            pl.BlockSpec((1, width), lambda k: (0, 0)),
        ],
        out_specs=[pl.BlockSpec(o.shape, lambda k: (0, 0)) for o in outs],
        scratch=[pltpu.VMEM((width, 128), F32)],
        macs=2 * rows * width * cols,
    )


def dgated_kernel(g, w, out):
    acc = None
    for i in range(w.shape[1] // CT):
        hi, lo = split(w[:, tile(i)])
        part = mm(g[:, tile(i)], hi, NT) + mm(g[:, tile(i)], lo, NT)
        acc = part if acc is None else acc + part
    out[...] = acc


def dgated(g, w):
    rows, width = g.shape
    cols = w.shape[0]
    wide = min(cols, 512)
    return call(
        dgated_kernel,
        [g, w],
        [S((rows, cols))],
        grid=(cols // wide,),
        in_specs=[
            pl.BlockSpec((rows, width), lambda i: (0, 0)),
            pl.BlockSpec((wide, width), lambda i: (i, 0)),
        ],
        out_specs=[pl.BlockSpec((rows, wide), lambda i: (0, i))],
        macs=2 * rows * width * cols,
    )[0]


def front_kernel(sc, ext, bh, bl, cw, cb, gw, act, qh, ql, kh, kl, vh, vl, ph, pl_, gates):
    rows = act.shape[0]
    nt = act.shape[1] // CT
    masks = conv_masks(sc[0] * rows, rows, cw.shape[0], sc)
    total = jnp.zeros((16, rows), F32)
    for ct in range(nt):
        c = conv_tile(ext, ct, cw, cb, masks)
        a = c * sigmoid(c)
        act[:, tile(ct)] = a
        a2 = split(a)
        m2 = split(ext[HALO : HALO + rows, tile(ct)])
        for m, (src, oh, ol) in enumerate(((a2, qh, ql), (a2, kh, kl), (m2, vh, vl))):
            y = split(mm3(src, (bh[m, ct], bl[m, ct]), NN))
            oh[:, tile(ct)], ol[:, tile(ct)] = y
            total = total + mm3(split(gw[m, :, tile(ct)]), y, NT)
            if m == 0:
                ph[:, tile(ct)], pl_[:, tile(ct)] = split(mm3(y, (bh[1, ct], bl[1, ct]), NT))
    gates[...] = total[0:8, :]


def gate_kernel(sc, parts, bias, out):
    heads = bias.shape[0]
    width = parts.shape[1]
    rows8 = parts[...]
    hd = sc[1]
    r = iota((8, width), 0)
    gi = jnp.sum(jnp.where(r == hd, rows8, 0.0), axis=0, keepdims=True)
    gf = jnp.sum(jnp.where(r == hd + heads, rows8, 0.0), axis=0, keepdims=True)
    b = jnp.float32(0.0)
    for h in range(heads):
        b = jnp.where(hd == h, bias[h], b)
    gf = gf + b
    u = jnp.exp(-jnp.abs(gf))
    w = 1.0 + u
    log1p = jnp.where(w == 1.0, u, jnp.log(w) * (u / jnp.where(w == 1.0, 1.0, w - 1.0)))
    keep = jnp.minimum(gf, 0.0) - log1p
    leave = jnp.where(gf >= 0.0, u, 1.0) / w
    upto = iota((width, width), 1) <= iota((width, width), 0)
    run = to_row(jnp.sum(jnp.where(upto, keep, 0.0), axis=1, keepdims=True), width)
    end = jnp.sum(keep, axis=1, keepdims=True)
    vals = [gi - run + end, run, jnp.broadcast_to(end, (1, width)), leave, gi, gi - run]
    res = jnp.zeros((8, width), F32)
    for i, v in enumerate(vals):
        res = jnp.where(r == i, v, res)
    out[...] = res


def between(gv, me, low, high):
    total = jnp.zeros((1, gv.shape[2]), F32)
    for t in range(1, gv.shape[0]):
        run = jnp.bitwise_xor(me, t)
        total = total + jnp.where((run > low) & (run < high), gv[t, 2:3, :], 0.0)
    return total


def local_kernel(sc, qh, ql, kh, kl, vh, vl, gv, hid):
    rows, cols = hid.shape
    nt = cols // CT
    s = jnp.zeros((rows, rows), F32)
    for ct in range(nt):
        s = s + mm3((qh[:, tile(ct)], ql[:, tile(ct)]), (kh[:, tile(ct)], kl[:, tile(ct)]), NT)
    base = sc[0] * rows
    allowed = (iota((rows, rows), 0) >= iota((rows, rows), 1)) & (
        seg_at(base, (rows, 1), 0, sc) == seg_at(base, (1, rows), 1, sc)
    )
    w = weight_of(allowed, to_col(gv[1:2, :], rows) + gv[5:6, :])
    p = split(s * (1.0 / math.sqrt(cols)) * w)
    for ct in range(nt):
        hid[:, tile(ct)] = mm3(p, (vh[:, tile(ct)], vl[:, tile(ct)]), NN)


def block_kernel(count, slot, flip, *refs):
    sc, pays, refs = refs[0], refs[1 : 1 + count], refs[1 + count :]
    ph, pl_, gv, cw, cb = refs[:5]
    u_in = refs[5] if slot else None
    u, ah, al, mh, ml, ps, ws, ext = refs[-8:]
    rows, cols = u.shape
    nt = cols // CT
    i = pl.program_id(0)
    me, src = sc[0], sc[6 + slot + i]
    long = HALO + rows

    @pl.when(i == 0)
    def _():
        u[...] = u_in[...] if slot else jnp.zeros_like(u)

    for b, pay in enumerate(pays):

        place = jnp.where(me // 2 == 2, 3 - b, b) if flip and b else b

        @pl.when((i == place) & (src != me))
        def _(pay=pay):
            scale = scales_of(pay[0:16, 0 : up(long, 128)], long)
            for ct in range(nt):
                ext[:, tile(ct)] = pay[:, tile(ct)].astype(I32).astype(F32) * scale

    @pl.when(src != me)
    def _():
        masks = conv_masks(src * rows, rows, cw.shape[0], sc)
        for ct in range(nt):
            c = conv_tile(ext, ct, cw, cb, masks)
            ah[0, :, tile(ct)], al[0, :, tile(ct)] = split(c * sigmoid(c))

    @pl.when(src < me)
    def _():
        s = jnp.zeros((rows, rows), F32)
        for ct in range(nt):
            t = tile(ct)
            mh[0, :, t], ml[0, :, t] = split(ext[HALO:long, t])
            s = s + mm3((ph[:, t], pl_[:, t]), (ah[0, :, t], al[0, :, t]), NT)
        w = pair_weight(sc, gv, me, src, rows) * (1.0 / math.sqrt(cols))
        s = s * w
        ws[0], ps[0] = w, s
        p = split(s)
        for ct in range(nt):
            t = tile(ct)
            u[:, t] += mm3(p, (mh[0, :, t], ml[0, :, t]), NN)


def pair_weight(sc, gv, me, src, rows):
    allowed = seg_at(me * rows, (rows, 1), 0, sc) == seg_at(src * rows, (1, rows), 1, sc)
    row = between(gv, me, src, me) + gv[jnp.bitwise_xor(me, src), 0:1, :]
    return weight_of(allowed, to_col(gv[0, 1:2, :], rows) + row)


def finish_kernel(hid_in, u, bh, bl, act, z, dg, gn, sk, st, gh, gl, zh, zl, dh, dl, eh, el, dact, rowtot, sums, payd, pays, buf, norm, hid):
    rows, cols = hid.shape
    nt = cols // CT
    total = jnp.zeros((rows, 1), F32)
    for ct in range(nt):
        t = tile(ct)
        h = hid_in[:, t] + mm3(split(u[:, t]), (bh[2, ct], bl[2, ct]), NN)
        hid[:, t] = h
        total = total + jnp.sum(h, axis=1, keepdims=True)
    mean = total * (1.0 / cols)
    total = jnp.zeros((rows, 1), F32)
    for ct in range(nt):
        d = hid[:, tile(ct)] - mean
        total = total + jnp.sum(d * d, axis=1, keepdims=True)
    rstd = lax.rsqrt(total * (1.0 / cols) + EPS)
    m1 = jnp.zeros((rows, 1), F32)
    m2 = jnp.zeros((rows, 1), F32)
    xm, xr = st[HALO : HALO + rows, 0:1], st[HALO : HALO + rows, 1:2]
    r8 = iota((8, CT), 0)
    for ct in range(nt):
        t = tile(ct)
        n = (hid[:, t] - mean) * rstd
        a = act[:, t]
        full = n * gn[:, t] + sk[:, t] * a
        zz = z[HALO : HALO + rows, t]
        sg = sigmoid(zz)
        gate = zz * sg
        gated = full * gate
        buf[0, :, t] = gated
        gh[:, t], gl[:, t] = split(gated)
        dgt = dg[:, t]
        da = dgt * gate
        dz = dgt * full * (sg * (1.0 + zz * (1.0 - sg)))
        zh[:, t], zl[:, t] = split(dz)
        dzr = dz * xr
        buf[1, :, t] = dzr
        dact[:, t] = da * sk[:, t]
        dn = da * gn[:, t]
        buf[2, :, t] = dn
        norm[:, t] = n
        m1 = m1 + jnp.sum(dn, axis=1, keepdims=True)
        m2 = m2 + jnp.sum(dn * n, axis=1, keepdims=True)
        s0 = jnp.sum(da * n, axis=0, keepdims=True)
        s1 = jnp.sum(da * a, axis=0, keepdims=True)
        s2 = jnp.sum(dzr * xm, axis=0, keepdims=True)
        sums[:, t] = jnp.where(r8 == 0, s0, jnp.where(r8 == 1, s1, jnp.where(r8 == 2, s2, 0.0)))
    m1, m2 = m1 * (1.0 / cols), m2 * (1.0 / cols)
    total = jnp.zeros((rows, 1), F32)
    for ct in range(nt):
        t = tile(ct)
        d = rstd * (buf[2, :, t] - m1 - norm[:, t] * m2)
        buf[2, :, t] = d
        d2 = split(d)
        dh[:, t], dl[:, t] = d2
        eh[:, t], el[:, t] = split(mm3(d2, (bh[2, ct], bl[2, ct]), NT))
        total = total + jnp.sum(d * hid[:, t], axis=1, keepdims=True)
    rowtot[...] = jnp.broadcast_to(total, rowtot.shape)
    quantize(lambda ct: buf[2, :, tile(ct)], payd, rows, nt, False)
    quantize(lambda ct: buf[0, :, tile(ct)], pays.at[0], rows, nt, False)
    quantize(lambda ct: buf[1, :, tile(ct)], pays.at[1], rows, nt, False)


def part_rows(a, buf, sc, keep, give):
    buf[...] = a
    q = a.shape[0] // 4
    mine = lax.rem(sc[1], 2)
    for half in range(2):
        at = pl.multiple_of(half * 2 * q + mine * q, q)
        keep[half * q : half * q + q, :] = buf[pl.ds(at, q), :]
        at = pl.multiple_of(half * 2 * q + (1 - mine) * q, q)
        give[half * q : half * q + q, :] = buf[pl.ds(at, q), :]


def branch_kernel(sc, gh, gl, w, keep, give, buf):
    acc = None
    for i in range(w.shape[0] // CT):
        part = mm3((gh[:, tile(i)], gl[:, tile(i)]), split(w[i * CT : (i + 1) * CT, :]), NN)
        acc = part if acc is None else acc + part
    part_rows(acc, buf, sc, keep, give)


def branch_of(sc, gh, gl, w):
    rows, cols = gh.shape
    width = w.shape[1]
    wide = 512
    half = pl.BlockSpec((rows // 2, wide), lambda i: (0, i))
    return call(
        branch_kernel,
        [sc, gh, gl, w],
        [S((rows // 2, width))] * 2,
        grid=(width // wide,),
        in_specs=[SMEM, None, None, pl.BlockSpec((cols, wide), lambda i: (0, i))],
        out_specs=[half, half],
        scratch=[pltpu.VMEM((rows, wide), F32)],
        macs=3 * rows * width * cols,
    )


def result_kernel(sc, a, b, x, out, squares):
    q = out.shape[0]
    branch = a[...] + b[...]
    result = x[pl.ds(pl.multiple_of(sc[1] * q, q), q), :].astype(F32) + branch
    out[...] = result.astype(BF16)
    r2 = jnp.sum(jnp.sum(result * result, axis=1, keepdims=True), axis=0, keepdims=True)
    b2 = jnp.sum(jnp.sum(branch * branch, axis=1, keepdims=True), axis=0, keepdims=True)
    lane = iota(squares.shape, 1)
    squares[...] = jnp.where(lane == 0, r2, jnp.where(lane == 1, b2, 0.0))


def local_back(sc, qh, ql, kh, kl, vh, vl, dh, dl, gv, bh, bl, dq_in, dq, dk, dv, col, rh, rl):
    rows, cols = dq.shape
    nt = cols // CT
    st = jnp.zeros((rows, rows), F32)
    dpt = jnp.zeros((rows, rows), F32)
    for ct in range(nt):
        t = tile(ct)
        st = st + mm3((kh[:, t], kl[:, t]), (qh[:, t], ql[:, t]), NT)
        dpt = dpt + mm3((vh[:, t], vl[:, t]), (dh[:, t], dl[:, t]), NT)
        rh[:, t], rl[:, t] = split(mm3((kh[:, t], kl[:, t]), (bh[0, ct], bl[0, ct]), NT))
    base = sc[0] * rows
    allowed = (iota((rows, rows), 1) >= iota((rows, rows), 0)) & (
        seg_at(base, (rows, 1), 0, sc) == seg_at(base, (1, rows), 1, sc)
    )
    w = weight_of(allowed, gv[1:2, :] + to_col(gv[5:6, :], rows))
    scaled = w * (1.0 / math.sqrt(cols))
    pt = st * scaled
    dst = dpt * scaled
    col[...] = jnp.broadcast_to(jnp.sum(dpt * pt, axis=1, keepdims=True), col.shape)
    pt2, dst2, ds2 = split(pt), split(dst), split(dst.T)
    for ct in range(nt):
        t = tile(ct)
        dv[:, t] = mm3(pt2, (dh[:, t], dl[:, t]), NN)
        dk[:, t] = mm3(dst2, (qh[:, t], ql[:, t]), NN)
        dq[:, t] = dq_in[:, t] + mm3(ds2, (kh[:, t], kl[:, t]), NN)


def flow_kernel(sc, mh, ml, ps, ws, eh, el, pay_in, dsh, dsl, pay, vec):
    rows = eh.shape[0]
    nt = eh.shape[1] // CT
    i, last = pl.program_id(0), pl.num_programs(0) - 1
    me, src = sc[0], sc[6 + i]

    @pl.when(i == 0)
    def _():
        vec[...] = jnp.zeros_like(vec)

    @pl.when(src < me)
    def _():
        dp = jnp.zeros((rows, rows), F32)
        for ct in range(nt):
            t = tile(ct)
            dp = dp + mm3((eh[:, t], el[:, t]), (mh[0, :, t], ml[0, :, t]), NT)
        dsh[0], dsl[0] = split(dp * ws[0])
        flow = jnp.sum(dp * ps[0], axis=0, keepdims=True)
        flow = jnp.sum(flow, axis=1, keepdims=True)
        lane = iota(vec.shape, 1)
        vec[...] += jnp.where((lane > src) & (lane < me), flow, 0.0)

    @pl.when(i == last)
    def _():
        v = vec[0:1, :]
        top = jnp.maximum(jnp.max(jnp.abs(v), axis=1, keepdims=True), 1e-30)
        code = jnp.ceil(jnp.log(top * (1.0 / 32000.0)) * (1.0 / UNIT))
        v = v * jnp.exp(code * (-UNIT))
        whole = jnp.floor(v)
        digits = [whole, jnp.floor((v - whole) * 32767.0 + 0.5), jnp.broadcast_to(code, v.shape)]
        r = iota((16, 128), 0)
        out = pay_in[:, 0:128].astype(I32)
        for k, d in enumerate(digits):
            out = jnp.where(r == k + 1, d.astype(I32), out)
        pay[...] = pay_in[...]
        pay[:, 0:128] = out.astype(I16)


def flows(sc, bufs, e2, pay):
    mh, ml, ps, ws = bufs[2:]
    slots, rows, cols = mh.shape
    moving = pl.BlockSpec((1, rows, cols), lambda i: (i, 0, 0))
    square = pl.BlockSpec((1, rows, rows), lambda i: (i, 0, 0))
    codes = pl.BlockSpec((16, cols), lambda i: (rows // 16, 0))
    return call(
        flow_kernel,
        [sc, mh, ml, ps, ws, *e2, pay],
        [S((slots, rows, rows), BF16)] * 2 + [pay],
        grid=(slots,),
        in_specs=[SMEM] + [moving] * 2 + [square] * 2 + [None] * 2 + [codes],
        out_specs=[square, square, codes],
        scratch=[pltpu.VMEM((8, 128), F32)],
        aliases={7: 2},
        weight=0,
        macs=slots * 3 * rows * rows * cols // 2,
    )


def earlier_kernel(sc, ah, al, dsh, dsl, bh, bl, dq, acc):
    nt = dq.shape[1] // CT
    i, last = pl.program_id(0), pl.num_programs(0) - 1

    @pl.when(i == 0)
    def _():
        acc[...] = jnp.zeros_like(acc)

    @pl.when(sc[6 + i] < sc[0])
    def _():
        ds = (dsh[0], dsl[0])
        for ct in range(nt):
            t = tile(ct)
            acc[:, t] += mm3(ds, (ah[0, :, t], al[0, :, t]), NN)

    @pl.when(i == last)
    def _():
        for ct in range(nt):
            t = tile(ct)
            dq[:, t] = mm3(split(acc[:, t]), (bh[1, ct], bl[1, ct]), NN)


def earlier(sc, bufs, ds, bh, bl):
    slots, rows, cols = bufs[0].shape
    moving = pl.BlockSpec((1, rows, cols), lambda i: (i, 0, 0))
    square = pl.BlockSpec((1, rows, rows), lambda i: (i, 0, 0))
    return call(
        earlier_kernel,
        [sc, *bufs[:2], *ds, bh, bl],
        [S((rows, cols))],
        grid=(slots,),
        in_specs=[SMEM] + [moving] * 2 + [square] * 2 + [None] * 2,
        scratch=[pltpu.VMEM((rows, cols), F32)],
        weight=0,
        macs=slots * 3 * rows * rows * cols // 2,
    )[0]


def pick(slots, i):
    out = slots[0]
    for b, slot in enumerate(slots[1:]):
        out = jnp.where(i == b + 1, slot, out)
    return out


def later_kernel(slots, *refs):
    count = len(slots)
    sc, pays, refs = refs[0], refs[1 : 1 + count], refs[1 + count :]
    ah, al, rh, rl, vh, vl, gv = refs[:7]
    e_in, dv_in, col_in, flow_in = refs[7:11] if len(refs) == 17 else (None, refs[7], None, None)
    e, dv, col, flow, ph, pl_ = refs[-6:]
    rows, cols = e.shape
    nt = cols // CT
    i = pl.program_id(0)
    me, src = sc[0], sc[6 + pick(slots, i)]

    @pl.when(i == 0)
    def _():
        e[...] = jnp.zeros_like(e) if e_in is None else e_in[...]
        dv[...] = dv_in[...]
        col[...] = jnp.zeros_like(col) if col_in is None else col_in[...]
        flow[...] = jnp.zeros_like(flow) if flow_in is None else flow_in[...]

    for b, pay in enumerate(pays):

        @pl.when((src > me) & (i == b))
        def _(pay=pay):
            scale = scales_of(pay[rows : rows + 16, 0:rows], rows)
            for ct in range(nt):
                t = tile(ct)
                ph[:, t], pl_[:, t] = split(pay[0:rows, t].astype(I32).astype(F32) * scale)
            d = pay[rows : rows + 16, 0:128].astype(I32).astype(F32)
            v = (d[1:2, :] + d[2:3, :] * (1.0 / 32767.0)) * jnp.exp(d[3:4, :] * UNIT)
            v = jnp.where(iota((1, 128), 1) == me, v, 0.0)
            flow[...] += jnp.sum(v, axis=1, keepdims=True)

    @pl.when(src > me)
    def _():
        st = jnp.zeros((rows, rows), F32)
        dpt = jnp.zeros((rows, rows), F32)
        for ct in range(nt):
            t = tile(ct)
            st = st + mm3((rh[:, t], rl[:, t]), (ah[0, :, t], al[0, :, t]), NT)
            dpt = dpt + mm3((vh[:, t], vl[:, t]), (ph[:, t], pl_[:, t]), NT)
        allowed = seg_at(me * rows, (rows, 1), 0, sc) == seg_at(src * rows, (1, rows), 1, sc)
        row = between(gv, me, me, src) + gv[jnp.bitwise_xor(me, src), 1:2, :]
        w = weight_of(allowed, to_col(gv[0, 0:1, :], rows) + row)
        scaled = w * (1.0 / math.sqrt(cols))
        pt = st * scaled
        col[...] += jnp.sum(dpt * pt, axis=1, keepdims=True)
        pt2, dst2 = split(pt), split(dpt * scaled)
        for ct in range(nt):
            t = tile(ct)
            dv[:, t] += mm3(pt2, (ph[:, t], pl_[:, t]), NN)
            e[:, t] += mm3(dst2, (ah[0, :, t], al[0, :, t]), NN)


def gate_back_kernel(sc, col_here, col_later, rowtot, gv, flow, out):
    rows = rowtot.shape[0]
    here, later = col_here[:, 0:1], col_later[:, 0:1]
    t, p = iota((rows, rows), 1), iota((rows, rows), 0)
    val = to_row(rowtot[:, 0:1] - here, rows)
    dlk = jnp.sum(jnp.where(t >= p, val, 0.0), axis=1, keepdims=True)
    dlk = dlk + jnp.sum(jnp.where(t < p, to_row(later, rows), 0.0), axis=1, keepdims=True)
    dlk = dlk + flow[0:1, 0:1]
    r = iota((8, rows), 0)
    d_in = to_row(here + later, rows)
    d_f = to_row(dlk, rows) * gv[3:4, :]
    out[...] = jnp.where(r == sc[1], d_in, jnp.where(r == sc[1] + out.shape[0] // 2, d_f, 0.0))


def back_kernel(sc, ext, dact, dq, dk, e, dv, bh, bl, cw, cb, gw, dg, dm, rim, d0h, d0l, d1h, d1l, d2h, d2l, dco, dcs):
    rows = dq.shape[0]
    kw = cw.shape[0]
    base = sc[0] * rows
    masks = conv_masks(base, rows, kw, sc)
    long = HALO + rows
    here = seg_at(base - HALO, (long, 1), 0, sc)
    back_masks = []
    for tap in range(kw):
        there = seg_at(base - HALO + kw - 1 - tap, (long, 1), 0, sc)
        back_masks.append(jnp.where(there == here, 1.0, 0.0))
    g2 = split(jnp.concatenate([dg[...], jnp.zeros((8, rows), F32)], axis=0))
    dcs[0:HALO, :] = jnp.zeros((HALO, CT), F32)
    dcs[long : HALO + long, :] = jnp.zeros((HALO, CT), F32)
    dk_all = dk[...] + mm3(split(e[...]), (bh[0, 0], bl[0, 0]), NN)
    grads = (dq[...], dk_all, dv[...])
    kept = ((d0h, d0l), (d1h, d1l), (d2h, d2l))
    back = []
    for m in range(3):
        d2 = split(grads[m] + mm3(g2, split(gw[m]), TN))
        kept[m][0][...], kept[m][1][...] = d2
        back.append(mm3(d2, (bh[m, 0], bl[m, 0]), NT))
    c = conv_tile(ext, 0, cw, cb, masks)
    sg = sigmoid(c)
    dc = (dact[...] + back[0] + back[1]) * (sg * (1.0 + c * (1.0 - sg)))
    dco[...] = dc
    dcs[HALO:long, :] = dc
    dext = jnp.zeros((long, CT), F32)
    for tap in range(kw):
        at = kw - 1 - tap
        dext = dext + cw[tap : tap + 1, :] * (dcs[at : at + long, :] * back_masks[tap])
    rim[...] = dext[0:HALO, :]
    dm[...] = dext[HALO:, :] + back[2]


def small_kernel(sc, ext, act, dc, d0h, d0l, d1h, d1l, d2h, d2l, qh, ql, kh, kl, vh, vl, dg, cw, pack):
    rows = act.shape[0]
    kw = cw.shape[0]
    masks = conv_masks(sc[0] * rows, rows, kw, sc)
    long = HALO + rows
    g = jnp.concatenate([dg[...], jnp.zeros((8, rows), F32)], axis=0)
    g2 = split(g)
    pack[...] = jnp.zeros_like(pack)
    pack[41:42, 0:128] = to_row(jnp.sum(g, axis=1, keepdims=True), 128)
    group = 4
    sub, lane = iota((CT, CT), 0), iota((CT, CT), 1)
    diagonal = (sub - lax.rem(sub, group)) == (lane - lax.rem(lane, group))
    a2 = split(act[...])
    m2 = split(ext[HALO:long, :])
    grads = ((d0h, d0l), (d1h, d1l), (d2h, d2l))
    stored = ((qh, ql), (kh, kl), (vh, vl))
    for m in range(3):
        gate_rows = mm3(g2, (stored[m][0][...], stored[m][1][...]), NN)
        pack[17 + 8 * m : 25 + 8 * m, :] = gate_rows[0:8, :]
        d2 = (grads[m][0][...], grads[m][1][...])
        outer = jnp.where(diagonal, mm3(a2 if m < 2 else m2, d2, TN), 0.0)
        eight = outer[0:8, :]
        for r in range(1, CT // 8):
            eight = eight + outer[8 * r : 8 * r + 8, :]
        pack[5 + group * m : 5 + group * (m + 1), :] = eight[0:4, :] + eight[4:8, :]
    d = dc[...]
    pack[4:5, :] = jnp.sum(d, axis=0, keepdims=True)
    for tap in range(kw):
        at = HALO - (kw - 1) + tap
        pack[tap : tap + 1, :] = jnp.sum(d * (ext[at : at + rows, :] * masks[tap]), axis=0, keepdims=True)


def by_columns(kernel, ins, outs, scratch=(), macs=0, fixed=(), weight=10):
    def spec(a, index=None):
        if index == 0:
            return SMEM
        if index in fixed:
            return None
        if len(a.shape) == 2:
            return pl.BlockSpec((a.shape[0], CT), lambda i: (0, i))
        if len(a.shape) == 3:
            return pl.BlockSpec((a.shape[0], a.shape[1], CT), lambda i: (0, 0, i))
        return pl.BlockSpec((a.shape[0], 1, CT, CT), lambda i: (0, i, 0, 0))

    return call(
        kernel,
        ins,
        outs,
        grid=(outs[0].shape[1] // CT,),
        in_specs=[spec(a, k) for k, a in enumerate(ins)],
        out_specs=[spec(o) for o in outs],
        scratch=scratch,
        macs=macs,
        weight=weight,
    )


def send_kernel(dm, rim, st, mh, ml, pay, ux, buf):
    rows, cols = dm.shape
    nt = cols // CT
    xm, xr = st[HALO : HALO + rows, 0:1], st[HALO : HALO + rows, 1:2]
    for ct in range(nt):
        t = tile(ct)
        buf[:, t] = dm[:, t]
        buf[rows - HALO : rows, t] = dm[rows - HALO : rows, t] + rim[:, t]
        d = buf[:, t]
        mh[:, t], ml[:, t] = split(d)
        d = d * xr
        buf[:, t] = d
        ux[:, t] = jnp.broadcast_to(jnp.sum(d * xm, axis=0, keepdims=True), (8, CT))
    quantize(lambda ct: buf[:, tile(ct)], pay, rows, nt, False)


def beside_kernel(sc, *refs):
    ins, (zh, zl, w, g), outs, out = refs[:12], refs[12:16], refs[16:22], refs[22]

    @pl.when(pl.program_id(0) == 0)
    def _():
        local_back(sc, *ins, *outs)

    out[...] = mm3((zh[...], zl[...]), split(w[...] * to_col(g[0], CT)), NT)


def beside(sc, locals_in, zh, zl, w, gain):
    rows, cols = zh.shape
    width = w.shape[0]
    return call(
        beside_kernel,
        [sc, *locals_in, zh, zl, w, gain.reshape(width // CT, 1, CT)],
        [S((rows, cols))] * 3 + [S((rows, 128))] + [S((rows, cols), BF16)] * 2 + [S((rows, width))],
        grid=(width // CT,),
        in_specs=[SMEM]
        + [None] * 14
        + [pl.BlockSpec((CT, cols), lambda i: (i, 0)), pl.BlockSpec((1, 1, CT), lambda i: (i, 0, 0))],
        out_specs=[None] * 6 + [pl.BlockSpec((rows, CT), lambda i: (0, i))],
        macs=3 * rows * width * cols,
        weight=10,
    )


def dnorm_kernel(sc, ah, al, w, g, other, x, st, keep, give, ln, buf):
    a = other[...] + mm3((ah[...], al[...]), split(w[...] * to_col(g[0], CT)), NT)
    part_rows(a, buf, sc, keep, give)
    rows = a.shape[0]
    xhat = (x[...].astype(F32) - st[HALO : HALO + rows, 0:1]) * st[HALO : HALO + rows, 1:2]
    ln[0] = jnp.sum(a * xhat, axis=0, keepdims=True) / g[0]


def dnorm(sc, ah, al, w, gain, other, x, st):
    rows, cols = ah.shape
    width = w.shape[0]
    gspec = pl.BlockSpec((1, 1, CT), lambda i: (i, 0, 0))
    wide = pl.BlockSpec((rows, CT), lambda i: (0, i))
    half = pl.BlockSpec((rows // 2, CT), lambda i: (0, i))
    return call(
        dnorm_kernel,
        [sc, ah, al, w, gain.reshape(width // CT, 1, CT), other, x, st],
        [S((rows // 2, width)), S((rows // 2, width)), S((width // CT, 1, CT))],
        grid=(width // CT,),
        in_specs=[SMEM, None, None, pl.BlockSpec((CT, cols), lambda i: (i, 0)), gspec, wide, wide, None],
        out_specs=[half, half, gspec],
        scratch=[pltpu.VMEM((rows, CT), F32)],
        macs=3 * rows * width * cols,
    )


def second_kernel(sc, a, b, keep, give):
    q = keep.shape[0]
    mine = sc[1] // 2
    at = pl.multiple_of(mine * q, q)
    keep[...] = a[pl.ds(at, q), :] + b[pl.ds(at, q), :]
    at = pl.multiple_of((1 - mine) * q, q)
    give[...] = a[pl.ds(at, q), :] + b[pl.ds(at, q), :]


def norm_back_kernel(sc, a, b, x, g, out):
    q, width = out.shape
    at = pl.multiple_of(sc[1] * q, q)
    xs = x[pl.ds(at, q), :].astype(F32)
    dn = a[...] + b[...]
    c = xs - jnp.mean(xs, axis=1, keepdims=True)
    rstd = lax.rsqrt(jnp.mean(c * c, axis=1, keepdims=True) + EPS)
    xhat = c * rstd
    m1 = jnp.mean(dn, axis=1, keepdims=True)
    m2 = jnp.mean(dn * xhat, axis=1, keepdims=True)
    out[...] = g[pl.ds(at, q), :].astype(F32) + rstd * (dn - m1 - xhat * m2)


def left_kernel(sc, x, g, *outs):
    m = len(outs)
    wide = outs[0].shape[1]
    ring, kind = sc[0] // 2, lax.rem(sc[1], 2)
    for s, out in enumerate(outs):
        cols = pl.ds(pl.multiple_of(lax.rem(ring - s + m, m) * wide, wide), wide)

        @pl.when(kind == 0)
        def _(out=out, cols=cols):
            out[...] = x[:, cols]

        @pl.when(kind == 1)
        def _(out=out, cols=cols):
            out[...] = g[:, cols]


def join_kernel(sc, own, a, b, c, out):
    q = own.shape[0]
    for bits, part in enumerate((own, a, b, c)):
        at = pl.multiple_of(jnp.bitwise_xor(sc[1], bits) * q, q)
        out[pl.ds(at, q), :] = part[...]


def wgrad_kernel(m, kinds, sc, *refs):
    parts, refs = refs[:2], refs[2:]
    count = len(refs) // 2 - 2
    pays, codes = refs[:count], refs[count : 2 * count]
    keep, pay, buf, left, scale = refs[2 * count :]
    rows, hf = left.shape[3:]
    kind = pick(kinds, pl.program_id(0))
    ct, last = pl.program_id(1), pl.num_programs(1) - 1
    odd = lax.rem(sc[0], 2)
    ring = sc[0] // 2
    mine, other = left.at[kind, odd], left.at[kind, 1 - odd]

    @pl.when((pl.program_id(0) == 0) & (ct == 0))
    def _():
        for bits, part in enumerate(parts):
            at = jnp.bitwise_xor(lax.rem(sc[1], 2), bits)
            for half in range(2):
                left[at, half] = part[:, :, half * hf : (half + 1) * hf]

    def slots(refs):
        every = [r[0].astype(I32) for r in refs]
        if m != 4:
            return every
        own, down1, up1, down2, up2, three = every
        far = jnp.where(ring == m - 1, three, 0)
        near = jnp.where(ring == 0, three, 0)
        return [own, down1 + far, down2 + up2, up1 + near]

    @pl.when(ct == 0)
    def _():
        for s, c in enumerate(slots(codes)):
            col = jnp.exp(to_col(c.astype(F32)[0:1, :], rows) * UNIT)
            scale[s] = jnp.broadcast_to(col, (rows, 128))

    a = jnp.zeros((hf, CT), F32)
    b = jnp.zeros((hf, CT), F32)
    for s, q in enumerate(slots(pays)):
        hi, lo = split(q.astype(F32) * scale[s][:, 0:1])
        a = a + (mm(mine[s], hi, TN) + mm(mine[s], lo, TN))
        b = b + (mm(other[s], hi, TN) + mm(other[s], lo, TN))
    keep[0] = a
    buf[:, pl.ds(pl.multiple_of(ct * CT, CT), CT)] = b

    @pl.when(ct == last)
    def _():
        quantize(lambda c: buf[:, tile(c)], pay.at[0], hf, buf.shape[1] // CT, False)


def wgrad(sc, left, kinds, pays):
    m, rows, hf = left[0].shape
    hf = hf // 2
    cols = pays[0].shape[2]
    count = len(kinds)
    return call(
        functools.partial(wgrad_kernel, m, kinds),
        [sc, *left, *pays, *pays],
        [S((count, hf, cols)), S((count, hf + 16, cols), I16)],
        grid=(count, cols // CT),
        in_specs=[SMEM] + [None] * 2
        + [pl.BlockSpec((1, rows, CT), lambda p, i: (p, 0, i))] * len(pays)
        + [pl.BlockSpec((1, 16, rows), lambda p, i: (p, rows // 16, 0))] * len(pays),
        out_specs=[
            pl.BlockSpec((1, hf, CT), lambda p, i: (p, 0, i)),
            pl.BlockSpec((1, hf + 16, cols), lambda p, i: (p, 0, 0)),
        ],
        scratch=[pltpu.VMEM((hf, cols), F32), pltpu.VMEM((2, 2, m, rows, hf), BF16), pltpu.VMEM((m, rows, 128), F32)],
        macs=4 * count * m * hf * rows * cols,
    )


def received(pay, ct, rows):
    return pay[0:rows, tile(ct)].astype(I32).astype(F32)


def down_kernel(keep, pay, out):
    rows, cols = keep.shape[1:]
    scale = scales_of(pay[0, rows : rows + 16, 0 : up(rows, 128)], rows)
    for ct in range(cols // CT):
        t = keep[0, :, tile(ct)] + received(pay.at[0], ct, rows) * scale
        out[tile(ct), :] = t.T


def up_kernel(which, keep, pay, gain, u, out):
    rows, cols = out.shape
    scale = scales_of(pay[which, rows : rows + 16, 0 : up(rows, 128)], rows)
    g = to_col(gain[...], rows)
    for ct in range(cols // CT):
        t = keep[which, :, tile(ct)] + received(pay.at[which], ct, rows) * scale
        out[:, tile(ct)] = g * (t - u[:, tile(ct)])


def shifted(a, by):
    n = lax.axis_size("seq")
    return lax.ppermute(a, "seq", [(i, (i + by) % n) for i in range(n)])


def swapped(a, axis, bit):
    n = lax.axis_size(axis)
    return lax.ppermute(a, axis, [(i, i ^ bit) for i in range(n)])


def sum_over(a, axis):
    bit = 1
    while bit < lax.axis_size(axis):
        a = a + swapped(a, axis, bit)
        bit *= 2
    return a


def moved(a, pairs):
    return lax.ppermute(a, "seq", pairs)


def gather_runs(pay):
    n = lax.axis_size("seq")
    if n != 8:
        return [[shifted(pay, s) for s in range(1, n)]]
    z = lax.axis_index("seq") // 2
    step_up, step_down = [(i, i + 2) for i in range(6)], [(i + 2, i) for i in range(6)]
    up1, down1 = moved(pay, step_up), moved(pay, step_down)
    x = swapped(pay, "seq", 1)
    up2 = moved(jnp.where(z == 0, x, up1), step_up)
    down2 = moved(jnp.where(z == 3, x, down1), step_down)
    side = swapped(jnp.where(z < 2, down1, up1), "seq", 1)
    far = jnp.where(z < 2, down2, up2)
    three = moved(far, [(2, 0), (3, 1), (4, 6), (5, 7)])
    side2 = swapped(far, "seq", 1)
    side3 = moved(three, [(0, 1), (1, 0), (6, 7), (7, 6)])
    return [[x, up1, down1], [up2, down2, side], [side2, three], [side3, side3]]


def gather_later(pay, steps):
    n = lax.axis_size("seq")
    if n != 8:
        last = pay
        for step in steps[:2]:
            last = step(last)
        return [last], [], [(list(range(n - 1)), [shifted(pay, s) for s in range(1, n)])]
    one = moved(pay, [(i, i - 2) for i in range(2, 8)])
    x = moved(pay, [(i, i - 1) for i in range(1, 8, 2)])
    done = steps[0](pay)
    two = moved(after(one, done), [(i, i - 2) for i in range(2, 6)])
    x_one = moved(after(one, done), [(i, i ^ 1) for i in range(6)])
    done = steps[1](done)
    three = moved(after(two, done), [(i, i - 2) for i in range(2, 4)])
    x_two = moved(after(two, done), [(i, i ^ 1) for i in range(4)])
    state = steps[2]([0, 2], [x, one])
    x_three = moved(after(three, state[0]), [(0, 1), (1, 0)])
    return [two, x], state, [([5, 4], [x_one, two]), ([6, 7, 8], [x_two, three, x_three])]


def gather_xor(a):
    a = a[None]
    bit = 1
    while bit < lax.axis_size("seq"):
        a = jnp.concatenate([a, swapped(a, "seq", bit)])
        bit *= 2
    return a


def sources(me, n):
    if n != 8:
        return [lax.rem(me - s + n, n) for s in range(1, n)]
    z, x = me // 2, lax.rem(me, 2)

    def run(ring, other):
        return ring * 2 + (1 - x if other else x)

    up2 = jnp.where(z == 1, run(0, True), run(z - 2, False))
    return [
        run(z, True),
        jnp.where(z > 0, run(z - 1, False), me),
        jnp.where(z < 3, run(z + 1, False), me),
        jnp.where(z > 0, up2, me),
        jnp.where(z == 2, run(1, True), jnp.where(z < 3, run(z + 2, False), me)),
        jnp.where(z == 2, run(3, True), run(jnp.where(z < 2, z + 1, z - 1), True)),
        run(jnp.where(z < 2, z + 2, z - 2), True),
        jnp.where(z == 0, run(3, False), jnp.where(z == 3, run(0, False), me)),
        jnp.where(z == 0, run(3, True), jnp.where(z == 3, run(0, True), me)),
        me,
    ]


def ring_up(pay):
    m = lax.axis_size("seq") // 2
    if m != 4:
        return [shifted(pay, -2 * s) for s in range(1, m)]
    return [moved(pay, [(i, i + 2) for i in range(6)])]


def ring_down(pay):
    if lax.axis_size("seq") != 8:
        return []
    return [moved(pay, [(i + 2, i) for i in range(6)])]


def ring_up2(up):
    return [moved(a, [(i, i + 2) for i in range(2, 6)]) for a in up] if lax.axis_size("seq") == 8 else []


def ring_down2(down):
    return [moved(a, [(i, i - 2) for i in range(2, 6)]) for a in down]


def ring_third(up, down, up2, down2):
    last = [moved(b + a, [(2, 0), (3, 1), (4, 6), (5, 7)]) for a, b in zip(up2, down2)]
    return down + up + down2 + up2 + last


def after(array, *others):
    if isinstance(array, list):
        return list(lax.optimization_barrier((*array, *others))[: len(array)])
    return lax.optimization_barrier((array, *others))[0]


def per_device(
    stream,
    ln_gain,
    up_x,
    up_z,
    conv_w,
    conv_b,
    qkv_w,
    gate_w,
    gate_bias,
    gn_gain,
    skip,
    down_w,
    cotangent,
    lengths,
):
    rows, width = stream.shape
    cols = up_x.shape[1]
    kw = conv_w.shape[0]
    heads = gate_w.shape[0] // 2
    n = lax.axis_size("seq")
    m = n // 2
    me, hd = lax.axis_index("seq"), lax.axis_index("head")
    starts = jnp.cumsum(lengths) - lengths
    order = sources(me, n)
    sc = jnp.concatenate([jnp.stack([me, hd]), starts, jnp.stack(order)]).astype(I32)
    cb, gn, sk = conv_b.reshape(1, cols), gn_gain.reshape(1, cols), skip.reshape(1, cols)
    gw = jnp.pad(gate_w.transpose(1, 0, 2), ((0, 0), (0, 16 - 2 * heads), (0, 0)))
    tall = S((rows, cols))
    tall16 = S((rows, cols), BF16)

    hf = width // m // 2
    slices = call(
        left_kernel,
        [sc, stream, cotangent],
        [S((rows, 2 * hf), BF16)] * m,
        in_specs=[SMEM, None, None],
        weight=0,
    )
    left = [jnp.stack([shifted(a, -2 * k) if k else a for k, a in enumerate(slices)])]

    halo = lax.ppermute(stream[rows - HALO :], "seq", [(i, i + 1) for i in range(n - 1)])
    nt = cols // CT
    bh, bl = call(prep_kernel, [qkv_w], [S((3, nt, CT, CT), BF16)] * 2)
    x_ext = after(jnp.concatenate([jnp.ones((1, width), BF16), halo[1:], stream]), bh)
    mixed, stat, pay = proj(x_ext, up_x, ln_gain, True)
    runs = gather_runs(pay)
    hops = [runs[min(k, len(runs) - 1)] for k in range(3)]

    act, qh, ql, kh, kl, vh, vl, ph, pl_, gate_part = call(
        front_kernel,
        [after(sc, *left), mixed, bh, bl, conv_w, cb, gw],
        [tall] + [tall16] * 8 + [S((8, rows))],
        in_specs=[SMEM] + [None] * 6,
        macs=12 * rows * cols * CT,
    )
    (gv,) = call(
        gate_kernel,
        [after(sc, *hops[0]), sum_over(gate_part, "head"), gate_bias],
        [S((8, rows))],
        in_specs=[SMEM, None, SMEM],
        weight=0,
    )
    gvs = gather_xor(gv)

    left.append(swapped(left[0], "head", 1))
    outgate = proj(after(x_ext, gate_part, *hops[0]), up_z, ln_gain, False)[0]
    dgate = dgated(after(cotangent, outgate, *hops[1]), down_w)
    (hid,) = call(
        local_kernel,
        [sc, qh, ql, kh, kl, vh, vl, gv],
        [tall],
        in_specs=[SMEM] + [None] * 7,
        macs=6 * rows * rows * cols,
    )
    slots_all = sum(map(len, runs))
    u, bufs = None, []
    slot = 0
    for stage, pays in enumerate(runs):
        count = len(pays)
        ins = [after(sc, *hops[2]) if stage == 0 else sc, *pays, ph, pl_, gvs, conv_w, cb]
        specs = [SMEM] + [None] * (count + 5)
        aliases = {}
        if slot:
            ins += [u, *bufs]
            specs += [None] + [pl.BlockSpec(memory_space=pl.ANY)] * 6
            aliases = {6 + count + i: i for i in range(7)}
        place = pl.BlockSpec((1, rows, cols), lambda i, slot=slot: (slot + i, 0, 0))
        square = pl.BlockSpec((1, rows, rows), lambda i, slot=slot: (slot + i, 0, 0))
        u, *bufs = call(
            functools.partial(block_kernel, count, slot, n == 8 and stage == 1),
            ins,
            [tall] + [S((slots_all, rows, cols), BF16)] * 4 + [S((slots_all, rows, rows))] * 2,
            grid=(count,),
            in_specs=specs,
            out_specs=[None] + [place] * 4 + [square] * 2,
            scratch=[pltpu.VMEM((HALO + rows, cols), F32)],
            aliases=aliases,
            macs=count * 6 * rows * rows * cols,
            )
        slot += count

    gh, gl, zh, zl, dh, dl, eh, el, dact, rowtot, sums, payd, pays = call(
        finish_kernel,
        [hid, u, bh, bl, act, outgate, dgate, gn, sk, stat],
        [tall16] * 8
        + [tall, S((rows, 128)), S((8, cols)), S((rows + 16, cols), I16), S((2, rows + 16, cols), I16)],
        scratch=[pltpu.VMEM((3, rows, cols), F32)] + [pltpu.VMEM((rows, cols), F32)] * 2,
        macs=3 * rows * cols * CT,
    )

    *ds, payd = flows(sc, bufs, (eh, el), payd)
    dq = earlier(sc, bufs, ds, bh, bl)
    up = ring_up(pays)
    kept_beside = []

    def step_norm(last):
        ins = [qh, ql, kh, kl, vh, vl, dh, dl, gv, bh, bl, dq]
        kept_beside.append(beside(sc, ins, zh, zl, up_z, ln_gain))
        return kept_beside[0][-1]

    def step_branch(last):
        kept_beside.append(branch_of(after(sc, *up), after(gh, last), gl, down_w))
        return kept_beside[1][0]

    def step_later(slots, payloads, state=None, weight=10, last=()):
        last = last if state else kept_beside[1][:1]
        dv, rh, rl = kept_beside[0][2], kept_beside[0][4], kept_beside[0][5]
        count = len(slots)
        place = pl.BlockSpec((1, rows, cols), lambda i, slots=slots: (pick(slots, i), 0, 0))
        ins = [after(sc, *last), *payloads, bufs[0], bufs[1], rh, rl, vh, vl, gvs]
        ins += state or [dv]
        at = 8 + count
        return call(
            functools.partial(later_kernel, slots),
            ins,
            [tall, tall, S((rows, 128)), S((8, 128))],
            grid=(count,),
            in_specs=[SMEM] + [None] * count + [place, place] + [None] * (len(ins) - count - 3),
            scratch=[pltpu.VMEM((rows, cols), BF16)] * 2,
            aliases={at + k: k for k in range(4)} if state else {at: 1},
            macs=count * 6 * rows * rows * cols,
            weight=weight,
        )

    hop, state, back_runs = gather_later(payd, (step_norm, step_branch, step_later))
    (dq, dk, _, col_here, rh, rl, dn_z), branch = kept_beside
    share = rows // 4

    def second(keep, give, weight):
        return call(
            second_kernel,
            [sc, keep, swapped(give, "head", 1)],
            [S((share, width))] * 2,
            in_specs=[SMEM, None, None],
            weight=weight,
        )

    def join(own, last):
        other = swapped(own, "head", 2)
        parts = [own, swapped(own, "head", 1), other, swapped(other, "head", 1)]
        return call(
            join_kernel,
            [after(sc, last), *parts],
            [S((rows, width), own.dtype)],
            in_specs=[SMEM] + [None] * 4,
            weight=0,
        )[0]

    keep, give = second(*branch, 0)
    result, squares = call(
        result_kernel,
        [sc, keep, swapped(give, "head", 2), stream],
        [S((share, width), BF16), S((1, width // 2))],
        in_specs=[SMEM] + [None] * 3,
        weight=0,
    )

    down = ring_down(after(pays, *hop, branch[0]))
    up2 = ring_up2(up)
    for step, (slots, payloads) in enumerate(back_runs):
        state = step_later(slots, payloads, state, 10)
    e, dv, col_later, flow = state
    (dgates,) = call(
        gate_back_kernel,
        [after(sc, *up2, *down), col_here, col_later, rowtot, gv, flow],
        [S((8, rows))],
        in_specs=[SMEM] + [None] * 5,
        weight=0,
    )
    dgates = sum_over(dgates, "head")
    dm, rim, *kept = by_columns(
        back_kernel,
        [after(sc, result), mixed, dact, dq, dk, e, dv, bh, bl, conv_w, cb, gw, dgates],
        [tall, S((HALO, cols))] + [tall16] * 6 + [tall],
        scratch=[pltpu.VMEM((2 * HALO + rows, CT), F32)],
        macs=30 * rows * cols * CT,
        fixed=(12,),
    )
    down2 = ring_down2(down)
    early = ring_third(up, down, up2, down2)
    rim = lax.ppermute(rim, "seq", [(i + 1, i) for i in range(n - 1)])
    (pack,) = by_columns(
        small_kernel,
        [after(sc, result), mixed, act, kept[6], *kept[:6], qh, ql, kh, kl, vh, vl, dgates, conv_w],
        [S((48, cols))],
        macs=30 * rows * cols * CT,
        fixed=(16,),
        weight=0,
    )
    mh, ml, paym, ux = call(
        send_kernel,
        [dm, rim, after(stat, pack, *down2)],
        [tall16] * 2 + [S((rows + 16, cols), I16), S((8, cols))],
        scratch=[pltpu.VMEM((rows, cols), F32)],
        weight=0,
    )
    up, down = ring_up(paym[None]), ring_down(paym[None])

    keep_early, give_early = wgrad(after(sc, paym), left, (1, 0), [pays] + early)
    got_early = swapped(give_early, "seq", 1)
    keep, give, ln_part = dnorm(
        after(sc, keep_early, *up, *down), mh, ml, up_x, ln_gain, dn_z, stream, stat
    )
    far = after(up + down, keep_early)
    up2, down2 = ring_up2(far[: len(up)]), ring_down2(far[len(up) :])
    late = ring_third(up, down, up2, down2)
    keep, give = second(keep, after(give, *up2, *down2), 0)
    lns = width // cols
    tail = jnp.concatenate([ln_part.reshape(lns, cols), squares])
    tail = sum_over(after(tail, *up2, *down2), "head")
    small = jnp.concatenate([pack, sums, ux[:1], tail])
    small = small + swapped(small, "seq", 1)
    keep_x, give_x = wgrad(after(sc, small, give), left, (0,), [paym[None]] + late)
    got_x = swapped(give_x, "seq", 1)
    (grad_share,) = call(
        norm_back_kernel,
        [after(sc, keep_x), keep, swapped(give, "head", 2), stream, cotangent],
        [S((share, width))],
        in_specs=[SMEM] + [None] * 4,
        weight=0,
    )
    small, bit = after(small, keep_x, grad_share), 2
    while bit < n:
        small = small + swapped(small, "seq", bit)
        bit *= 2
    output = join(result, keep_x)
    grad_stream = join(grad_share, keep_x)
    (grad_down,) = call(
        down_kernel, [after(keep_early, keep_x), got_early], [S((cols, hf))], weight=0
    )
    tail = small[57:]
    grad_ln = tail[:lns].reshape(width)
    rms_pair = jnp.sqrt(tail[lns, :2] / (rows * n * width))
    gain_here = lax.dynamic_slice_in_dim(ln_gain, me * hf, hf, 0)[None]
    (grad_up_z,) = call(
        functools.partial(up_kernel, 1), [keep_early, got_early, gain_here, small[50:51]], [S((hf, cols))], weight=0
    )
    (grad_up_x,) = call(
        functools.partial(up_kernel, 0), [keep_x, got_x, gain_here, small[56:57]], [S((hf, cols))], weight=0
    )
    return (
        output,
        rms_pair,
        grad_stream,
        grad_up_x,
        grad_up_z,
        grad_down,
        grad_ln,
        small[0:kw],
        small[4],
        small[5:17].reshape(3, 4, cols),
        small[17:41].reshape(3, 2 * heads, cols).transpose(1, 0, 2),
        small[41, heads : 2 * heads],
        small[48],
        small[49],
    )


def solution(mesh):
    return jax.shard_map(
        per_device,
        mesh=mesh,
        in_specs=(
            P("seq", None),
            P(),
            P(None, "head"),
            P(None, "head"),
            P(None, "head"),
            P("head"),
            P(None, None, "head"),
            P(None, None, "head"),
            P(),
            P("head"),
            P("head"),
            P("head", None),
            P("seq", None),
            P(),
        ),
        out_specs=(
            P("seq", None),
            P(),
            P("seq", None),
            P("seq", "head"),
            P("seq", "head"),
            P("head", "seq"),
            P(),
            P(None, "head"),
            P("head"),
            P(None, None, "head"),
            P(None, None, "head"),
            P(),
            P("head"),
            P("head"),
        ),
        check_vma=False,
    )
```
